512 devices in a mesh: dom: 64 (over z_hi, y, x, core), sp: 8 (over z_lo).
Axes of the slice: x: 4, y: 4, z: 16 (z_hi: 2, z_lo: 8; z = z_hi * 8 + z_lo), core: 2. Of those that a mesh axis runs over, the one named last changes fastest.
Arguments:
- positions: float32 [3, 32768], P(None, ('dom', 'sp')), may hold values from -1 to 1
- neighbours: int32 [24, 32768], P(None, ('dom', 'sp')), may hold values from 0 to 1279, as said below
- counts: int32 [32768], P(('dom', 'sp')), may hold values from 12 to 24, as said below
- send_lists: int32 [64, 6, 128], P('dom'), may hold values from 0 to 511
- sparse_points: bfloat16 [16384, 512], P('sp'), may hold values from -0.25 to 0.25
- weights: float32 [16384], P('sp'), may hold values from -1280 to 1280
Outputs:
- energies: float32 [32768], P(('dom', 'sp'))
- forces: float32 [3, 32768], P(None, ('dom', 'sp'))
The draws below stay inside these ranges and needn't reach their ends.
Inputs may be any that keep to these rules, and one draw needn't show every extreme that they name: `neighbours`: each atom's neighbour slots index its domain's table and never its own slot; slots at and beyond the atom's count are padding. `counts`: every device holds an atom with 24 live neighbours. `send_lists`: local indices of the sending domain's atoms; an atom may be sent through several faces.
All inputs are finite; a program needn't handle non-finite values.
Results may differ from the reference program's by a relative error of at most 0.0088.
Values may be sent and summed in bfloat16 or wider, within the bound.
A program may use at most 64 MiB of HBM per device.

```python
import math
import jax
import jax.numpy as jnp
import numpy as np
from jax import lax

ATOM_DEV = 64
NBR = 24
DESC = 512
GHOST = 128
FACES = 6
ATOM_DOM = 512
TABLE = 1280
ATOMS = 32768
SPARSE = 16384
N_DOM = 64


def draw_neighbours(key, part):
    key = jax.random.fold_in(key, 11)
    own_slot = jnp.arange(ATOMS, dtype=jnp.int32) % ATOM_DOM
    picks = jax.random.randint(key, (NBR, ATOMS), 0, TABLE - 1, dtype=jnp.int32)
    return picks + (picks >= own_slot[None, :]).astype(jnp.int32)


def draw_counts(key, part):
    key = jax.random.fold_in(key, 23)
    tallies = jax.random.randint(key, (ATOMS,), 12, NBR + 1, dtype=jnp.int32)
    first = jnp.arange(ATOMS, dtype=jnp.int32) % ATOM_DEV == 0
    return jnp.where(first, NBR, tallies).astype(jnp.int32)


def set_ends(drawn, rng, low, largest):
    dims = drawn.shape
    index_at = [jax.random.randint(jax.random.fold_in(rng, axis), (), 0, dims[axis]) for axis in range(len(dims))]
    drawn = drawn.at[tuple(index_at)].set(low)
    longest = dims.index(max(dims))
    index_at[longest] = (index_at[longest] + 1) % dims[longest]
    return drawn.at[tuple(index_at)].set(largest)


def levels(rng, shape, cuts, least, top_value):
    def one(position, blocks):
        heights = jax.random.uniform(jax.random.fold_in(jax.random.fold_in(rng, 6), position), (blocks,), jnp.float32, least / len(cuts), top_value / len(cuts))
        return jnp.repeat(jnp.exp(heights), shape[position] // blocks).reshape((-1,) + (1,) * (len(shape) - position - 1))

    factor_of = one(*cuts[0])
    for cut in cuts[1:]:
        factor_of = factor_of * one(*cut)
    return factor_of


def scatter_about(key, extent, width, limit, shards=(), kind=jnp.bfloat16):
    loudness = levels(key, extent, shards, -0.22, 0.18) if shards else 1.0
    result = jax.random.normal(key, extent, jnp.float32) * width * loudness
    return jnp.minimum(jnp.maximum(result, -limit), limit).astype(kind)


def setup_inputs(seed: int = 0) -> dict:
    key_of = jax.random.split(jax.random.key(seed), 7)
    positions = jnp.clip(jax.random.uniform(key_of[0], (3, ATOMS), jnp.float32, -1.0, 1.0) * levels(key_of[0], (3, ATOMS), ((1, 512),), -0.4, 0.0), -1.0, 1.0)
    neighbours = draw_neighbours(jax.random.fold_in(key_of[6], 71), 0)
    counts = draw_counts(jax.random.fold_in(key_of[6], 71), 0)
    send_lists = set_ends(jax.random.randint(key_of[3], (N_DOM, FACES, GHOST), 0, ATOM_DOM), jax.random.fold_in(key_of[3], 1), 0, ATOM_DOM - 1).astype(jnp.int32)
    sparse_points = scatter_about(key_of[4], (SPARSE, DESC), DESC ** -0.5, 0.25, ((0, 8),))
    weights = scatter_about(key_of[5], (SPARSE,), (262144.0 / (105 * SPARSE) ** 0.5), 1280.0, ((0, 8),), jnp.float32)
    return {"positions": positions, "neighbours": neighbours, "counts": counts, "send_lists": send_lists, "sparse_points": sparse_points, "weights": weights}


def monomial_table():
    power_x, power_y, power_z, factors, starts = ([], [], [], [], [])
    for degree in range(8):
        starts.append(len(power_x))
        for exp_x in range(degree, -1, -1):
            for exp_y in range(degree - exp_x, -1, -1):
                exp_z = degree - exp_x - exp_y
                power_x.append(exp_x)
                power_y.append(exp_y)
                power_z.append(exp_z)
                factors.append(math.factorial(degree) // (math.factorial(exp_x) * math.factorial(exp_y) * math.factorial(exp_z)))
    starts.append(len(power_x))
    return (np.array(power_x), np.array(power_y), np.array(power_z), np.array(factors, dtype=np.float32), starts)

def describe(atom_table, centre, neighbours, counts):
    power_x, power_y, power_z, factors, starts = monomial_table()
    here = atom_table[:, centre]
    there = atom_table[:, neighbours]
    offsets = (there - here[:, None, :]) * 0.5
    squared = lax.optimization_barrier(jnp.sum(offsets * offsets, axis=0))
    slots = jnp.arange(neighbours.shape[0], dtype=jnp.int32)
    in_list = (slots[:, None] < counts[None, :]).astype(jnp.float32)
    cutoff = (1.0 - squared / 3.5) ** 2 * in_list
    centres = 0.05 + 0.15 * jnp.arange(8, dtype=jnp.float32)
    gap = squared[None] - centres[:, None, None]
    radial = jnp.exp(-30.0 * gap * gap) * cutoff[None]
    powers = [jnp.ones_like(offsets)]
    for degree in range(7):
        powers.append(powers[-1] * offsets)
    powers = jnp.stack(powers, 0)
    monomials = powers[power_x, 0] * powers[power_y, 1] * powers[power_z, 2]
    density = jnp.einsum('nka,mka->nma', radial, monomials, precision=lax.Precision.HIGHEST)
    blocks = []
    for degree in range(8):
        part = density[:, starts[degree]:starts[degree + 1]]
        weighted = part * factors[starts[degree]:starts[degree + 1]][None, :, None]
        blocks.append(jnp.einsum('nma,qma->nqa', weighted, part, precision=lax.Precision.HIGHEST))
    spectrum = jnp.stack(blocks, 2).reshape(-1, centre.shape[0])
    scale = lax.rsqrt(lax.optimization_barrier(jnp.sum(spectrum * spectrum, axis=0, keepdims=True)) + 1e-06)
    return spectrum * scale

def reference(positions, neighbours, counts, send_lists, sparse_points, weights):
    domains = jnp.arange(N_DOM, dtype=jnp.int32)
    grouped = positions.reshape(3, N_DOM, ATOM_DOM)
    pieces = [grouped]
    for face in range(FACES):
        partner = jnp.bitwise_xor(domains, 1 << face)
        pieces.append(grouped[:, partner[:, None], send_lists[partner, face, :]])
    tables = jnp.concatenate(pieces, axis=2).transpose(1, 0, 2)
    near_lists = neighbours.reshape(NBR, N_DOM, ATOM_DOM).transpose(1, 0, 2)
    tallies = counts.reshape(N_DOM, ATOM_DOM)
    centre = jnp.arange(ATOM_DOM, dtype=jnp.int32)

    def one_domain(items):
        atom_table, near, tally = items

        def local(table_in):
            return describe(table_in, centre, near, tally)
        descriptor, pull = jax.vjp(local, atom_table)
        shared = descriptor.astype(jnp.bfloat16)
        scores = jnp.dot(sparse_points, shared, preferred_element_type=jnp.float32)
        squares = scores * scores
        energy = lax.optimization_barrier(jnp.sum(weights[:, None] * squares * squares, axis=0))
        slopes = (4.0 * weights[:, None] * squares * scores).astype(jnp.bfloat16)
        grad_q = lax.dot_general(sparse_points, slopes, (((0,), (0,)), ((), ())), preferred_element_type=jnp.float32)
        grad_table, = pull(grad_q)
        return (energy, grad_table)
    energies, grads = lax.map(one_domain, (tables, near_lists, tallies))
    own = grads[:, :, :ATOM_DOM].transpose(1, 0, 2)
    ghosts = grads[:, :, ATOM_DOM:].reshape(N_DOM, 3, FACES, GHOST)
    for face in range(FACES):
        partner = jnp.bitwise_xor(domains, 1 << face)
        returned = ghosts[partner, :, face, :].transpose(1, 0, 2)
        own = own.at[:, domains[:, None], send_lists[:, face, :]].add(returned)
    return (energies.reshape(ATOMS), -own.reshape(3, ATOMS))
```

```python
import math

import jax
import jax.numpy as jnp
import numpy as np
from jax import lax
from jax.experimental import pallas as pl
from jax.experimental.pallas import tpu as pltpu
from jax.sharding import PartitionSpec as P

F32, BF16 = jnp.float32, jnp.bfloat16
MESH = pl.DeviceIdType.MESH
SLOTS = 12
ROWS = 160
BACK = 176
CHUNK = 512


def powers():
    found, starts = [], []
    for degree in range(8):
        starts.append(len(found))
        for a in range(degree, -1, -1):
            for b in range(degree - a, -1, -1):
                found.append((a, b, degree - a - b))
    return found, starts + [len(found)]


POWERS, STARTS = powers()
PLACE = {p: i for i, p in enumerate(POWERS)}
SPREAD = [
    float(math.factorial(sum(p)) * math.prod(math.factorial(e) for e in p)) for p in POWERS
]


def raised(m, axis):
    p = list(POWERS[m])
    p[axis] += 1
    return PLACE[tuple(p)]


def expansion():
    e = np.zeros((2 * ROWS, 512), np.float32)
    for n in range(8):
        for n2 in range(8):
            for l in range(8):
                r = (n2 - n) % 8
                first = n
                if r > 4:
                    r, first = 8 - r, n2
                if r == 0:
                    group, half = 16 + l % 4, l // 4
                else:
                    group, half = {1: (l, 0), 3: (l, 1), 2: (8 + l, 0), 4: (8 + l, 1)}[r]
                e[half * ROWS + group * 8 + first, (n * 8 + n2) * 8 + l] = 1.0
    return e


def up(x, k):
    return x if k % 8 == 0 else pltpu.roll(x, (8 - k) % 8, 0)


def swap(x):
    return pltpu.roll(x, 64, 1)


def pieces(x, count):
    out = []
    for _ in range(count):
        p = x.astype(BF16).astype(F32)
        out.append(p)
        x = x - p
    return out


def one_hot(row):
    return jnp.where(lax.broadcasted_iota(jnp.int32, (128, 128), 0) == row, 1.0, 0.0).astype(BF16)


def kernel(
    faces, pos_ref, near_ref, count_ref, lists_ref, sparse_hbm, weight_ref, fold_hbm, spread_hbm,
    energy_ref, force_ref,
    posbuf, ghost_out, tab, pack, index, ohs, ohn, looked, offs, base, mono, radial, slope_r, dens,
    spec, dbuf, rbuf, gbuf, vbuf, descs, slopes, sparse, fold, spread, folded, wide, left, pulls,
    gtab, gret, domg, fin,
    local_sem, pos_s, pos_r, gho_s, gho_r, des_s, des_r, gra_s, gra_r, ret_s, ret_r, fin_s, fin_r,
):
    dom, sp = lax.axis_index("dom"), lax.axis_index("sp")
    n_dom, n_sp = lax.axis_size("dom"), lax.axis_size("sp")
    below = n_dom // 2
    ring = 2 * n_sp
    z = (dom // below) * n_sp + sp
    rest = lax.rem(dom, below)
    side = 1 - 2 * lax.rem(dom, 2)

    def along(delta):
        there = lax.rem(z + delta + ring, ring)
        return (rest + (there // n_sp) * below, lax.rem(there, n_sp))

    def peer(delta):
        return (dom, lax.rem(sp + delta, n_sp))

    def partner(face):
        bit = lax.rem(dom // 2**face, 2)
        return (dom + (1 - 2 * bit) * 2**face, sp)

    delta = [0, 1, -1, 2, -2, 3, -3, 4 * side]
    lane = lax.broadcasted_iota(jnp.int32, (8, 128), 1)
    low = lane < 64
    row8 = lax.broadcasted_iota(jnp.int32, (8, 128), 0)

    loads = [
        pltpu.make_async_copy(sparse_hbm, sparse, local_sem.at[0]),
        pltpu.make_async_copy(fold_hbm, fold, local_sem.at[1]),
        pltpu.make_async_copy(spread_hbm, spread, local_sem.at[2]),
    ]
    for load in loads:
        load.start()

    barrier = pltpu.get_barrier_semaphore()
    greeted = [peer(d) for d in range(1, 8)] + [partner(f) for f in range(faces)]
    greeted += [along(d) for d in (1, -1, 2, -2, 3, -3, 4, -4)]
    for who in greeted:
        pl.semaphore_signal(barrier, inc=1, device_id=who, device_id_type=MESH)

    posbuf[sp] = jnp.zeros((8, 128), F32)
    posbuf[sp, 0:3, 0:64] = pos_ref[...]
    here = posbuf[sp]
    here = here + swap(here)
    posbuf[sp] = here
    pl.semaphore_wait(barrier, len(greeted))

    def remote(src, dst, s, r, who):
        return pltpu.make_async_remote_copy(
            src_ref=src, dst_ref=dst, send_sem=s, recv_sem=r, device_id=who, device_id_type=MESH
        )

    sent_pos = [
        remote(posbuf.at[sp], posbuf.at[sp], pos_s.at[d - 1], pos_r.at[d - 1], peer(d))
        for d in range(1, 8)
    ]
    for c in sent_pos:
        c.start()

    for f in range(faces):
        ohs[:, f * 128 : (f + 1) * 128] = one_hot(lists_ref[f : f + 1, :] & 127)
    pack[...] = jnp.zeros((24, 128), jnp.int32)
    pack[:, 0:64] = near_ref[...]
    index[0:8] = jnp.where(low, pack[0:8], swap(pack[8:16]))
    last = pack[16:24]
    last = jnp.where(low, last, swap(pltpu.roll(last, 4, 0)))
    index[8:16] = jnp.where(row8 < 4, last, 0)
    for j in range(SLOTS):
        ohn[:, j * 128 : (j + 1) * 128] = one_hot(index[j : j + 1, :] & 127)

    for c in sent_pos:
        c.wait()

    for hi in range(4):
        tab[hi] = jnp.where(low, posbuf[2 * hi], posbuf[2 * hi + 1])

    own = tab[0:4].reshape(32, 128)
    parts = jnp.concatenate(pieces(own, 3), axis=0).astype(BF16)
    out = jnp.dot(parts, ohs[...], preferred_element_type=F32)
    out = out[0:32] + out[32:64] + out[64:96]
    sent_ghost = []
    for f in range(faces):
        which = lists_ref[f : f + 1, :] // 128
        tile = jnp.zeros((8, 128), F32)
        for hi in range(4):
            part = out[hi * 8 : hi * 8 + 8, f * 128 : (f + 1) * 128]
            tile = jnp.where(which == hi, part, tile)
        ghost_out[f] = tile
        c = remote(ghost_out.at[f], tab.at[4 + f], gho_s.at[f], gho_r.at[f], partner(f))
        c.start()
        sent_ghost.append(c)

    def look(first, last, into):
        n = (last - first) * 8
        values = tab[first:last].reshape(n, 128)
        split = jnp.concatenate(pieces(values, 3), axis=0).astype(BF16)
        for q in range(4):
            at = slice(q * 384, (q + 1) * 384)
            got = jnp.dot(split, ohn[:, at], preferred_element_type=F32)
            got = got[0:n] + got[n : 2 * n] + got[2 * n : 3 * n]
            for u in range(3):
                j = q * 3 + u
                which = index[j : j + 1, :] // 128
                tile = looked[j] if into else jnp.zeros((8, 128), F32)
                for hi in range(first, last):
                    part = got[(hi - first) * 8 : (hi - first) * 8 + 8, u * 128 : (u + 1) * 128]
                    tile = jnp.where(which == hi, part, tile)
                looked[j] = tile

    look(0, 4, False)
    for load in loads:
        load.wait()
    points = sparse.shape[0]

    @pl.loop(0, points // CHUNK)
    def _(c):
        at = pl.ds(pl.multiple_of(c * CHUNK, CHUNK), CHUNK)
        folded[:, at] = lax.dot_general(
            fold[...], sparse[at, :], (((1,), (1,)), ((), ())), preferred_element_type=F32
        ).astype(BF16)

    @pl.loop(0, points // 128)
    def _(c):
        column = jnp.broadcast_to(4.0 * weight_ref[pl.ds(c, 1), :], (128, 128)).T
        wide[pl.ds(pl.multiple_of(c * 128, 128), 128), :] = column

    for c in sent_ghost:
        c.wait()
    look(4, 4 + faces, True)

    offs[...] = jnp.zeros(offs.shape, F32)
    for j in range(SLOTS):
        offs[j] = 0.5 * (looked[j] - here)
    x, y, zz = offs[:, 0, :], offs[:, 1, :], offs[:, 2, :]
    squared = x * x + y * y + zz * zz
    j16 = lax.broadcasted_iota(jnp.int32, (16, 128), 0)
    h16 = lax.broadcasted_iota(jnp.int32, (16, 128), 1) // 64
    slot = jnp.where(j16 < 8, j16 + 8 * h16, 8 + j16 + 4 * h16)
    pack[0:8] = jnp.zeros((8, 128), jnp.int32)
    pack[0:1, 0:64] = count_ref[...]
    counts = pack[0:8]
    counts = (counts + swap(counts))[0:1]
    live = jnp.where((slot < counts) & (j16 < SLOTS), 1.0, 0.0)
    inside = 1.0 - squared * (1.0 / 3.5)
    base[0] = squared
    base[1] = inside * inside * live
    base[2] = (-2.0 / 3.5) * inside * live
    mono[0] = jnp.ones((16, 128), F32)
    for m in range(1, len(POWERS)):
        p = list(POWERS[m])
        axis = 2 if p[2] else 1 if p[1] else 0
        by = (x, y, zz)[axis] * (1.0 / p[axis])
        p[axis] -= 1
        mono[m] = mono[PLACE[tuple(p)]] * by
    centre = 0.05 + 0.15 * row8.astype(F32)
    for j in range(SLOTS):
        gap = base[0, j : j + 1, :] - centre
        bell = jnp.exp(-30.0 * gap * gap)
        r = bell * base[1, j : j + 1, :]
        radial[j] = r
        slope_r[j] = r * (-60.0 * gap) + bell * base[2, j : j + 1, :]

    @pl.loop(0, len(POWERS) // 8)
    def _(block):
        rs = [radial[j] for j in range(SLOTS)]
        for u in range(8):
            m = block * 8 + u
            rows = mono[m]
            total = rs[0] * rows[0:1, :]
            for j in range(1, SLOTS):
                total = total + rs[j] * rows[j : j + 1, :]
            dens[m] = total + swap(total)

    def turned(d):
        return jnp.where(low, d, up(d, 2))

    zero = []
    for l in range(8):
        s0 = s1 = s2 = None
        for m in range(STARTS[l], STARTS[l + 1]):
            d = dens[m]
            t = turned(d)
            f = d * SPREAD[m]
            a, b, c = f * d, f * up(t, 1), f * up(t, 2)
            s0, s1, s2 = (a, b, c) if s0 is None else (s0 + a, s1 + b, s2 + c)
        spec[l] = s1
        spec[8 + l] = s2
        zero.append(s0)
    for l in range(4):
        spec[16 + l] = jnp.where(low, zero[l], zero[l + 4])
    twice = jnp.where(low, 2.0, 1.0)

    def times(g):
        return 2.0 if g < 8 else twice if g < 16 else 1.0

    def both(tile):
        row = jnp.sum(tile, axis=0, keepdims=True)
        tile = jnp.broadcast_to(row, (8, 128))
        return tile + swap(tile)

    total = jnp.zeros((8, 128), F32)
    for g in range(20):
        v = spec[g]
        total = total + times(g) * v * v
    scale = lax.rsqrt(both(total) + 1e-06)
    for g in range(0, 20, 2):
        two = jnp.concatenate([spec[g] * scale, spec[g + 1] * scale], axis=0)
        dbuf[0, g * 8 : g * 8 + 16, :] = two.astype(BF16)

    sent_desc = [
        remote(dbuf.at[0], dbuf.at[t], des_s.at[t - 1], des_r.at[t - 1], along(delta[t]))
        for t in range(1, 8)
    ]
    for c in sent_desc:
        c.start()

    wlow = lax.broadcasted_iota(jnp.int32, (ROWS, 128), 1) < 64
    sent_grad = [None] * 8
    for slots in ((0, 1, 2, 3), (4, 5, 6, 7)):
        for t in slots:
            if t:
                sent_desc[t - 1].wait_recv()
        for k in range(2):
            xa = dbuf[slots[2 * k]].astype(F32)
            xb = dbuf[slots[2 * k + 1]].astype(F32)
            at = slice(k * 128, (k + 1) * 128)
            vbuf[0:ROWS, at] = jnp.where(wlow, xa, swap(xb)).astype(BF16)
            vbuf[ROWS : 2 * ROWS, at] = jnp.where(wlow, swap(xa), xb).astype(BF16)
        descs[...] = jnp.dot(spread[...], vbuf[...], preferred_element_type=F32).astype(BF16)
        energy = jnp.zeros((8, 256), F32)
        for c in range(points // CHUNK):
            at = slice(c * CHUNK, (c + 1) * CHUNK)
            score = jnp.dot(sparse[at, :], descs[...], preferred_element_type=F32)
            w = wide[at, :]
            square = score * score
            ws = jnp.concatenate([w, w], axis=1) * square
            energy = energy + jnp.sum((ws * square).reshape(CHUNK // 8, 8, 256), axis=0)
            slopes[at, :] = (ws * score).astype(BF16)
        energy = jnp.sum(energy, axis=0, keepdims=True)
        grad = jnp.dot(folded[...], slopes[...], preferred_element_type=F32)
        for k in range(2):
            a, b = slots[2 * k], slots[2 * k + 1]
            at = slice(k * 128, (k + 1) * 128)
            lo, hi = grad[0:ROWS, at], grad[ROWS : 2 * ROWS, at]
            rbuf[a, 0:ROWS, :] = jnp.where(wlow, lo, swap(hi)).astype(BF16)
            rbuf[b, 0:ROWS, :] = jnp.where(wlow, swap(lo), hi).astype(BF16)
            e = jnp.broadcast_to(energy[:, at], (8, 128))
            for t, mine in ((a, e), (b, swap(e))):
                p = pieces(mine, 3)
                tile = jnp.where(row8 == 0, p[0], jnp.where(row8 == 1, p[1], jnp.where(row8 == 2, p[2], 0.0)))
                tile = jnp.concatenate([tile, jnp.zeros((8, 128), F32)], axis=0)
                rbuf[t, ROWS:BACK, :] = tile.astype(BF16)
        for t in slots:
            if t:
                c = remote(rbuf.at[t], gbuf.at[t - 1], gra_s.at[t - 1], gra_r.at[t - 1], along(-delta[t]))
                c.start()
                sent_grad[t] = c

    summed = rbuf[0].astype(F32)
    for t in range(1, 8):
        sent_grad[t].wait_recv()
        summed = summed + gbuf[t - 1].astype(F32)
    last = summed[ROWS : ROWS + 8, :]
    energy_ref[...] = (0.25 * jnp.sum(last, axis=0, keepdims=True))[:, 0:64]

    dot = jnp.zeros((8, 128), F32)
    for g in range(20):
        dot = dot + summed[g * 8 : g * 8 + 8, :] * spec[g]
    dot = both(dot) * scale
    pull = []
    for g in range(20):
        pull.append(scale * (summed[g * 8 : g * 8 + 8, :] - times(g) * (spec[g] * scale) * dot))
    for l in range(8):
        ha, hb, h0 = pull[l], pull[8 + l], pull[16 + l % 4]
        h0 = swap(h0) if l < 4 else h0
        other = swap(ha)
        k1 = ha
        k2 = jnp.where(low, hb, hb + up(hb, 4))
        k5 = jnp.where(low, up(other, -3), up(other, -1))
        k6 = jnp.where(low, up(hb, -2), 2.0 * h0)
        for m in range(STARTS[l], STARTS[l + 1]):
            t = turned(dens[m])
            v = k1 * up(t, 1) + k2 * up(t, 2) + (k5 * up(t, 5) + k6 * up(t, 6))
            left[m] = (v + swap(v)) * SPREAD[m]

    @pl.loop(0, SLOTS // 4)
    def _(block):
        q = [[None] * 4 for _ in range(4)]

        def add(old, new):
            return new if old is None else old + new

        for m in range(len(POWERS)):
            d = [left[m]]
            if m < STARTS[7]:
                d += [left[raised(m, axis)] for axis in range(3)]
            for u in range(4):
                b = mono[m, pl.ds(block * 4 + u, 1), :]
                for axis in range(len(d)):
                    q[axis][u] = add(q[axis][u], d[axis] * b)
        for u in range(4):
            j = block * 4 + u
            r = radial[j]
            by_square = jnp.sum(slope_r[j] * q[0][u], axis=0, keepdims=True)
            gx, gy, gz = (jnp.sum(r * q[axis][u], axis=0, keepdims=True) for axis in (1, 2, 3))
            straight = jnp.where(row8 == 0, gx, jnp.where(row8 == 1, gy, jnp.where(row8 == 2, gz, 0.0)))
            pulls[j] = 0.5 * straight + offs[j] * by_square

    centre_grad = pulls[0]
    for j in range(1, SLOTS):
        centre_grad = centre_grad + pulls[j]
    centre_grad = centre_grad + swap(centre_grad)

    def placed(tiles, which, first, last):
        rows = []
        split = [pieces(tile, 2) for tile in tiles]
        for p in range(2):
            for hi in range(first, last):
                rows.append(jnp.concatenate(
                    [jnp.where(w == hi, s[p], 0.0) for w, s in zip(which, split)], axis=1
                ))
        return jnp.concatenate(rows, axis=0).astype(BF16)

    over_lanes = (((1,), (1,)), ((), ()))

    def scatter(first, last):
        n = (last - first) * 8
        total = jnp.zeros((n, 128), F32)
        for q in range(4):
            js = range(q * 3, q * 3 + 3)
            which = [index[j : j + 1, :] // 128 for j in js]
            rows = placed([pulls[j] for j in js], which, first, last)
            got = lax.dot_general(
                rows, ohn[:, q * 384 : (q + 1) * 384], over_lanes, preferred_element_type=F32
            )
            total = total + got[0:n] + got[n : 2 * n]
        return total.reshape(last - first, 8, 128)

    gtab[4 : 4 + faces] = scatter(4, 4 + faces)
    sent_back = []
    for f in range(faces):
        c = remote(gtab.at[4 + f], gret.at[f], ret_s.at[f], ret_r.at[f], partner(f))
        c.start()
        sent_back.append(c)
    own = scatter(0, 4)
    for c in sent_back:
        c.wait_recv()
    which = [lists_ref[f : f + 1, :] // 128 for f in range(faces)]
    rows = placed([gret[f] for f in range(faces)], which, 0, 4)
    got = lax.dot_general(rows, ohs[...], over_lanes, preferred_element_type=F32)
    domg[...] = own + (got[0:32] + got[32:64]).reshape(4, 8, 128)
    sent_fin = []
    for d in range(1, 8):
        who = peer(d)
        c = remote(domg.at[who[1] // 2], fin.at[d - 1], fin_s.at[d - 1], fin_r.at[d - 1], who)
        c.start()
        sent_fin.append(c)
    mine = domg[sp // 2]
    for d in range(1, 8):
        sent_fin[d - 1].wait_recv()
        mine = mine + fin[d - 1]
    odd = jnp.where(lax.rem(sp, 2) == 1, 1, 0)
    mine = jnp.where(odd == 1, swap(mine), mine)
    force_ref[...] = (centre_grad - mine)[0:3, 0:64]
    for c in sent_desc + sent_grad[1:] + sent_back + sent_fin:
        c.wait_send()


def body(positions, neighbours, counts, send_lists, sparse_points, weights):
    faces = send_lists.shape[1]
    points = sparse_points.shape[0]
    fold = expansion()
    vmem = pl.BlockSpec(memory_space=pltpu.VMEM)
    hbm = pl.BlockSpec(memory_space=pl.ANY)
    dma = pltpu.SemaphoreType.DMA
    energies, forces = pl.pallas_call(
        lambda *refs: kernel(faces, *refs),
        out_shape=(
            jax.ShapeDtypeStruct((1, 64), F32),
            jax.ShapeDtypeStruct((3, 64), F32),
        ),
        in_specs=[vmem, vmem, vmem, vmem, hbm, vmem, hbm, hbm],
        out_specs=(vmem, vmem),
        scratch_shapes=[
            pltpu.VMEM((8, 8, 128), F32),
            pltpu.VMEM((faces, 8, 128), F32),
            pltpu.VMEM((4 + faces, 8, 128), F32),
            pltpu.VMEM((24, 128), jnp.int32),
            pltpu.VMEM((16, 128), jnp.int32),
            pltpu.VMEM((128, faces * 128), BF16),
            pltpu.VMEM((128, SLOTS * 128), BF16),
            pltpu.VMEM((SLOTS, 8, 128), F32),
            pltpu.VMEM((16, 8, 128), F32),
            pltpu.VMEM((3, 16, 128), F32),
            pltpu.VMEM((120, 16, 128), F32),
            pltpu.VMEM((SLOTS, 8, 128), F32),
            pltpu.VMEM((SLOTS, 8, 128), F32),
            pltpu.VMEM((120, 8, 128), F32),
            pltpu.VMEM((20, 8, 128), F32),
            pltpu.VMEM((8, ROWS, 128), BF16),
            pltpu.VMEM((8, BACK, 128), BF16),
            pltpu.VMEM((7, BACK, 128), BF16),
            pltpu.VMEM((2 * ROWS, 256), BF16),
            pltpu.VMEM((512, 256), BF16),
            pltpu.VMEM((points, 256), BF16),
            pltpu.VMEM((points, 512), BF16),
            pltpu.VMEM((2 * ROWS, 512), BF16),
            pltpu.VMEM((512, 2 * ROWS), BF16),
            pltpu.VMEM((2 * ROWS, points), BF16),
            pltpu.VMEM((points, 128), F32),
            pltpu.VMEM((120, 8, 128), F32),
            pltpu.VMEM((SLOTS, 8, 128), F32),
            pltpu.VMEM((4 + faces, 8, 128), F32),
            pltpu.VMEM((faces, 8, 128), F32),
            pltpu.VMEM((4, 8, 128), F32),
            pltpu.VMEM((7, 8, 128), F32),
            dma((3,)),
            dma((7,)), dma((7,)),
            dma((faces,)), dma((faces,)),
            dma((7,)), dma((7,)),
            dma((7,)), dma((7,)),
            dma((faces,)), dma((faces,)),
            dma((7,)), dma((7,)),
        ],
        compiler_params=pltpu.CompilerParams(
            collective_id=0, has_side_effects=True, vmem_limit_bytes=48 * 2**20
        ),
        name="gap_forces",
    )(
        positions,
        neighbours,
        counts.reshape(1, -1),
        send_lists[0],
        sparse_points,
        weights.reshape(-1, 128),
        jnp.asarray(fold, BF16),
        jnp.asarray(fold.T, BF16),
    )
    return energies.reshape(-1), forces


def solution(mesh):
    in_specs = (
        P(None, ("dom", "sp")),
        P(None, ("dom", "sp")),
        P(("dom", "sp")),
        P("dom", None, None),
        P("sp", None),
        P("sp"),
    )
    out_specs = (P(("dom", "sp")), P(None, ("dom", "sp")))
    return jax.shard_map(body, mesh=mesh, in_specs=in_specs, out_specs=out_specs, check_vma=False)
```

```python
import math

import jax
import jax.numpy as jnp
from jax import lax
from jax.experimental import pallas as pl
from jax.experimental.pallas import tpu as pltpu
from jax.sharding import PartitionSpec as P

F32, BF16 = jnp.float32, jnp.bfloat16
MESH = pl.DeviceIdType.MESH
SLOTS = 12
ROWS = 160
BACK = 176
CHUNK = 512


def powers():
    found, starts = [], []
    for degree in range(8):
        starts.append(len(found))
        for a in range(degree, -1, -1):
            for b in range(degree - a, -1, -1):
                found.append((a, b, degree - a - b))
    return found, starts + [len(found)]


POWERS, STARTS = powers()
PLACE = {p: i for i, p in enumerate(POWERS)}
SPREAD = [
    float(math.factorial(sum(p)) * math.prod(math.factorial(e) for e in p)) for p in POWERS
]


def raised(m, axis):
    p = list(POWERS[m])
    p[axis] += 1
    return PLACE[tuple(p)]


def packed_place(e):
    n, n2, l = e // 64, (e // 8) & 7, e & 7
    r = (n2 - n) & 7
    first = jnp.where(r > 4, n2, n)
    r = jnp.where(r > 4, 8 - r, r)
    group = jnp.where(r == 0, 16 + (l & 3), jnp.where((r & 1) == 1, l, 8 + l))
    half = jnp.where(r == 0, l // 4, jnp.where(r > 2, 1, 0))
    return half * ROWS + group * 8 + first


def up(x, k):
    return x if k % 8 == 0 else pltpu.roll(x, (8 - k) % 8, 0)


def swap(x):
    return pltpu.roll(x, 64, 1)


def pieces(x, count):
    out = []
    for _ in range(count):
        p = x.astype(BF16).astype(F32)
        out.append(p)
        x = x - p
    return out


def one_hot(row):
    return jnp.where(lax.broadcasted_iota(jnp.int32, (128, 128), 0) == row, 1.0, 0.0).astype(BF16)


def kernel(
    faces, pos_hbm, near_hbm, count_hbm, lists_hbm, sparse_hbm, weight_hbm,
    energy_ref, force_ref,
    pos_ref, near_ref, count_ref, lists_ref, weight_ref,
    posbuf, topbuf, ghost_out, tab, pack, index, ohs, oht, ohn, looked, offs, base, mono, radial, slope_r, dens,
    spec, dbuf, rbuf, gbuf, vbuf, descs, slopes, sparse, fold, spread, folded, wide, left, pulls,
    gtab, gret, domg, fin, topg, fintop,
    local_sem, pos_s, pos_r, top_s, top_r, gho_s, gho_r, des_s, des_r, gra_s, gra_r, ret_s, ret_r, fin_s, fin_r, fit_s, fit_r,
):
    dom, sp = lax.axis_index("dom"), lax.axis_index("sp")
    n_dom, n_sp = lax.axis_size("dom"), lax.axis_size("sp")
    below = n_dom // 2
    ring = 2 * n_sp
    z = (dom // below) * n_sp + sp
    rest = lax.rem(dom, below)
    side = 1 - 2 * lax.rem(dom, 2)

    def along(delta):
        there = lax.rem(z + delta + ring, ring)
        return (rest + (there // n_sp) * below, lax.rem(there, n_sp))

    def peer(delta):
        return (dom, lax.rem(sp + delta, n_sp))

    def partner(face):
        bit = lax.rem(dom // 2**face, 2)
        return (dom + (1 - 2 * bit) * 2**face, sp)

    delta = [0, 1, -1, 2, -2, 3, -3, 4 * side]
    lane = lax.broadcasted_iota(jnp.int32, (8, 128), 1)
    low = lane < 64
    row8 = lax.broadcasted_iota(jnp.int32, (8, 128), 0)

    def above(d):
        return (lax.rem(dom + below, n_dom), lax.rem(sp + d, n_sp))

    pairs = [
        (pos_hbm, pos_ref), (lists_hbm, lists_ref), (near_hbm, near_ref), (count_hbm, count_ref),
        (weight_hbm, weight_ref), (sparse_hbm, sparse),
    ]
    loads = [pltpu.make_async_copy(a, b, local_sem.at[i]) for i, (a, b) in enumerate(pairs)]
    for load in loads:
        load.start()

    barrier = pltpu.get_barrier_semaphore()
    greeted = [peer(d) for d in range(1, 8)] + [partner(f) for f in range(faces - 1)]
    greeted += [along(d) for d in (1, -1, 2, -2, 3, -3, 4, -4)] + [above(d) for d in range(8)]
    for who in greeted:
        pl.semaphore_signal(barrier, inc=1, device_id=who, device_id_type=MESH)

    loads[0].wait()
    loads[1].wait()
    top = faces - 1
    posbuf[sp] = jnp.zeros((8, 128), F32)
    posbuf[sp, 0:3, 0:64] = pos_ref[...]
    here = posbuf[sp]
    here = here + swap(here)
    here = jnp.where(row8 == 3, lists_ref[top].astype(F32), here)
    posbuf[sp] = here
    for load in loads[2:5]:
        load.wait()
    for f in range(top):
        ohs[:, f * 128 : (f + 1) * 128] = one_hot(lists_ref[f] & 127)
    pack[...] = jnp.zeros((24, 128), jnp.int32)
    pack[:, 0:64] = near_ref[...]
    index[0:8] = jnp.where(low, pack[0:8], swap(pack[8:16]))
    last = pack[16:24]
    last = jnp.where(low, last, swap(pltpu.roll(last, 4, 0)))
    index[8:16] = jnp.where(row8 < 4, last, 0)
    for j in range(SLOTS):
        ohn[:, j * 128 : (j + 1) * 128] = one_hot(index[j : j + 1, :] & 127)
    pl.semaphore_wait(barrier, len(greeted))

    def remote(src, dst, s, r, who):
        return pltpu.make_async_remote_copy(
            src_ref=src, dst_ref=dst, send_sem=s, recv_sem=r, device_id=who, device_id_type=MESH
        )

    sent_pos = [
        remote(posbuf.at[sp], posbuf.at[sp], pos_s.at[d - 1], pos_r.at[d - 1], peer(d))
        for d in range(1, 8)
    ]
    for c in sent_pos:
        c.start()

    sent_top = [
        remote(posbuf.at[sp], topbuf.at[sp], top_s.at[d], top_r.at[d], above(d)) for d in range(8)
    ]
    for c in sent_top:
        c.start()

    place = packed_place(lax.broadcasted_iota(jnp.int32, (8, 512), 1))[0:1]
    numbers = lax.broadcasted_iota(jnp.int32, (2 * ROWS, 512), 0)
    fold[...] = jnp.where(numbers == place, 1.0, 0.0).astype(BF16)
    place = packed_place(lax.broadcasted_iota(jnp.int32, (512, 128), 0))
    for k in range(0, 2 * ROWS, 128):
        n = min(128, 2 * ROWS - k)
        numbers = k + lax.broadcasted_iota(jnp.int32, (512, 128), 1)
        spread[:, k : k + n] = jnp.where(numbers == place, 1.0, 0.0).astype(BF16)[:, 0:n]
    for load in loads[5:]:
        load.wait()
    points = sparse.shape[0]

    @pl.loop(0, points // 128)
    def _(c):
        column = jnp.broadcast_to(4.0 * weight_ref[pl.ds(c, 1), :], (128, 128)).T
        wide[pl.ds(pl.multiple_of(c * 128, 128), 128), :] = column

    @pl.loop(0, points // CHUNK)
    def _(c):
        at = pl.ds(pl.multiple_of(c * CHUNK, CHUNK), CHUNK)
        folded[:, at] = lax.dot_general(
            fold[...], sparse[at, :], (((1,), (1,)), ((), ())), preferred_element_type=F32
        ).astype(BF16)

    for c in sent_pos:
        c.wait()

    for hi in range(4):
        tab[hi] = jnp.where(low, posbuf[2 * hi], posbuf[2 * hi + 1])

    def gather(tiles, hots):
        parts = jnp.concatenate(pieces(tiles.reshape(32, 128), 3), axis=0).astype(BF16)
        out = jnp.dot(parts, hots, preferred_element_type=F32)
        return out[0:32] + out[32:64] + out[64:96]

    def chosen(out, which):
        tile = jnp.zeros((8, 128), F32)
        for hi in range(4):
            tile = jnp.where(which == hi, out[hi * 8 : hi * 8 + 8], tile)
        return tile

    out = gather(tab[0:4], ohs[...])
    sent_ghost = []
    for f in range(top):
        ghost_out[f] = chosen(out[:, f * 128 : (f + 1) * 128], lists_ref[f] // 128)
        c = remote(ghost_out.at[f], tab.at[4 + f], gho_s.at[f], gho_r.at[f], partner(f))
        c.start()
        sent_ghost.append(c)

    def look(first, last, into):
        n = (last - first) * 8
        values = tab[first:last].reshape(n, 128)
        split = jnp.concatenate(pieces(values, 3), axis=0).astype(BF16)
        for q in range(4):
            at = slice(q * 384, (q + 1) * 384)
            got = jnp.dot(split, ohn[:, at], preferred_element_type=F32)
            got = got[0:n] + got[n : 2 * n] + got[2 * n : 3 * n]
            for u in range(3):
                j = q * 3 + u
                which = index[j : j + 1, :] // 128
                tile = looked[j] if into else jnp.zeros((8, 128), F32)
                for hi in range(first, last):
                    part = got[(hi - first) * 8 : (hi - first) * 8 + 8, u * 128 : (u + 1) * 128]
                    tile = jnp.where(which == hi, part, tile)
                looked[j] = tile

    look(0, 4, False)
    for c in sent_top:
        c.wait()
    far = jnp.concatenate(
        [jnp.where(low, topbuf[2 * hi], topbuf[2 * hi + 1]) for hi in range(4)], axis=0
    )
    top_list = topbuf[sp, 3:4, :].astype(jnp.int32)
    oht[...] = one_hot(top_list & 127)
    tab[4 + top] = chosen(gather(far, oht[...]), top_list // 128)

    for c in sent_ghost:
        c.wait()
    look(4, 4 + faces, True)

    offs[...] = jnp.zeros(offs.shape, F32)
    for j in range(SLOTS):
        offs[j] = 0.5 * (looked[j] - here)
    x, y, zz = offs[:, 0, :], offs[:, 1, :], offs[:, 2, :]
    squared = x * x + y * y + zz * zz
    j16 = lax.broadcasted_iota(jnp.int32, (16, 128), 0)
    h16 = lax.broadcasted_iota(jnp.int32, (16, 128), 1) // 64
    slot = jnp.where(j16 < 8, j16 + 8 * h16, 8 + j16 + 4 * h16)
    pack[0:8] = jnp.zeros((8, 128), jnp.int32)
    pack[0:1, 0:64] = count_ref[...]
    counts = pack[0:8]
    counts = (counts + swap(counts))[0:1]
    live = jnp.where((slot < counts) & (j16 < SLOTS), 1.0, 0.0)
    inside = 1.0 - squared * (1.0 / 3.5)
    base[0] = squared
    base[1] = inside * inside * live
    base[2] = (-2.0 / 3.5) * inside * live
    mono[0] = jnp.ones((16, 128), F32)
    for m in range(1, len(POWERS)):
        p = list(POWERS[m])
        axis = 2 if p[2] else 1 if p[1] else 0
        by = (x, y, zz)[axis] * (1.0 / p[axis])
        p[axis] -= 1
        mono[m] = mono[PLACE[tuple(p)]] * by
    centre = 0.05 + 0.15 * row8.astype(F32)
    for j in range(SLOTS):
        gap = base[0, j : j + 1, :] - centre
        bell = jnp.exp(-30.0 * gap * gap)
        r = bell * base[1, j : j + 1, :]
        radial[j] = r
        slope_r[j] = r * (-60.0 * gap) + bell * base[2, j : j + 1, :]

    @pl.loop(0, len(POWERS) // 8)
    def _(block):
        rs = [radial[j] for j in range(SLOTS)]
        for u in range(8):
            m = block * 8 + u
            rows = mono[m]
            total = rs[0] * rows[0:1, :]
            for j in range(1, SLOTS):
                total = total + rs[j] * rows[j : j + 1, :]
            dens[m] = total + swap(total)

    def turned(d):
        return jnp.where(low, d, up(d, 2))

    zero = []
    for l in range(8):
        s0 = s1 = s2 = None
        for m in range(STARTS[l], STARTS[l + 1]):
            d = dens[m]
            t = turned(d)
            f = d * SPREAD[m]
            a, b, c = f * d, f * up(t, 1), f * up(t, 2)
            s0, s1, s2 = (a, b, c) if s0 is None else (s0 + a, s1 + b, s2 + c)
        spec[l] = s1
        spec[8 + l] = s2
        zero.append(s0)
    for l in range(4):
        spec[16 + l] = jnp.where(low, zero[l], zero[l + 4])
    twice = jnp.where(low, 2.0, 1.0)

    def times(g):
        return 2.0 if g < 8 else twice if g < 16 else 1.0

    def both(tile):
        row = jnp.sum(tile, axis=0, keepdims=True)
        tile = jnp.broadcast_to(row, (8, 128))
        return tile + swap(tile)

    total = jnp.zeros((8, 128), F32)
    for g in range(20):
        v = spec[g]
        total = total + times(g) * v * v
    scale = lax.rsqrt(both(total) + 1e-06)
    for g in range(0, 20, 2):
        two = jnp.concatenate([spec[g] * scale, spec[g + 1] * scale], axis=0)
        dbuf[0, g * 8 : g * 8 + 16, :] = two.astype(BF16)

    sent_desc = [
        remote(dbuf.at[0], dbuf.at[t], des_s.at[t - 1], des_r.at[t - 1], along(delta[t]))
        for t in range(1, 8)
    ]
    for t in (7, 5, 6, 3, 4, 1, 2):
        sent_desc[t - 1].start()

    wlow = lax.broadcasted_iota(jnp.int32, (ROWS, 128), 1) < 64
    sent_grad = [None] * 8
    for slots in ((0, 1, 2, 3), (4, 5, 6, 7)):
        for t in slots:
            if t:
                sent_desc[t - 1].wait_recv()
        for k in range(2):
            xa = dbuf[slots[2 * k]].astype(F32)
            xb = dbuf[slots[2 * k + 1]].astype(F32)
            at = slice(k * 128, (k + 1) * 128)
            vbuf[0:ROWS, at] = jnp.where(wlow, xa, swap(xb)).astype(BF16)
            vbuf[ROWS : 2 * ROWS, at] = jnp.where(wlow, swap(xa), xb).astype(BF16)
        descs[...] = jnp.dot(spread[...], vbuf[...], preferred_element_type=F32).astype(BF16)
        energy = jnp.zeros((8, 256), F32)
        for c in range(points // CHUNK):
            at = slice(c * CHUNK, (c + 1) * CHUNK)
            score = jnp.dot(sparse[at, :], descs[...], preferred_element_type=F32)
            w = wide[at, :]
            square = score * score
            ws = jnp.concatenate([w, w], axis=1) * square
            energy = energy + jnp.sum((ws * square).reshape(CHUNK // 8, 8, 256), axis=0)
            slopes[at, :] = (ws * score).astype(BF16)
        energy = jnp.sum(energy, axis=0, keepdims=True)
        grad = jnp.dot(folded[...], slopes[...], preferred_element_type=F32)
        for k in range(2):
            a, b = slots[2 * k], slots[2 * k + 1]
            at = slice(k * 128, (k + 1) * 128)
            lo, hi = grad[0:ROWS, at], grad[ROWS : 2 * ROWS, at]
            rbuf[a, 0:ROWS, :] = jnp.where(wlow, lo, swap(hi)).astype(BF16)
            rbuf[b, 0:ROWS, :] = jnp.where(wlow, swap(lo), hi).astype(BF16)
            e = jnp.broadcast_to(energy[:, at], (8, 128))
            for t, mine in ((a, e), (b, swap(e))):
                p = pieces(mine, 3)
                tile = jnp.where(row8 == 0, p[0], jnp.where(row8 == 1, p[1], jnp.where(row8 == 2, p[2], 0.0)))
                tile = jnp.concatenate([tile, jnp.zeros((8, 128), F32)], axis=0)
                rbuf[t, ROWS:BACK, :] = tile.astype(BF16)
        for t in slots:
            if t:
                c = remote(rbuf.at[t], gbuf.at[t - 1], gra_s.at[t - 1], gra_r.at[t - 1], along(-delta[t]))
                c.start()
                sent_grad[t] = c

    summed = rbuf[0].astype(F32)
    for t in range(1, 8):
        sent_grad[t].wait_recv()
        summed = summed + gbuf[t - 1].astype(F32)
    last = summed[ROWS : ROWS + 8, :]
    energy_ref[...] = (0.25 * jnp.sum(last, axis=0, keepdims=True))[:, 0:64]

    dot = jnp.zeros((8, 128), F32)
    for g in range(20):
        dot = dot + summed[g * 8 : g * 8 + 8, :] * spec[g]
    dot = both(dot) * scale
    pull = []
    for g in range(20):
        pull.append(scale * (summed[g * 8 : g * 8 + 8, :] - times(g) * (spec[g] * scale) * dot))
    for l in range(8):
        ha, hb, h0 = pull[l], pull[8 + l], pull[16 + l % 4]
        h0 = swap(h0) if l < 4 else h0
        other = swap(ha)
        k1 = ha
        k2 = jnp.where(low, hb, hb + up(hb, 4))
        k5 = jnp.where(low, up(other, -3), up(other, -1))
        k6 = jnp.where(low, up(hb, -2), 2.0 * h0)
        for m in range(STARTS[l], STARTS[l + 1]):
            t = turned(dens[m])
            v = k1 * up(t, 1) + k2 * up(t, 2) + (k5 * up(t, 5) + k6 * up(t, 6))
            left[m] = (v + swap(v)) * SPREAD[m]

    @pl.loop(0, SLOTS // 4)
    def _(block):
        q = [[None] * 4 for _ in range(4)]

        def add(old, new):
            return new if old is None else old + new

        for m in range(len(POWERS)):
            d = [left[m]]
            if m < STARTS[7]:
                d += [left[raised(m, axis)] for axis in range(3)]
            for u in range(4):
                b = mono[m, pl.ds(block * 4 + u, 1), :]
                for axis in range(len(d)):
                    q[axis][u] = add(q[axis][u], d[axis] * b)
        for u in range(4):
            j = block * 4 + u
            r = radial[j]
            by_square = jnp.sum(slope_r[j] * q[0][u], axis=0, keepdims=True)
            gx, gy, gz = (jnp.sum(r * q[axis][u], axis=0, keepdims=True) for axis in (1, 2, 3))
            straight = jnp.where(row8 == 0, gx, jnp.where(row8 == 1, gy, jnp.where(row8 == 2, gz, 0.0)))
            pulls[j] = 0.5 * straight + offs[j] * by_square

    centre_grad = pulls[0]
    for j in range(1, SLOTS):
        centre_grad = centre_grad + pulls[j]
    centre_grad = centre_grad + swap(centre_grad)

    def placed(tiles, which, first, last):
        rows = []
        split = [pieces(tile, 2) for tile in tiles]
        for p in range(2):
            for hi in range(first, last):
                rows.append(jnp.concatenate(
                    [jnp.where(w == hi, s[p], 0.0) for w, s in zip(which, split)], axis=1
                ))
        return jnp.concatenate(rows, axis=0).astype(BF16)

    over_lanes = (((1,), (1,)), ((), ()))

    def scatter(first, last):
        n = (last - first) * 8
        total = jnp.zeros((n, 128), F32)
        for q in range(4):
            js = range(q * 3, q * 3 + 3)
            which = [index[j : j + 1, :] // 128 for j in js]
            rows = placed([pulls[j] for j in js], which, first, last)
            got = lax.dot_general(
                rows, ohn[:, q * 384 : (q + 1) * 384], over_lanes, preferred_element_type=F32
            )
            total = total + got[0:n] + got[n : 2 * n]
        return total.reshape(last - first, 8, 128)

    gtab[4 : 4 + faces] = scatter(4, 4 + faces)
    sent_back = []
    for f in range(top):
        c = remote(gtab.at[4 + f], gret.at[f], ret_s.at[f], ret_r.at[f], partner(f))
        c.start()
        sent_back.append(c)

    def home(tiles, which, hots):
        got = lax.dot_general(
            placed(tiles, which, 0, 4), hots, over_lanes, preferred_element_type=F32
        )
        return (got[0:32] + got[32:64]).reshape(4, 8, 128)

    topg[...] = home([gtab[4 + top]], [top_list // 128], oht[...])
    sent_top = []
    for d in range(8):
        who = above(d)
        c = remote(topg.at[who[1] // 2], fintop.at[d], fit_s.at[d], fit_r.at[d], who)
        c.start()
        sent_top.append(c)
    own = scatter(0, 4)
    for c in sent_back:
        c.wait_recv()
    which = [lists_ref[f] // 128 for f in range(top)]
    domg[...] = own + home([gret[f] for f in range(top)], which, ohs[...])
    sent_fin = []
    for d in range(1, 8):
        who = peer(d)
        c = remote(domg.at[who[1] // 2], fin.at[d - 1], fin_s.at[d - 1], fin_r.at[d - 1], who)
        c.start()
        sent_fin.append(c)
    mine = domg[sp // 2]
    for d in range(8):
        sent_top[d].wait_recv()
        mine = mine + fintop[d]
    for d in range(1, 8):
        sent_fin[d - 1].wait_recv()
        mine = mine + fin[d - 1]
    odd = jnp.where(lax.rem(sp, 2) == 1, 1, 0)
    mine = jnp.where(odd == 1, swap(mine), mine)
    force_ref[...] = (centre_grad - mine)[0:3, 0:64]
    for c in sent_desc + sent_grad[1:] + sent_back + sent_top + sent_fin:
        c.wait_send()


def body(positions, neighbours, counts, send_lists, sparse_points, weights):
    faces = send_lists.shape[1]
    points = sparse_points.shape[0]
    vmem = pl.BlockSpec(memory_space=pltpu.VMEM)
    hbm = pl.BlockSpec(memory_space=pl.ANY)
    dma = pltpu.SemaphoreType.DMA
    energies, forces = pl.pallas_call(
        lambda *refs: kernel(faces, *refs),
        out_shape=(
            jax.ShapeDtypeStruct((1, 64), F32),
            jax.ShapeDtypeStruct((3, 64), F32),
        ),
        in_specs=[hbm] * 6,
        out_specs=(vmem, vmem),
        scratch_shapes=[
            pltpu.VMEM(positions.shape, F32),
            pltpu.VMEM(neighbours.shape, jnp.int32),
            pltpu.VMEM((1, counts.shape[0]), jnp.int32),
            pltpu.VMEM((faces, 1, 128), jnp.int32),
            pltpu.VMEM((points // 128, 128), F32),
            pltpu.VMEM((8, 8, 128), F32),
            pltpu.VMEM((8, 8, 128), F32),
            pltpu.VMEM((faces - 1, 8, 128), F32),
            pltpu.VMEM((4 + faces, 8, 128), F32),
            pltpu.VMEM((24, 128), jnp.int32),
            pltpu.VMEM((16, 128), jnp.int32),
            pltpu.VMEM((128, (faces - 1) * 128), BF16),
            pltpu.VMEM((128, 128), BF16),
            pltpu.VMEM((128, SLOTS * 128), BF16),
            pltpu.VMEM((SLOTS, 8, 128), F32),
            pltpu.VMEM((16, 8, 128), F32),
            pltpu.VMEM((3, 16, 128), F32),
            pltpu.VMEM((120, 16, 128), F32),
            pltpu.VMEM((SLOTS, 8, 128), F32),
            pltpu.VMEM((SLOTS, 8, 128), F32),
            pltpu.VMEM((120, 8, 128), F32),
            pltpu.VMEM((20, 8, 128), F32),
            pltpu.VMEM((8, ROWS, 128), BF16),
            pltpu.VMEM((8, BACK, 128), BF16),
            pltpu.VMEM((7, BACK, 128), BF16),
            pltpu.VMEM((2 * ROWS, 256), BF16),
            pltpu.VMEM((512, 256), BF16),
            pltpu.VMEM((points, 256), BF16),
            pltpu.VMEM((points, 512), BF16),
            pltpu.VMEM((2 * ROWS, 512), BF16),
            pltpu.VMEM((512, 2 * ROWS), BF16),
            pltpu.VMEM((2 * ROWS, points), BF16),
            pltpu.VMEM((points, 128), F32),
            pltpu.VMEM((120, 8, 128), F32),
            pltpu.VMEM((SLOTS, 8, 128), F32),
            pltpu.VMEM((4 + faces, 8, 128), F32),
            pltpu.VMEM((faces - 1, 8, 128), F32),
            pltpu.VMEM((4, 8, 128), F32),
            pltpu.VMEM((7, 8, 128), F32),
            pltpu.VMEM((4, 8, 128), F32),
            pltpu.VMEM((8, 8, 128), F32),
            dma((6,)),
            dma((7,)), dma((7,)),
            dma((8,)), dma((8,)),
            dma((faces - 1,)), dma((faces - 1,)),
            dma((7,)), dma((7,)),
            dma((7,)), dma((7,)),
            dma((faces - 1,)), dma((faces - 1,)),
            dma((7,)), dma((7,)),
            dma((8,)), dma((8,)),
        ],
        compiler_params=pltpu.CompilerParams(
            collective_id=0, has_side_effects=True, vmem_limit_bytes=60 * 2**20
        ),
        name="gap_forces",
    )(
        positions,
        neighbours,
        counts.reshape(1, -1),
        send_lists.transpose(1, 0, 2),
        sparse_points,
        weights.reshape(-1, 128),
    )
    return energies.reshape(-1), forces


def solution(mesh):
    in_specs = (
        P(None, ("dom", "sp")),
        P(None, ("dom", "sp")),
        P(("dom", "sp")),
        P("dom", None, None),
        P("sp", None),
        P("sp"),
    )
    out_specs = (P(("dom", "sp")), P(None, ("dom", "sp")))
    return jax.shard_map(body, mesh=mesh, in_specs=in_specs, out_specs=out_specs, check_vma=False)
```

```python
import math

import jax
import jax.numpy as jnp
from jax import lax
from jax.experimental import pallas as pl
from jax.experimental.pallas import tpu as pltpu
from jax.sharding import PartitionSpec as P

F32, BF16 = jnp.float32, jnp.bfloat16
MESH = pl.DeviceIdType.MESH
SLOTS = 12
ROWS = 160
BACK = 176
CHUNK = 512


def powers():
    found, starts = [], []
    for degree in range(8):
        starts.append(len(found))
        for a in range(degree, -1, -1):
            for b in range(degree - a, -1, -1):
                found.append((a, b, degree - a - b))
    return found, starts + [len(found)]


POWERS, STARTS = powers()
PLACE = {p: i for i, p in enumerate(POWERS)}
SPREAD = [
    float(math.factorial(sum(p)) * math.prod(math.factorial(e) for e in p)) for p in POWERS
]


FLAT = {(a, b): i for i, (a, b) in enumerate((a, b) for a in range(8) for b in range(8 - a))}


def packed_place(e):
    n, n2, l = e // 64, (e // 8) & 7, e & 7
    r = (n2 - n) & 7
    first = jnp.where(r > 4, n2, n)
    r = jnp.where(r > 4, 8 - r, r)
    group = jnp.where(r == 0, 16 + (l & 3), jnp.where((r & 1) == 1, l, 8 + l))
    half = jnp.where(r == 0, l // 4, jnp.where(r > 2, 1, 0))
    return half * ROWS + group * 8 + first


def up(x, k):
    return x if k % 8 == 0 else pltpu.roll(x, (8 - k) % 8, 0)


def swap(x):
    return pltpu.roll(x, 64, 1)


def pieces(x, count):
    out = []
    for _ in range(count):
        p = x.astype(BF16).astype(F32)
        out.append(p)
        x = x - p
    return out


def one_hot(row):
    return jnp.where(lax.broadcasted_iota(jnp.int32, (128, 128), 0) == row, 1.0, 0.0).astype(BF16)


def kernel(
    faces, pos_hbm, near_hbm, count_hbm, lists_hbm, sparse_hbm, weight_hbm,
    out_ref,
    pos_ref, near_ref, count_ref, lists_ref, weight_ref,
    posbuf, topbuf, ghost_out, tab, pack, index, ohs, oht, ohn, looked, offs, zpow, planar, radial, slope_r, dens,
    spec, dbuf, rbuf, gbuf, vbuf, descs, slopes, sparse, fold, spread, folded, wide, left, pulls,
    gtab, gret, domg, fin, topg, fintop,
    local_sem, pos_s, pos_r, top_s, top_r, gho_s, gho_r, des_s, des_r, gra_s, gra_r, ret_s, ret_r, fin_s, fin_r, fit_s, fit_r,
):
    dom, sp = lax.axis_index("dom"), lax.axis_index("sp")
    n_dom, n_sp = lax.axis_size("dom"), lax.axis_size("sp")
    below = n_dom // 2
    ring = 2 * n_sp
    z = (dom // below) * n_sp + sp
    rest = lax.rem(dom, below)
    side = 1 - 2 * lax.rem(dom, 2)

    def along(delta):
        there = lax.rem(z + delta + ring, ring)
        return (rest + (there // n_sp) * below, lax.rem(there, n_sp))

    def peer(delta):
        return (dom, lax.rem(sp + delta, n_sp))

    def partner(face):
        bit = lax.rem(dom // 2**face, 2)
        return (dom + (1 - 2 * bit) * 2**face, sp)

    delta = [0, 1, -1, 2, -2, 3, -3, 4 * side]
    lane = lax.broadcasted_iota(jnp.int32, (8, 128), 1)
    low = lane < 64
    row8 = lax.broadcasted_iota(jnp.int32, (8, 128), 0)

    def above(d):
        return (lax.rem(dom + below, n_dom), lax.rem(sp + d, n_sp))

    pairs = [
        (pos_hbm, pos_ref), (lists_hbm, lists_ref), (near_hbm, near_ref), (count_hbm, count_ref),
        (weight_hbm, weight_ref), (sparse_hbm, sparse),
    ]
    loads = [pltpu.make_async_copy(a, b, local_sem.at[i]) for i, (a, b) in enumerate(pairs)]
    for load in loads:
        load.start()

    barrier = pltpu.get_barrier_semaphore()
    greeted = [peer(d) for d in range(1, 8)] + [partner(f) for f in range(faces - 1)]
    greeted += [along(d) for d in (1, -1, 2, -2, 3, -3, 4, -4)] + [above(d) for d in range(8)]
    for who in greeted:
        pl.semaphore_signal(barrier, inc=1, device_id=who, device_id_type=MESH)

    loads[0].wait()
    loads[1].wait()
    top = faces - 1
    posbuf[sp] = jnp.zeros((8, 128), F32)
    posbuf[sp, 0:3, 0:64] = pos_ref[...]
    here = posbuf[sp]
    here = here + swap(here)
    here = jnp.where(row8 == 3, lists_ref[top].astype(F32), here)
    posbuf[sp] = here
    for load in loads[2:5]:
        load.wait()
    for f in range(top):
        ohs[:, f * 128 : (f + 1) * 128] = one_hot(lists_ref[f] & 127)
    pack[...] = jnp.zeros((24, 128), jnp.int32)
    pack[:, 0:64] = near_ref[...]
    index[0:8] = jnp.where(low, pack[0:8], swap(pack[8:16]))
    last = pack[16:24]
    last = jnp.where(low, last, swap(pltpu.roll(last, 4, 0)))
    index[8:16] = jnp.where(row8 < 4, last, 0)
    for j in range(SLOTS):
        ohn[:, j * 128 : (j + 1) * 128] = one_hot(index[j : j + 1, :] & 127)
    pl.semaphore_wait(barrier, len(greeted))

    def remote(src, dst, s, r, who):
        return pltpu.make_async_remote_copy(
            src_ref=src, dst_ref=dst, send_sem=s, recv_sem=r, device_id=who, device_id_type=MESH
        )

    sent_pos = [
        remote(posbuf.at[sp], posbuf.at[sp], pos_s.at[d - 1], pos_r.at[d - 1], peer(d))
        for d in range(1, 8)
    ]
    for c in sent_pos:
        c.start()

    sent_top = [
        remote(posbuf.at[sp], topbuf.at[sp], top_s.at[d], top_r.at[d], above(d)) for d in range(8)
    ]
    for c in sent_top:
        c.start()

    place = packed_place(lax.broadcasted_iota(jnp.int32, (8, 512), 1))[0:1]
    numbers = lax.broadcasted_iota(jnp.int32, (2 * ROWS, 512), 0)
    fold[...] = jnp.where(numbers == place, 1.0, 0.0).astype(BF16)
    place = packed_place(lax.broadcasted_iota(jnp.int32, (512, 128), 0))
    for k in range(0, 2 * ROWS, 128):
        n = min(128, 2 * ROWS - k)
        numbers = k + lax.broadcasted_iota(jnp.int32, (512, 128), 1)
        spread[:, k : k + n] = jnp.where(numbers == place, 1.0, 0.0).astype(BF16)[:, 0:n]
    for load in loads[5:]:
        load.wait()
    points = sparse.shape[0]

    @pl.loop(0, points // 128)
    def _(c):
        column = jnp.broadcast_to(4.0 * weight_ref[pl.ds(c, 1), :], (128, 128)).T
        wide[pl.ds(pl.multiple_of(c * 128, 128), 128), :] = column

    @pl.loop(0, points // CHUNK)
    def _(c):
        at = pl.ds(pl.multiple_of(c * CHUNK, CHUNK), CHUNK)
        folded[:, at] = lax.dot_general(
            fold[...], sparse[at, :], (((1,), (1,)), ((), ())), preferred_element_type=F32
        ).astype(BF16)

    for c in sent_pos:
        c.wait()

    for hi in range(4):
        tab[hi] = jnp.where(low, posbuf[2 * hi], posbuf[2 * hi + 1])

    def gather(tiles, hots):
        parts = jnp.concatenate(pieces(tiles.reshape(32, 128), 3), axis=0).astype(BF16)
        out = jnp.dot(parts, hots, preferred_element_type=F32)
        return out[0:32] + out[32:64] + out[64:96]

    def chosen(out, which):
        tile = jnp.zeros((8, 128), F32)
        for hi in range(4):
            tile = jnp.where(which == hi, out[hi * 8 : hi * 8 + 8], tile)
        return tile

    out = gather(tab[0:4], ohs[...])
    sent_ghost = []
    for f in range(top):
        ghost_out[f] = chosen(out[:, f * 128 : (f + 1) * 128], lists_ref[f] // 128)
        c = remote(ghost_out.at[f], tab.at[4 + f], gho_s.at[f], gho_r.at[f], partner(f))
        c.start()
        sent_ghost.append(c)

    def look(first, last, into):
        n = (last - first) * 8
        values = tab[first:last].reshape(n, 128)
        split = jnp.concatenate(pieces(values, 3), axis=0).astype(BF16)
        for q in range(4):
            at = slice(q * 384, (q + 1) * 384)
            got = jnp.dot(split, ohn[:, at], preferred_element_type=F32)
            got = got[0:n] + got[n : 2 * n] + got[2 * n : 3 * n]
            for u in range(3):
                j = q * 3 + u
                which = index[j : j + 1, :] // 128
                tile = looked[j] if into else jnp.zeros((8, 128), F32)
                for hi in range(first, last):
                    part = got[(hi - first) * 8 : (hi - first) * 8 + 8, u * 128 : (u + 1) * 128]
                    tile = jnp.where(which == hi, part, tile)
                looked[j] = tile

    look(0, 4, False)
    for c in sent_top:
        c.wait()
    far = jnp.concatenate(
        [jnp.where(low, topbuf[2 * hi], topbuf[2 * hi + 1]) for hi in range(4)], axis=0
    )
    top_list = topbuf[sp, 3:4, :].astype(jnp.int32)
    oht[...] = one_hot(top_list & 127)
    tab[4 + top] = chosen(gather(far, oht[...]), top_list // 128)

    for c in sent_ghost:
        c.wait()
    look(4, 4 + faces, True)

    pack[0:8] = jnp.zeros((8, 128), jnp.int32)
    pack[0:1, 0:64] = count_ref[...]
    counts = pack[0:8]
    counts = jnp.broadcast_to((counts + swap(counts))[0:1], (8, 128))
    upper = lane // 64
    centre = 0.05 + 0.15 * row8.astype(F32)
    for j in range(SLOTS):
        off = 0.5 * (looked[j] - here)
        offs[j] = off
        x, y, zz = (jnp.broadcast_to(off[axis : axis + 1], (8, 128)) for axis in range(3))
        squared = x * x + y * y + zz * zz
        slot = j + 8 * upper if j < 8 else 8 + j + 4 * upper
        live = jnp.where(slot < counts, 1.0, 0.0)
        inside = 1.0 - squared * (1.0 / 3.5)
        gap = squared - centre
        bell = jnp.exp(-30.0 * gap * gap) * live
        r = bell * (inside * inside)
        radial[j] = r
        slope_r[j] = r * (-60.0 * gap) + bell * ((-2.0 / 3.5) * inside)
        power = {0: None}
        for c in range(1, 8):
            power[c] = zz if c == 1 else power[c - 1] * (zz * (1.0 / c))
            zpow[j, c - 1] = power[c]
        ys = [None]
        for c in range(1, 8):
            ys.append(y if c == 1 else ys[c - 1] * (y * (1.0 / c)))
        xs = None
        for c in range(8):
            xs = None if c == 0 else x if c == 1 else xs * (x * (1.0 / c))
            for d in range(8 - c):
                if c + d:
                    planar[j, FLAT[c, d] - 1] = xs if d == 0 else ys[d] if c == 0 else xs * ys[d]

    for (a, b), at in FLAT.items():
        rs = [radial[j] for j in range(SLOTS)]
        if at:
            rs = [r * planar[j, at - 1] for j, r in enumerate(rs)]
        for c in range(8 - a - b):
            terms = [r if c == 0 else r * zpow[j, c - 1] for j, r in enumerate(rs)]
            while len(terms) > 1:
                terms = [sum(terms[i : i + 2][1:], terms[i]) for i in range(0, len(terms), 2)]
            dens[PLACE[a, b, c]] = terms[0] + swap(terms[0])

    def turned(d):
        return jnp.where(low, d, up(d, 2))

    zero = []
    for l in range(8):
        s0 = s1 = s2 = None
        for m in range(STARTS[l], STARTS[l + 1]):
            d = dens[m]
            t = turned(d)
            f = d * SPREAD[m]
            a, b, c = f * d, f * up(t, 1), f * up(t, 2)
            s0, s1, s2 = (a, b, c) if s0 is None else (s0 + a, s1 + b, s2 + c)
        spec[l] = s1
        spec[8 + l] = s2
        zero.append(s0)
    for l in range(4):
        spec[16 + l] = jnp.where(low, zero[l], zero[l + 4])
    twice = jnp.where(low, 2.0, 1.0)

    def times(g):
        return 2.0 if g < 8 else twice if g < 16 else 1.0

    def both(tile):
        row = jnp.sum(tile, axis=0, keepdims=True)
        tile = jnp.broadcast_to(row, (8, 128))
        return tile + swap(tile)

    total = jnp.zeros((8, 128), F32)
    for g in range(20):
        v = spec[g]
        total = total + times(g) * v * v
    scale = lax.rsqrt(both(total) + 1e-06)
    for g in range(0, 20, 2):
        two = jnp.concatenate([spec[g] * scale, spec[g + 1] * scale], axis=0)
        dbuf[0, g * 8 : g * 8 + 16, :] = two.astype(BF16)

    sent_desc = [
        remote(dbuf.at[0], dbuf.at[t], des_s.at[t - 1], des_r.at[t - 1], along(delta[t]))
        for t in range(1, 8)
    ]
    for t in (7, 5, 6, 3, 4, 1, 2):
        sent_desc[t - 1].start()

    wlow = lax.broadcasted_iota(jnp.int32, (ROWS, 128), 1) < 64
    sent_grad = [None] * 8
    for slots in ((7, 5, 6, 0), (3, 4, 1, 2)):
        for t in slots:
            if t:
                sent_desc[t - 1].wait_recv()
        for k in range(2):
            xa = dbuf[slots[2 * k]].astype(F32)
            xb = dbuf[slots[2 * k + 1]].astype(F32)
            at = slice(k * 128, (k + 1) * 128)
            vbuf[0:ROWS, at] = jnp.where(wlow, xa, swap(xb)).astype(BF16)
            vbuf[ROWS : 2 * ROWS, at] = jnp.where(wlow, swap(xa), xb).astype(BF16)
        descs[...] = jnp.dot(spread[...], vbuf[...], preferred_element_type=F32).astype(BF16)
        energy = jnp.zeros((8, 256), F32)
        for c in range(points // CHUNK):
            at = slice(c * CHUNK, (c + 1) * CHUNK)
            score = jnp.dot(sparse[at, :], descs[...], preferred_element_type=F32)
            w = wide[at, :]
            square = score * score
            ws = jnp.concatenate([w, w], axis=1) * square
            energy = energy + jnp.sum((ws * square).reshape(CHUNK // 8, 8, 256), axis=0)
            slopes[at, :] = (ws * score).astype(BF16)
        energy = jnp.sum(energy, axis=0, keepdims=True)
        grad = jnp.dot(folded[...], slopes[...], preferred_element_type=F32)
        for k in range(2):
            a, b = slots[2 * k], slots[2 * k + 1]
            at = slice(k * 128, (k + 1) * 128)
            lo, hi = grad[0:ROWS, at], grad[ROWS : 2 * ROWS, at]
            rbuf[a, 0:ROWS, :] = jnp.where(wlow, lo, swap(hi)).astype(BF16)
            rbuf[b, 0:ROWS, :] = jnp.where(wlow, swap(lo), hi).astype(BF16)
            e = jnp.broadcast_to(energy[:, at], (8, 128))
            for t, mine in ((a, e), (b, swap(e))):
                p = pieces(mine, 3)
                tile = jnp.where(row8 == 0, p[0], jnp.where(row8 == 1, p[1], jnp.where(row8 == 2, p[2], 0.0)))
                tile = jnp.concatenate([tile, jnp.zeros((8, 128), F32)], axis=0)
                rbuf[t, ROWS:BACK, :] = tile.astype(BF16)
        for t in slots:
            if t:
                c = remote(rbuf.at[t], gbuf.at[t - 1], gra_s.at[t - 1], gra_r.at[t - 1], along(-delta[t]))
                c.start()
                sent_grad[t] = c

    summed = rbuf[0].astype(F32)
    for t in range(1, 8):
        sent_grad[t].wait_recv()
        summed = summed + gbuf[t - 1].astype(F32)
    last = summed[ROWS : ROWS + 8, :]
    energy = 0.25 * jnp.sum(last, axis=0, keepdims=True)

    dot = jnp.zeros((8, 128), F32)
    for g in range(20):
        dot = dot + summed[g * 8 : g * 8 + 8, :] * spec[g]
    dot = both(dot) * scale
    pull = []
    for g in range(20):
        pull.append(scale * (summed[g * 8 : g * 8 + 8, :] - times(g) * (spec[g] * scale) * dot))
    for l in range(8):
        ha, hb, h0 = pull[l], pull[8 + l], pull[16 + l % 4]
        h0 = swap(h0) if l < 4 else h0
        other = swap(ha)
        k1 = ha
        k2 = jnp.where(low, hb, hb + up(hb, 4))
        k5 = jnp.where(low, up(other, -3), up(other, -1))
        k6 = jnp.where(low, up(hb, -2), 2.0 * h0)
        for m in range(STARTS[l], STARTS[l + 1]):
            t = turned(dens[m])
            v = k1 * up(t, 1) + k2 * up(t, 2) + (k5 * up(t, 5) + k6 * up(t, 6))
            left[m] = (v + swap(v)) * SPREAD[m]

    @pl.loop(0, SLOTS // 3)
    def _(block):
        js = [block * 3 + u for u in range(3)]
        zp = [[None] + [zpow[j, c] for c in range(7)] for j in js]
        q = [[None] * 3 for _ in range(4)]

        def add(old, new):
            return new if old is None else old + new

        def mul(tile, factor):
            return tile if factor is None else tile * factor

        for (a, b), at in FLAT.items():
            level, deriv = [None] * 3, [None] * 3
            for c in range(8 - a - b):
                d = left[PLACE[a, b, c]]
                for u in range(3):
                    level[u] = add(level[u], mul(d, zp[u][c]))
                    if c:
                        deriv[u] = add(deriv[u], mul(d, zp[u][c - 1]))
            for u, j in enumerate(js):
                flat = planar[j, at - 1] if at else None
                q[0][u] = add(q[0][u], mul(level[u], flat))
                if deriv[u] is not None:
                    q[3][u] = add(q[3][u], mul(deriv[u], flat))
                for axis, lower in ((1, (a - 1, b)), (2, (a, b - 1))):
                    if lower in FLAT:
                        flat = planar[j, FLAT[lower] - 1] if FLAT[lower] else None
                        q[axis][u] = add(q[axis][u], mul(level[u], flat))
        for u, j in enumerate(js):
            r = radial[j]
            by_square = jnp.sum(slope_r[j] * q[0][u], axis=0, keepdims=True)
            gx, gy, gz = (jnp.sum(r * q[axis][u], axis=0, keepdims=True) for axis in (1, 2, 3))
            straight = jnp.where(row8 == 0, gx, jnp.where(row8 == 1, gy, jnp.where(row8 == 2, gz, 0.0)))
            pulls[j] = 0.5 * straight + offs[j] * by_square

    centre_grad = pulls[0]
    for j in range(1, SLOTS):
        centre_grad = centre_grad + pulls[j]
    centre_grad = centre_grad + swap(centre_grad)

    def placed(tiles, which, first, last):
        rows = []
        split = [pieces(tile, 2) for tile in tiles]
        for p in range(2):
            for hi in range(first, last):
                rows.append(jnp.concatenate(
                    [jnp.where(w == hi, s[p], 0.0) for w, s in zip(which, split)], axis=1
                ))
        return jnp.concatenate(rows, axis=0).astype(BF16)

    over_lanes = (((1,), (1,)), ((), ()))

    def scatter(first, last):
        n = (last - first) * 8
        total = jnp.zeros((n, 128), F32)
        for q in range(4):
            js = range(q * 3, q * 3 + 3)
            which = [index[j : j + 1, :] // 128 for j in js]
            rows = placed([pulls[j] for j in js], which, first, last)
            got = lax.dot_general(
                rows, ohn[:, q * 384 : (q + 1) * 384], over_lanes, preferred_element_type=F32
            )
            total = total + got[0:n] + got[n : 2 * n]
        return total.reshape(last - first, 8, 128)

    gtab[4 : 4 + faces] = scatter(4, 4 + faces)
    sent_back = []
    for f in range(top):
        c = remote(gtab.at[4 + f], gret.at[f], ret_s.at[f], ret_r.at[f], partner(f))
        c.start()
        sent_back.append(c)

    def home(tiles, which, hots):
        got = lax.dot_general(
            placed(tiles, which, 0, 4), hots, over_lanes, preferred_element_type=F32
        )
        return (got[0:32] + got[32:64]).reshape(4, 8, 128)

    topg[...] = home([gtab[4 + top]], [top_list // 128], oht[...])
    sent_top = []
    for d in range(8):
        who = above(d)
        c = remote(topg.at[who[1] // 2], fintop.at[d], fit_s.at[d], fit_r.at[d], who)
        c.start()
        sent_top.append(c)
    own = scatter(0, 4)
    for c in sent_back:
        c.wait_recv()
    which = [lists_ref[f] // 128 for f in range(top)]
    domg[...] = own + home([gret[f] for f in range(top)], which, ohs[...])
    sent_fin = []
    for d in range(1, 8):
        who = peer(d)
        c = remote(domg.at[who[1] // 2], fin.at[d - 1], fin_s.at[d - 1], fin_r.at[d - 1], who)
        c.start()
        sent_fin.append(c)
    mine = domg[sp // 2]
    for d in range(8):
        sent_top[d].wait_recv()
        mine = mine + fintop[d]
    for d in range(1, 8):
        sent_fin[d - 1].wait_recv()
        mine = mine + fin[d - 1]
    odd = jnp.where(lax.rem(sp, 2) == 1, 1, 0)
    mine = jnp.where(odd == 1, swap(mine), mine)
    out_ref[...] = jnp.where(row8 == 3, energy, centre_grad - mine)
    for c in sent_desc + sent_grad[1:] + sent_back + sent_top + sent_fin:
        c.wait_send()


def body(positions, neighbours, counts, send_lists, sparse_points, weights):
    faces = send_lists.shape[1]
    points = sparse_points.shape[0]
    vmem = pl.BlockSpec(memory_space=pltpu.VMEM)
    hbm = pl.BlockSpec(memory_space=pl.ANY)
    dma = pltpu.SemaphoreType.DMA
    out = pl.pallas_call(
        lambda *refs: kernel(faces, *refs),
        out_shape=jax.ShapeDtypeStruct((8, 128), F32),
        in_specs=[hbm] * 6,
        out_specs=vmem,
        scratch_shapes=[
            pltpu.VMEM(positions.shape, F32),
            pltpu.VMEM(neighbours.shape, jnp.int32),
            pltpu.VMEM((1, counts.shape[0]), jnp.int32),
            pltpu.VMEM((faces, 1, 128), jnp.int32),
            pltpu.VMEM((points // 128, 128), F32),
            pltpu.VMEM((8, 8, 128), F32),
            pltpu.VMEM((8, 8, 128), F32),
            pltpu.VMEM((faces - 1, 8, 128), F32),
            pltpu.VMEM((4 + faces, 8, 128), F32),
            pltpu.VMEM((24, 128), jnp.int32),
            pltpu.VMEM((16, 128), jnp.int32),
            pltpu.VMEM((128, (faces - 1) * 128), BF16),
            pltpu.VMEM((128, 128), BF16),
            pltpu.VMEM((128, SLOTS * 128), BF16),
            pltpu.VMEM((SLOTS, 8, 128), F32),
            pltpu.VMEM((SLOTS, 8, 128), F32),
            pltpu.VMEM((SLOTS, 7, 8, 128), F32),
            pltpu.VMEM((SLOTS, 35, 8, 128), F32),
            pltpu.VMEM((SLOTS, 8, 128), F32),
            pltpu.VMEM((SLOTS, 8, 128), F32),
            pltpu.VMEM((120, 8, 128), F32),
            pltpu.VMEM((20, 8, 128), F32),
            pltpu.VMEM((8, ROWS, 128), BF16),
            pltpu.VMEM((8, BACK, 128), BF16),
            pltpu.VMEM((7, BACK, 128), BF16),
            pltpu.VMEM((2 * ROWS, 256), BF16),
            pltpu.VMEM((512, 256), BF16),
            pltpu.VMEM((points, 256), BF16),
            pltpu.VMEM((points, 512), BF16),
            pltpu.VMEM((2 * ROWS, 512), BF16),
            pltpu.VMEM((512, 2 * ROWS), BF16),
            pltpu.VMEM((2 * ROWS, points), BF16),
            pltpu.VMEM((points, 128), F32),
            pltpu.VMEM((120, 8, 128), F32),
            pltpu.VMEM((SLOTS, 8, 128), F32),
            pltpu.VMEM((4 + faces, 8, 128), F32),
            pltpu.VMEM((faces - 1, 8, 128), F32),
            pltpu.VMEM((4, 8, 128), F32),
            pltpu.VMEM((7, 8, 128), F32),
            pltpu.VMEM((4, 8, 128), F32),
            pltpu.VMEM((8, 8, 128), F32),
            dma((6,)),
            dma((7,)), dma((7,)),
            dma((8,)), dma((8,)),
            dma((faces - 1,)), dma((faces - 1,)),
            dma((7,)), dma((7,)),
            dma((7,)), dma((7,)),
            dma((faces - 1,)), dma((faces - 1,)),
            dma((7,)), dma((7,)),
            dma((8,)), dma((8,)),
        ],
        compiler_params=pltpu.CompilerParams(
            collective_id=0, has_side_effects=True, vmem_limit_bytes=60 * 2**20
        ),
        name="gap_forces",
    )(
        positions,
        neighbours,
        counts.reshape(1, -1),
        send_lists.transpose(1, 0, 2),
        sparse_points,
        weights.reshape(-1, 128),
    )
    return out[3, 0:64], out[0:3, 0:64]


def solution(mesh):
    in_specs = (
        P(None, ("dom", "sp")),
        P(None, ("dom", "sp")),
        P(("dom", "sp")),
        P("dom", None, None),
        P("sp", None),
        P("sp"),
    )
    out_specs = (P(("dom", "sp")), P(None, ("dom", "sp")))
    return jax.shard_map(body, mesh=mesh, in_specs=in_specs, out_specs=out_specs, check_vma=False)
```

```python
import math

import jax
import jax.numpy as jnp
from jax import lax
from jax.experimental import pallas as pl
from jax.experimental.pallas import tpu as pltpu
from jax.sharding import PartitionSpec as P

F32, BF16 = jnp.float32, jnp.bfloat16
MESH = pl.DeviceIdType.MESH
SLOTS = 12
ROWS = 144
BACK = 160
CHUNK = 512
FAR = (7, 1, 6, 2, 5, 3, 4)


def powers():
    found, starts = [], []
    for degree in range(8):
        starts.append(len(found))
        for a in range(degree, -1, -1):
            for b in range(degree - a, -1, -1):
                found.append((a, b, degree - a - b))
    return found, starts + [len(found)]


POWERS, STARTS = powers()
PLACE = {p: i for i, p in enumerate(POWERS)}
SPREAD = [
    float(math.factorial(sum(p)) * math.prod(math.factorial(e) for e in p)) for p in POWERS
]


FLAT = {(a, b): i for i, (a, b) in enumerate((a, b) for a in range(8) for b in range(8 - a))}


def packed_place(e):
    n, n2, l = e // 64, (e // 8) & 7, e & 7
    r = (n2 - n) & 7
    first = jnp.where(r > 4, n2, n)
    r = jnp.where(r > 4, 8 - r, r)
    row = jnp.where(r == 4, (first & 3) + 4 * (l & 1), first)
    diagonal = jnp.where(l < 4, 12 + l, 16 + (l & 1))
    group = jnp.where(
        r == 0, diagonal, jnp.where(r == 4, 8 + l // 2, jnp.where(r == 2, 8 + l, l))
    )
    half = jnp.where(r == 0, jnp.where((l == 4) | (l == 5), 0, 1), jnp.where(r > 2, 1, 0))
    return half * ROWS + group * 8 + row


def up(x, k):
    return x if k % 8 == 0 else pltpu.roll(x, (8 - k) % 8, 0)


def swap(x):
    return pltpu.roll(x, 64, 1)


def pieces(x, count):
    out = []
    for _ in range(count):
        p = x.astype(BF16).astype(F32)
        out.append(p)
        x = x - p
    return out


def one_hot(row):
    return jnp.where(lax.broadcasted_iota(jnp.int32, (128, 128), 0) == row, 1.0, 0.0).astype(BF16)


def kernel(
    faces, pos_hbm, near_hbm, count_hbm, lists_hbm, sparse_hbm, weight_hbm,
    out_ref,
    pos_ref, near_ref, count_ref, lists_ref, weight_ref,
    posbuf, topbuf, ghost_out, tab, pack, index, ohs, oht, ohn, looked, offs, zpow, planar, ahead, radial, slope_r, dens,
    spec, dbuf, rbuf, gbuf, vbuf, descs, slopes, sparse, fold, spread, folded, wide, left, pulls,
    gtab, gret, domg, fin, topg, fintop,
    local_sem, pos_s, pos_r, top_s, top_r, gho_s, gho_r, des_s, des_r, gra_s, gra_r, ret_s, ret_r, fin_s, fin_r, fit_s, fit_r,
):
    dom, sp = lax.axis_index("dom"), lax.axis_index("sp")
    n_dom, n_sp = lax.axis_size("dom"), lax.axis_size("sp")
    below = n_dom // 2
    ring = 2 * n_sp
    z = (dom // below) * n_sp + sp
    rest = lax.rem(dom, below)
    side = 1 - 2 * lax.rem(dom, 2)

    def along(delta):
        there = lax.rem(z + delta + ring, ring)
        return (rest + (there // n_sp) * below, lax.rem(there, n_sp))

    def peer(delta):
        return (dom, lax.rem(sp + delta, n_sp))

    def partner(face):
        bit = lax.rem(dom // 2**face, 2)
        return (dom + (1 - 2 * bit) * 2**face, sp)

    delta = [0, 1, -1, 2, -2, 3, -3, 4 * side]
    lane = lax.broadcasted_iota(jnp.int32, (8, 128), 1)
    low = lane < 64
    row8 = lax.broadcasted_iota(jnp.int32, (8, 128), 0)

    def above(d):
        return (lax.rem(dom + below, n_dom), lax.rem(sp + d, n_sp))

    barrier = pltpu.get_barrier_semaphore()
    greeted = [above(d) for d in (0, 1, 7, 2, 6, 3, 5, 4)] + [peer(d) for d in FAR]
    greeted += [along(d) for d in (4, -4, 3, -3, 2, -2, 1, -1)]
    greeted += [partner(f) for f in reversed(range(faces - 1))]
    for who in greeted:
        pl.semaphore_signal(barrier, inc=1, device_id=who, device_id_type=MESH)

    pairs = [
        (pos_hbm, pos_ref), (lists_hbm, lists_ref), (near_hbm, near_ref), (count_hbm, count_ref),
        (weight_hbm, weight_ref), (sparse_hbm, sparse),
    ]
    loads = [pltpu.make_async_copy(a, b, local_sem.at[i]) for i, (a, b) in enumerate(pairs)]
    for load in loads:
        load.start()

    loads[0].wait()
    loads[1].wait()
    top = faces - 1
    posbuf[sp] = jnp.zeros((8, 128), F32)
    posbuf[sp, 0:3, 0:64] = pos_ref[...]
    here = posbuf[sp]
    here = here + swap(here)
    here = jnp.where(row8 == 3, lists_ref[top].astype(F32), here)
    posbuf[sp] = here
    for load in loads[2:5]:
        load.wait()
    for f in range(top):
        ohs[:, f * 128 : (f + 1) * 128] = one_hot(lists_ref[f] & 127)
    pack[...] = jnp.zeros((24, 128), jnp.int32)
    pack[:, 0:64] = near_ref[...]
    index[0:8] = jnp.where(low, pack[0:8], swap(pack[8:16]))
    last = pack[16:24]
    last = jnp.where(low, last, swap(pltpu.roll(last, 4, 0)))
    index[8:16] = jnp.where(row8 < 4, last, 0)
    for j in range(SLOTS):
        ohn[:, j * 128 : (j + 1) * 128] = one_hot(index[j : j + 1, :] & 127)
    pl.semaphore_wait(barrier, len(greeted))

    def remote(src, dst, s, r, who):
        return pltpu.make_async_remote_copy(
            src_ref=src, dst_ref=dst, send_sem=s, recv_sem=r, device_id=who, device_id_type=MESH
        )

    sent_pos = [
        remote(posbuf.at[sp], posbuf.at[sp], pos_s.at[d - 1], pos_r.at[d - 1], peer(d))
        for d in range(1, 8)
    ]
    for d in FAR:
        sent_pos[d - 1].start()

    sent_top = [
        remote(posbuf.at[sp], topbuf.at[sp], top_s.at[d], top_r.at[d], above(d)) for d in range(8)
    ]
    for d in (0, 1, 7, 2, 6, 3, 5, 4):
        sent_top[d].start()

    place = packed_place(lax.broadcasted_iota(jnp.int32, (8, 512), 1))[0:1]
    numbers = lax.broadcasted_iota(jnp.int32, (2 * ROWS, 512), 0)
    fold[...] = jnp.where(numbers == place, 1.0, 0.0).astype(BF16)
    place = packed_place(lax.broadcasted_iota(jnp.int32, (512, 128), 0))
    for k in range(0, 2 * ROWS, 128):
        n = min(128, 2 * ROWS - k)
        numbers = k + lax.broadcasted_iota(jnp.int32, (512, 128), 1)
        spread[:, k : k + n] = jnp.where(numbers == place, 1.0, 0.0).astype(BF16)[:, 0:n]
    for load in loads[5:]:
        load.wait()
    points = sparse.shape[0]

    @pl.loop(0, points // 128)
    def _(c):
        column = jnp.broadcast_to(4.0 * weight_ref[pl.ds(c, 1), :], (128, 128)).T
        wide[pl.ds(pl.multiple_of(c * 128, 128), 128), :] = column

    @pl.loop(0, points // CHUNK)
    def _(c):
        at = pl.ds(pl.multiple_of(c * CHUNK, CHUNK), CHUNK)
        folded[:, at] = lax.dot_general(
            fold[...], sparse[at, :], (((1,), (1,)), ((), ())), preferred_element_type=F32
        ).astype(BF16)

    for c in sent_pos:
        c.wait()

    for hi in range(4):
        tab[hi] = jnp.where(low, posbuf[2 * hi], posbuf[2 * hi + 1])

    def gather(tiles, hots):
        parts = jnp.concatenate(pieces(tiles.reshape(32, 128), 3), axis=0).astype(BF16)
        out = jnp.dot(parts, hots, preferred_element_type=F32)
        return out[0:32] + out[32:64] + out[64:96]

    def chosen(out, which):
        tile = jnp.zeros((8, 128), F32)
        for hi in range(4):
            tile = jnp.where(which == hi, out[hi * 8 : hi * 8 + 8], tile)
        return tile

    out = gather(tab[0:4], ohs[...])
    sent_ghost = []
    for f in range(top):
        ghost_out[f] = chosen(out[:, f * 128 : (f + 1) * 128], lists_ref[f] // 128)
        c = remote(ghost_out.at[f], tab.at[4 + f], gho_s.at[f], gho_r.at[f], partner(f))
        c.start()
        sent_ghost.append(c)

    def look(first, last, into):
        n = (last - first) * 8
        values = tab[first:last].reshape(n, 128)
        split = jnp.concatenate(pieces(values, 3), axis=0).astype(BF16)
        for q in range(4):
            at = slice(q * 384, (q + 1) * 384)
            got = jnp.dot(split, ohn[:, at], preferred_element_type=F32)
            got = got[0:n] + got[n : 2 * n] + got[2 * n : 3 * n]
            for u in range(3):
                j = q * 3 + u
                which = index[j : j + 1, :] // 128
                tile = looked[j] if into else jnp.zeros((8, 128), F32)
                for hi in range(first, last):
                    part = got[(hi - first) * 8 : (hi - first) * 8 + 8, u * 128 : (u + 1) * 128]
                    tile = jnp.where(which == hi, part, tile)
                looked[j] = tile

    look(0, 4, False)
    for c in sent_top:
        c.wait()
    far = jnp.concatenate(
        [jnp.where(low, topbuf[2 * hi], topbuf[2 * hi + 1]) for hi in range(4)], axis=0
    )
    top_list = topbuf[sp, 3:4, :].astype(jnp.int32)
    oht[...] = one_hot(top_list & 127)
    tab[4 + top] = chosen(gather(far, oht[...]), top_list // 128)

    for c in sent_ghost:
        c.wait()
    look(4, 4 + faces, True)

    pack[0:8] = jnp.zeros((8, 128), jnp.int32)
    pack[0:1, 0:64] = count_ref[...]
    counts = pack[0:8]
    counts = jnp.broadcast_to((counts + swap(counts))[0:1], (8, 128))
    upper = lane // 64
    centre = 0.05 + 0.15 * row8.astype(F32)
    for j in range(SLOTS):
        off = 0.5 * (looked[j] - here)
        offs[j] = off
        x, y, zz = (jnp.broadcast_to(off[axis : axis + 1], (8, 128)) for axis in range(3))
        squared = x * x + y * y + zz * zz
        slot = j + 8 * upper if j < 8 else 8 + j + 4 * upper
        live = jnp.where(slot < counts, 1.0, 0.0)
        inside = 1.0 - squared * (1.0 / 3.5)
        gap = squared - centre
        bell = jnp.exp(-30.0 * gap * gap) * live
        r = bell * (inside * inside)
        radial[j] = r
        slope_r[j] = r * (-60.0 * gap) + bell * ((-2.0 / 3.5) * inside)
        power = {0: None}
        for c in range(1, 8):
            power[c] = zz if c == 1 else power[c - 1] * (zz * (1.0 / c))
            zpow[j, c - 1] = power[c]
        ys = [None]
        for c in range(1, 8):
            ys.append(y if c == 1 else ys[c - 1] * (y * (1.0 / c)))
        xs = None
        for c in range(8):
            xs = None if c == 0 else x if c == 1 else xs * (x * (1.0 / c))
            for d in range(8 - c):
                if c + d:
                    planar[j, FLAT[c, d] - 1] = xs if d == 0 else ys[d] if c == 0 else xs * ys[d]

    for (a, b), at in FLAT.items():
        rs = [radial[j] for j in range(SLOTS)]
        if at:
            rs = [r * planar[j, at - 1] for j, r in enumerate(rs)]
        for c in range(8 - a - b):
            terms = [r if c == 0 else r * zpow[j, c - 1] for j, r in enumerate(rs)]
            while len(terms) > 1:
                terms = [sum(terms[i : i + 2][1:], terms[i]) for i in range(0, len(terms), 2)]
            dens[PLACE[a, b, c]] = terms[0] + swap(terms[0])

    def turned(d):
        return jnp.where(low, d, up(d, 2))

    zero, four = [], []
    for l in range(8):
        s0 = s1 = s2 = None
        for m in range(STARTS[l], STARTS[l + 1]):
            d = dens[m]
            t = turned(d)
            y1, y2 = up(t, 1), up(t, 2)
            ahead[m, 0] = y1
            ahead[m, 1] = y2
            f = d * SPREAD[m]
            a, b, c = f * d, f * y1, f * y2
            s0, s1, s2 = (a, b, c) if s0 is None else (s0 + a, s1 + b, s2 + c)
        spec[l] = s1
        spec[8 + l] = s2
        zero.append(s0)
        four.append(s2)
    for l in range(4):
        pair = jnp.where(row8 < 4, four[2 * l], up(four[2 * l + 1], 4))
        spec[8 + l] = jnp.where(low, spec[8 + l], pair)
        spec[12 + l] = jnp.where(low, spec[12 + l], zero[l])
    for l in range(2):
        spec[16 + l] = jnp.where(low, zero[4 + l], zero[6 + l])
    twice = jnp.where(low, 2.0, 1.0)

    def times(g):
        return 2.0 if g < 12 else twice if g < 16 else 1.0

    def both(tile):
        row = jnp.sum(tile, axis=0, keepdims=True)
        tile = jnp.broadcast_to(row, (8, 128))
        return tile + swap(tile)

    total = jnp.zeros((8, 128), F32)
    for g in range(18):
        v = spec[g]
        total = total + times(g) * v * v
    scale = lax.rsqrt(both(total) + 1e-06)
    for g in range(0, 18, 2):
        two = jnp.concatenate([spec[g] * scale, spec[g + 1] * scale], axis=0)
        dbuf[0, g * 8 : g * 8 + 16, :] = two.astype(BF16)

    sent_desc = [
        remote(dbuf.at[0], dbuf.at[t], des_s.at[t - 1], des_r.at[t - 1], along(delta[t]))
        for t in range(1, 8)
    ]
    for t in (7, 5, 6, 3, 4, 1, 2):
        sent_desc[t - 1].start()

    wlow = lax.broadcasted_iota(jnp.int32, (ROWS, 128), 1) < 64
    sent_grad = [None] * 8
    for slots in ((7, 5, 6, 0), (3, 4, 1, 2)):
        for t in slots:
            if t:
                sent_desc[t - 1].wait_recv()
        for k in range(2):
            xa = dbuf[slots[2 * k]].astype(F32)
            xb = dbuf[slots[2 * k + 1]].astype(F32)
            at = slice(k * 128, (k + 1) * 128)
            vbuf[0:ROWS, at] = jnp.where(wlow, xa, swap(xb)).astype(BF16)
            vbuf[ROWS : 2 * ROWS, at] = jnp.where(wlow, swap(xa), xb).astype(BF16)
        descs[...] = jnp.dot(spread[...], vbuf[...], preferred_element_type=F32).astype(BF16)
        energy = jnp.zeros((8, 256), F32)
        for c in range(points // CHUNK):
            at = slice(c * CHUNK, (c + 1) * CHUNK)
            score = jnp.dot(sparse[at, :], descs[...], preferred_element_type=F32)
            w = wide[at, :]
            square = score * score
            ws = jnp.concatenate([w, w], axis=1) * square
            energy = energy + jnp.sum((ws * square).reshape(CHUNK // 8, 8, 256), axis=0)
            slopes[at, :] = (ws * score).astype(BF16)
        energy = jnp.sum(energy, axis=0, keepdims=True)
        grad = jnp.dot(folded[...], slopes[...], preferred_element_type=F32)
        for k in range(2):
            a, b = slots[2 * k], slots[2 * k + 1]
            at = slice(k * 128, (k + 1) * 128)
            lo, hi = grad[0:ROWS, at], grad[ROWS : 2 * ROWS, at]
            rbuf[a, 0:ROWS, :] = jnp.where(wlow, lo, swap(hi)).astype(BF16)
            rbuf[b, 0:ROWS, :] = jnp.where(wlow, swap(lo), hi).astype(BF16)
            e = jnp.broadcast_to(energy[:, at], (8, 128))
            for t, mine in ((a, e), (b, swap(e))):
                p = pieces(mine, 3)
                tile = jnp.where(row8 == 0, p[0], jnp.where(row8 == 1, p[1], jnp.where(row8 == 2, p[2], 0.0)))
                tile = jnp.concatenate([tile, jnp.zeros((8, 128), F32)], axis=0)
                rbuf[t, ROWS:BACK, :] = tile.astype(BF16)
        for t in slots:
            if t:
                c = remote(rbuf.at[t], gbuf.at[t - 1], gra_s.at[t - 1], gra_r.at[t - 1], along(-delta[t]))
                c.start()
                sent_grad[t] = c

    summed = rbuf[0].astype(F32)
    for t in range(1, 8):
        sent_grad[t].wait_recv()
        summed = summed + gbuf[t - 1].astype(F32)
    last = summed[ROWS : ROWS + 8, :]
    energy = 0.25 * jnp.sum(last, axis=0, keepdims=True)

    dot = jnp.zeros((8, 128), F32)
    for g in range(18):
        dot = dot + summed[g * 8 : g * 8 + 8, :] * spec[g]
    dot = both(dot) * scale
    pull = []
    for g in range(18):
        pull.append(scale * (summed[g * 8 : g * 8 + 8, :] - times(g) * (spec[g] * scale) * dot))
    for l in range(8):
        ha, hb = pull[l], pull[8 + l]
        h0 = pull[12 + l] if l < 4 else swap(pull[12 + l]) if l < 6 else pull[10 + l]
        pair = pull[8 + l // 2]
        h4 = jnp.where((row8 < 4) == (l % 2 == 0), pair, up(pair, 4))
        other = swap(ha)
        k1 = ha
        k2 = jnp.where(low, hb, h4)
        k5 = up(jnp.where(low, up(other, -3), up(other, -1)), 4)
        k6 = up(jnp.where(low, up(hb, -2), 2.0 * h0), 4)
        for m in range(STARTS[l], STARTS[l + 1]):
            y1, y2 = ahead[m, 0], ahead[m, 1]
            v = k1 * y1 + k2 * y2 + up(k5 * y1 + k6 * y2, 4)
            left[m] = (v + swap(v)) * SPREAD[m]

    @pl.loop(0, SLOTS // 3)
    def _(block):
        js = [block * 3 + u for u in range(3)]
        zp = [[None] + [zpow[j, c] for c in range(7)] for j in js]
        q = [[None] * 3 for _ in range(4)]

        def add(old, new):
            return new if old is None else old + new

        def mul(tile, factor):
            return tile if factor is None else tile * factor

        for (a, b), at in FLAT.items():
            level, deriv = [None] * 3, [None] * 3
            for c in range(8 - a - b):
                d = left[PLACE[a, b, c]]
                for u in range(3):
                    level[u] = add(level[u], mul(d, zp[u][c]))
                    if c:
                        deriv[u] = add(deriv[u], mul(d, zp[u][c - 1]))
            for u, j in enumerate(js):
                flat = planar[j, at - 1] if at else None
                q[0][u] = add(q[0][u], mul(level[u], flat))
                if deriv[u] is not None:
                    q[3][u] = add(q[3][u], mul(deriv[u], flat))
                for axis, lower in ((1, (a - 1, b)), (2, (a, b - 1))):
                    if lower in FLAT:
                        flat = planar[j, FLAT[lower] - 1] if FLAT[lower] else None
                        q[axis][u] = add(q[axis][u], mul(level[u], flat))
        for u, j in enumerate(js):
            r = radial[j]
            by_square = jnp.sum(slope_r[j] * q[0][u], axis=0, keepdims=True)
            gx, gy, gz = (jnp.sum(r * q[axis][u], axis=0, keepdims=True) for axis in (1, 2, 3))
            straight = jnp.where(row8 == 0, gx, jnp.where(row8 == 1, gy, jnp.where(row8 == 2, gz, 0.0)))
            pulls[j] = 0.5 * straight + offs[j] * by_square

    centre_grad = pulls[0]
    for j in range(1, SLOTS):
        centre_grad = centre_grad + pulls[j]
    centre_grad = centre_grad + swap(centre_grad)

    def placed(tiles, which, first, last):
        rows = []
        split = [pieces(tile, 2) for tile in tiles]
        for p in range(2):
            for hi in range(first, last):
                rows.append(jnp.concatenate(
                    [jnp.where(w == hi, s[p], 0.0) for w, s in zip(which, split)], axis=1
                ))
        return jnp.concatenate(rows, axis=0).astype(BF16)

    over_lanes = (((1,), (1,)), ((), ()))

    def scatter(first, last):
        n = (last - first) * 8
        total = jnp.zeros((n, 128), F32)
        for q in range(4):
            js = range(q * 3, q * 3 + 3)
            which = [index[j : j + 1, :] // 128 for j in js]
            rows = placed([pulls[j] for j in js], which, first, last)
            got = lax.dot_general(
                rows, ohn[:, q * 384 : (q + 1) * 384], over_lanes, preferred_element_type=F32
            )
            total = total + got[0:n] + got[n : 2 * n]
        return total.reshape(last - first, 8, 128)

    gtab[4 : 4 + faces] = scatter(4, 4 + faces)
    sent_back = []
    for f in range(top):
        c = remote(gtab.at[4 + f], gret.at[f], ret_s.at[f], ret_r.at[f], partner(f))
        c.start()
        sent_back.append(c)

    def home(tiles, which, hots):
        got = lax.dot_general(
            placed(tiles, which, 0, 4), hots, over_lanes, preferred_element_type=F32
        )
        return (got[0:32] + got[32:64]).reshape(4, 8, 128)

    topg[...] = home([gtab[4 + top]], [top_list // 128], oht[...])
    sent_top = []
    for d in range(8):
        who = above(d)
        c = remote(topg.at[who[1] // 2], fintop.at[d], fit_s.at[d], fit_r.at[d], who)
        c.start()
        sent_top.append(c)
    own = scatter(0, 4)
    for c in sent_back:
        c.wait_recv()
    which = [lists_ref[f] // 128 for f in range(top)]
    domg[...] = own + home([gret[f] for f in range(top)], which, ohs[...])
    sent_fin = [None] * 7
    for d in FAR:
        who = peer(d)
        c = remote(domg.at[who[1] // 2], fin.at[d - 1], fin_s.at[d - 1], fin_r.at[d - 1], who)
        c.start()
        sent_fin[d - 1] = c
    mine = domg[sp // 2]
    for d in range(8):
        sent_top[d].wait_recv()
        mine = mine + fintop[d]
    for d in reversed(FAR):
        sent_fin[d - 1].wait_recv()
        mine = mine + fin[d - 1]
    odd = jnp.where(lax.rem(sp, 2) == 1, 1, 0)
    mine = jnp.where(odd == 1, swap(mine), mine)
    out_ref[...] = jnp.where(row8 == 3, energy, centre_grad - mine)
    for c in sent_desc + sent_grad[1:] + sent_back + sent_top + sent_fin:
        c.wait_send()


def split_outputs(out_ref, energy_ref, force_ref):
    energy_ref[...] = out_ref[3:4, 0:64]
    force_ref[...] = out_ref[0:3, 0:64]


def body(positions, neighbours, counts, send_lists, sparse_points, weights):
    faces = send_lists.shape[1]
    points = sparse_points.shape[0]
    vmem = pl.BlockSpec(memory_space=pltpu.VMEM)
    hbm = pl.BlockSpec(memory_space=pl.ANY)
    dma = pltpu.SemaphoreType.DMA
    out = pl.pallas_call(
        lambda *refs: kernel(faces, *refs),
        out_shape=jax.ShapeDtypeStruct((8, 128), F32),
        in_specs=[hbm] * 6,
        out_specs=vmem,
        scratch_shapes=[
            pltpu.VMEM(positions.shape, F32),
            pltpu.VMEM(neighbours.shape, jnp.int32),
            pltpu.VMEM((1, counts.shape[0]), jnp.int32),
            pltpu.VMEM((faces, 1, 128), jnp.int32),
            pltpu.VMEM((points // 128, 128), F32),
            pltpu.VMEM((8, 8, 128), F32),
            pltpu.VMEM((8, 8, 128), F32),
            pltpu.VMEM((faces - 1, 8, 128), F32),
            pltpu.VMEM((4 + faces, 8, 128), F32),
            pltpu.VMEM((24, 128), jnp.int32),
            pltpu.VMEM((16, 128), jnp.int32),
            pltpu.VMEM((128, (faces - 1) * 128), BF16),
            pltpu.VMEM((128, 128), BF16),
            pltpu.VMEM((128, SLOTS * 128), BF16),
            pltpu.VMEM((SLOTS, 8, 128), F32),
            pltpu.VMEM((SLOTS, 8, 128), F32),
            pltpu.VMEM((SLOTS, 7, 8, 128), F32),
            pltpu.VMEM((SLOTS, 35, 8, 128), F32),
            pltpu.VMEM((120, 2, 8, 128), F32),
            pltpu.VMEM((SLOTS, 8, 128), F32),
            pltpu.VMEM((SLOTS, 8, 128), F32),
            pltpu.VMEM((120, 8, 128), F32),
            pltpu.VMEM((18, 8, 128), F32),
            pltpu.VMEM((8, ROWS, 128), BF16),
            pltpu.VMEM((8, BACK, 128), BF16),
            pltpu.VMEM((7, BACK, 128), BF16),
            pltpu.VMEM((2 * ROWS, 256), BF16),
            pltpu.VMEM((512, 256), BF16),
            pltpu.VMEM((points, 256), BF16),
            pltpu.VMEM((points, 512), BF16),
            pltpu.VMEM((2 * ROWS, 512), BF16),
            pltpu.VMEM((512, 2 * ROWS), BF16),
            pltpu.VMEM((2 * ROWS, points), BF16),
            pltpu.VMEM((points, 128), F32),
            pltpu.VMEM((120, 8, 128), F32),
            pltpu.VMEM((SLOTS, 8, 128), F32),
            pltpu.VMEM((4 + faces, 8, 128), F32),
            pltpu.VMEM((faces - 1, 8, 128), F32),
            pltpu.VMEM((4, 8, 128), F32),
            pltpu.VMEM((7, 8, 128), F32),
            pltpu.VMEM((4, 8, 128), F32),
            pltpu.VMEM((8, 8, 128), F32),
            dma((6,)),
            dma((7,)), dma((7,)),
            dma((8,)), dma((8,)),
            dma((faces - 1,)), dma((faces - 1,)),
            dma((7,)), dma((7,)),
            dma((7,)), dma((7,)),
            dma((faces - 1,)), dma((faces - 1,)),
            dma((7,)), dma((7,)),
            dma((8,)), dma((8,)),
        ],
        compiler_params=pltpu.CompilerParams(
            collective_id=0, has_side_effects=True, vmem_limit_bytes=60 * 2**20
        ),
        name="gap_forces",
    )(
        positions,
        neighbours,
        counts.reshape(1, -1),
        send_lists.transpose(1, 0, 2),
        sparse_points,
        weights.reshape(-1, 128),
    )
    energies, forces = pl.pallas_call(
        split_outputs,
        out_shape=(jax.ShapeDtypeStruct((1, 64), F32), jax.ShapeDtypeStruct((3, 64), F32)),
        in_specs=[vmem],
        out_specs=(vmem, vmem),
        compiler_params=pltpu.CompilerParams(vmem_limit_bytes=60 * 2**20),
        name="split_outputs",
    )(out)
    return energies.reshape(-1), forces


def solution(mesh):
    in_specs = (
        P(None, ("dom", "sp")),
        P(None, ("dom", "sp")),
        P(("dom", "sp")),
        P("dom", None, None),
        P("sp", None),
        P("sp"),
    )
    out_specs = (P(("dom", "sp")), P(None, ("dom", "sp")))
    return jax.shard_map(body, mesh=mesh, in_specs=in_specs, out_specs=out_specs, check_vma=False)
```

```python
import math

import jax
import jax.numpy as jnp
from jax import lax
from jax.experimental import pallas as pl
from jax.experimental.pallas import tpu as pltpu
from jax.sharding import PartitionSpec as P

F32, BF16 = jnp.float32, jnp.bfloat16
MESH = pl.DeviceIdType.MESH
SLOTS = 12
ROWS = 144
BACK = 160
CHUNK = 512
FAR = (7, 1, 6, 2, 5, 3, 4)


def powers():
    found, starts = [], []
    for degree in range(8):
        starts.append(len(found))
        for a in range(degree, -1, -1):
            for b in range(degree - a, -1, -1):
                found.append((a, b, degree - a - b))
    return found, starts + [len(found)]


POWERS, STARTS = powers()
PLACE = {p: i for i, p in enumerate(POWERS)}
SPREAD = [
    float(math.factorial(sum(p)) * math.prod(math.factorial(e) for e in p)) for p in POWERS
]


FLAT = {(a, b): i for i, (a, b) in enumerate((a, b) for a in range(8) for b in range(8 - a))}


def packed_place(e):
    n, n2, l = e // 64, (e // 8) & 7, e & 7
    r = (n2 - n) & 7
    first = jnp.where(r > 4, n2, n)
    r = jnp.where(r > 4, 8 - r, r)
    row = jnp.where(r == 4, (first & 3) + 4 * (l & 1), first)
    diagonal = jnp.where(l < 4, 12 + l, 16 + (l & 1))
    group = jnp.where(
        r == 0, diagonal, jnp.where(r == 4, 8 + l // 2, jnp.where(r == 2, 8 + l, l))
    )
    half = jnp.where(r == 0, jnp.where((l == 4) | (l == 5), 0, 1), jnp.where(r > 2, 1, 0))
    return half * ROWS + group * 8 + row


def up(x, k):
    return x if k % 8 == 0 else pltpu.roll(x, (8 - k) % 8, 0)


def swap(x):
    return pltpu.roll(x, 64, 1)


def pieces(x, count):
    out = []
    for _ in range(count):
        p = x.astype(BF16).astype(F32)
        out.append(p)
        x = x - p
    return out


def one_hot(row):
    return jnp.where(lax.broadcasted_iota(jnp.int32, (128, 128), 0) == row, 1.0, 0.0).astype(BF16)


def kernel(
    faces, pos_hbm, near_hbm, count_hbm, lists_hbm, sparse_hbm, weight_hbm,
    out_ref,
    pos_ref, near_ref, count_ref, lists_ref, weight_ref,
    posbuf, topbuf, ghost_out, tab, pack, index, ohs, oht, ohn, looked, offs, zpow, planar, ahead, radial, slope_r, dens,
    spec, dbuf, rbuf, gbuf, vbuf, descs, slopes, sparse, fold, spread, folded, wide, left, pulls,
    gtab, gret, domg, fin, topg, fintop,
    local_sem, pos_s, pos_r, top_s, top_r, gho_s, gho_r, des_s, des_r, gra_s, gra_r, ret_s, ret_r, fin_s, fin_r, fit_s, fit_r,
):
    dom, sp = lax.axis_index("dom"), lax.axis_index("sp")
    n_dom, n_sp = lax.axis_size("dom"), lax.axis_size("sp")
    below = n_dom // 2
    ring = 2 * n_sp
    z = (dom // below) * n_sp + sp
    rest = lax.rem(dom, below)
    side = 1 - 2 * lax.rem(dom, 2)

    def along(delta):
        there = lax.rem(z + delta + ring, ring)
        return (rest + (there // n_sp) * below, lax.rem(there, n_sp))

    def peer(delta):
        return (dom, lax.rem(sp + delta, n_sp))

    def partner(face):
        bit = lax.rem(dom // 2**face, 2)
        return (dom + (1 - 2 * bit) * 2**face, sp)

    delta = [0, 1, -1, 2, -2, 3, -3, 4 * side]
    lane = lax.broadcasted_iota(jnp.int32, (8, 128), 1)
    low = lane < 64
    row8 = lax.broadcasted_iota(jnp.int32, (8, 128), 0)

    def above(d):
        return (lax.rem(dom + below, n_dom), lax.rem(sp + d, n_sp))

    barrier = pltpu.get_barrier_semaphore()
    greeted = [above(d) for d in (0, 1, 7, 2, 6, 3, 5, 4)] + [peer(d) for d in FAR]
    greeted += [partner(f) for f in reversed(range(faces - 1))]
    for who in greeted:
        pl.semaphore_signal(barrier, inc=1, device_id=who, device_id_type=MESH)

    pairs = [
        (pos_hbm, pos_ref), (lists_hbm, lists_ref), (near_hbm, near_ref), (count_hbm, count_ref),
        (weight_hbm, weight_ref), (sparse_hbm, sparse),
    ]
    loads = [pltpu.make_async_copy(a, b, local_sem.at[i]) for i, (a, b) in enumerate(pairs)]
    for load in loads:
        load.start()

    loads[0].wait()
    loads[1].wait()
    top = faces - 1
    for buf in (posbuf, topbuf, tab, gret, fin, fintop):
        buf[:, 4:8, :] = jnp.zeros((buf.shape[0], 4, 128), F32)
    posbuf[sp] = jnp.zeros((8, 128), F32)
    posbuf[sp, 0:3, 0:64] = pos_ref[...]
    here = posbuf[sp]
    here = here + swap(here)
    here = jnp.where(row8 == 3, lists_ref[top].astype(F32), here)
    posbuf[sp] = here
    for load in loads[2:5]:
        load.wait()
    for f in range(top):
        ohs[:, f * 128 : (f + 1) * 128] = one_hot(lists_ref[f] & 127)
    pack[...] = jnp.zeros((24, 128), jnp.int32)
    pack[:, 0:64] = near_ref[...]
    index[0:8] = jnp.where(low, pack[0:8], swap(pack[8:16]))
    last = pack[16:24]
    last = jnp.where(low, last, swap(pltpu.roll(last, 4, 0)))
    index[8:16] = jnp.where(row8 < 4, last, 0)
    for j in range(SLOTS):
        ohn[:, j * 128 : (j + 1) * 128] = one_hot(index[j : j + 1, :] & 127)
    pl.semaphore_wait(barrier, len(greeted))

    def remote(src, dst, s, r, who):
        return pltpu.make_async_remote_copy(
            src_ref=src, dst_ref=dst, send_sem=s, recv_sem=r, device_id=who, device_id_type=MESH
        )

    sent_pos = [
        remote(posbuf.at[sp, 0:4], posbuf.at[sp, 0:4], pos_s.at[d - 1], pos_r.at[d - 1], peer(d))
        for d in range(1, 8)
    ]
    for d in FAR:
        sent_pos[d - 1].start()

    sent_top = [
        remote(posbuf.at[sp, 0:4], topbuf.at[sp, 0:4], top_s.at[d], top_r.at[d], above(d)) for d in range(8)
    ]
    for d in (0, 1, 7, 2, 6, 3, 5, 4):
        sent_top[d].start()

    place = packed_place(lax.broadcasted_iota(jnp.int32, (8, 512), 1))[0:1]
    numbers = lax.broadcasted_iota(jnp.int32, (2 * ROWS, 512), 0)
    fold[...] = jnp.where(numbers == place, 1.0, 0.0).astype(BF16)
    place = packed_place(lax.broadcasted_iota(jnp.int32, (512, 128), 0))
    for k in range(0, 2 * ROWS, 128):
        n = min(128, 2 * ROWS - k)
        numbers = k + lax.broadcasted_iota(jnp.int32, (512, 128), 1)
        spread[:, k : k + n] = jnp.where(numbers == place, 1.0, 0.0).astype(BF16)[:, 0:n]
    for load in loads[5:]:
        load.wait()
    points = sparse.shape[0]

    @pl.loop(0, points // 128)
    def _(c):
        column = jnp.broadcast_to(4.0 * weight_ref[pl.ds(c, 1), :], (128, 128)).T
        wide[pl.ds(pl.multiple_of(c * 128, 128), 128), :] = column

    @pl.loop(0, points // CHUNK)
    def _(c):
        at = pl.ds(pl.multiple_of(c * CHUNK, CHUNK), CHUNK)
        folded[:, at] = lax.dot_general(
            fold[...], sparse[at, :], (((1,), (1,)), ((), ())), preferred_element_type=F32
        ).astype(BF16)

    for c in sent_pos:
        c.wait()

    for hi in range(4):
        tab[hi] = jnp.where(low, posbuf[2 * hi], posbuf[2 * hi + 1])

    def gather(tiles, hots):
        parts = jnp.concatenate(pieces(tiles.reshape(32, 128), 3), axis=0).astype(BF16)
        out = jnp.dot(parts, hots, preferred_element_type=F32)
        return out[0:32] + out[32:64] + out[64:96]

    def chosen(out, which):
        tile = jnp.zeros((8, 128), F32)
        for hi in range(4):
            tile = jnp.where(which == hi, out[hi * 8 : hi * 8 + 8], tile)
        return tile

    out = gather(tab[0:4], ohs[...])
    sent_ghost = []
    for f in range(top):
        ghost_out[f] = chosen(out[:, f * 128 : (f + 1) * 128], lists_ref[f] // 128)
        c = remote(ghost_out.at[f, 0:4], tab.at[4 + f, 0:4], gho_s.at[f], gho_r.at[f], partner(f))
        c.start()
        sent_ghost.append(c)

    def look(first, last, into):
        n = (last - first) * 8
        values = tab[first:last].reshape(n, 128)
        split = jnp.concatenate(pieces(values, 3), axis=0).astype(BF16)
        for q in range(4):
            at = slice(q * 384, (q + 1) * 384)
            got = jnp.dot(split, ohn[:, at], preferred_element_type=F32)
            got = got[0:n] + got[n : 2 * n] + got[2 * n : 3 * n]
            for u in range(3):
                j = q * 3 + u
                which = index[j : j + 1, :] // 128
                tile = looked[j] if into else jnp.zeros((8, 128), F32)
                for hi in range(first, last):
                    part = got[(hi - first) * 8 : (hi - first) * 8 + 8, u * 128 : (u + 1) * 128]
                    tile = jnp.where(which == hi, part, tile)
                looked[j] = tile

    look(0, 4, False)
    for c in sent_top:
        c.wait()
    far = jnp.concatenate(
        [jnp.where(low, topbuf[2 * hi], topbuf[2 * hi + 1]) for hi in range(4)], axis=0
    )
    top_list = topbuf[sp, 3:4, :].astype(jnp.int32)
    oht[...] = one_hot(top_list & 127)
    tab[4 + top] = chosen(gather(far, oht[...]), top_list // 128)

    for c in sent_ghost:
        c.wait()
    look(4, 4 + faces, True)

    pack[0:8] = jnp.zeros((8, 128), jnp.int32)
    pack[0:1, 0:64] = count_ref[...]
    counts = pack[0:8]
    counts = jnp.broadcast_to((counts + swap(counts))[0:1], (8, 128))
    upper = lane // 64
    centre = 0.05 + 0.15 * row8.astype(F32)
    for j in range(SLOTS):
        off = 0.5 * (looked[j] - here)
        offs[j] = off
        x, y, zz = (jnp.broadcast_to(off[axis : axis + 1], (8, 128)) for axis in range(3))
        squared = x * x + y * y + zz * zz
        slot = j + 8 * upper if j < 8 else 8 + j + 4 * upper
        live = jnp.where(slot < counts, 1.0, 0.0)
        inside = 1.0 - squared * (1.0 / 3.5)
        gap = squared - centre
        bell = jnp.exp(-30.0 * gap * gap) * live
        r = bell * (inside * inside)
        radial[j] = r
        slope_r[j] = r * (-60.0 * gap) + bell * ((-2.0 / 3.5) * inside)
        power = {0: None}
        for c in range(1, 8):
            power[c] = zz if c == 1 else power[c - 1] * (zz * (1.0 / c))
            zpow[j, c - 1] = power[c]
        ys = [None]
        for c in range(1, 8):
            ys.append(y if c == 1 else ys[c - 1] * (y * (1.0 / c)))
        xs = None
        for c in range(8):
            xs = None if c == 0 else x if c == 1 else xs * (x * (1.0 / c))
            for d in range(8 - c):
                if c + d:
                    planar[j, FLAT[c, d] - 1] = xs if d == 0 else ys[d] if c == 0 else xs * ys[d]

    for (a, b), at in FLAT.items():
        rs = [radial[j] for j in range(SLOTS)]
        if at:
            rs = [r * planar[j, at - 1] for j, r in enumerate(rs)]
        for c in range(8 - a - b):
            terms = [r if c == 0 else r * zpow[j, c - 1] for j, r in enumerate(rs)]
            while len(terms) > 1:
                terms = [sum(terms[i : i + 2][1:], terms[i]) for i in range(0, len(terms), 2)]
            dens[PLACE[a, b, c]] = terms[0] + swap(terms[0])

    def turned(d):
        return jnp.where(low, d, up(d, 2))

    zero, four = [], []
    for l in range(8):
        s0 = s1 = s2 = None
        for m in range(STARTS[l], STARTS[l + 1]):
            d = dens[m]
            t = turned(d)
            y1, y2 = up(t, 1), up(t, 2)
            ahead[m, 0] = y1
            ahead[m, 1] = y2
            f = d * SPREAD[m]
            a, b, c = f * d, f * y1, f * y2
            s0, s1, s2 = (a, b, c) if s0 is None else (s0 + a, s1 + b, s2 + c)
        spec[l] = s1
        spec[8 + l] = s2
        zero.append(s0)
        four.append(s2)
    for l in range(4):
        pair = jnp.where(row8 < 4, four[2 * l], up(four[2 * l + 1], 4))
        spec[8 + l] = jnp.where(low, spec[8 + l], pair)
        spec[12 + l] = jnp.where(low, spec[12 + l], zero[l])
    for l in range(2):
        spec[16 + l] = jnp.where(low, zero[4 + l], zero[6 + l])
    twice = jnp.where(low, 2.0, 1.0)

    def times(g):
        return 2.0 if g < 12 else twice if g < 16 else 1.0

    def both(tile):
        row = jnp.sum(tile, axis=0, keepdims=True)
        tile = jnp.broadcast_to(row, (8, 128))
        return tile + swap(tile)

    total = jnp.zeros((8, 128), F32)
    for g in range(18):
        v = spec[g]
        total = total + times(g) * v * v
    scale = lax.rsqrt(both(total) + 1e-06)
    for g in range(0, 18, 2):
        two = jnp.concatenate([spec[g] * scale, spec[g + 1] * scale], axis=0)
        dbuf[0, g * 8 : g * 8 + 16, :] = two.astype(BF16)

    sent_desc = [
        remote(dbuf.at[0], dbuf.at[t], des_s.at[t - 1], des_r.at[t - 1], along(delta[t]))
        for t in range(1, 8)
    ]
    for t in (7, 5, 6, 3, 4, 1, 2):
        sent_desc[t - 1].start()

    wlow = lax.broadcasted_iota(jnp.int32, (ROWS, 128), 1) < 64
    sent_grad = [None] * 8
    for slots in ((7, 5, 6, 3), (4, 1, 2, 0)):
        for t in slots:
            if t:
                sent_desc[t - 1].wait_recv()
        for k in range(2):
            xa = dbuf[slots[2 * k]].astype(F32)
            xb = dbuf[slots[2 * k + 1]].astype(F32)
            at = slice(k * 128, (k + 1) * 128)
            vbuf[0:ROWS, at] = jnp.where(wlow, xa, swap(xb)).astype(BF16)
            vbuf[ROWS : 2 * ROWS, at] = jnp.where(wlow, swap(xa), xb).astype(BF16)
        descs[...] = jnp.dot(spread[...], vbuf[...], preferred_element_type=F32).astype(BF16)
        energy = jnp.zeros((8, 256), F32)
        for c in range(points // CHUNK):
            at = slice(c * CHUNK, (c + 1) * CHUNK)
            score = jnp.dot(sparse[at, :], descs[...], preferred_element_type=F32)
            w = wide[at, :]
            square = score * score
            ws = jnp.concatenate([w, w], axis=1) * square
            energy = energy + jnp.sum((ws * square).reshape(CHUNK // 8, 8, 256), axis=0)
            slopes[at, :] = (ws * score).astype(BF16)
        energy = jnp.sum(energy, axis=0, keepdims=True)
        grad = jnp.dot(folded[...], slopes[...], preferred_element_type=F32)
        for k in range(2):
            a, b = slots[2 * k], slots[2 * k + 1]
            at = slice(k * 128, (k + 1) * 128)
            lo, hi = grad[0:ROWS, at], grad[ROWS : 2 * ROWS, at]
            rbuf[a, 0:ROWS, :] = jnp.where(wlow, lo, swap(hi)).astype(BF16)
            rbuf[b, 0:ROWS, :] = jnp.where(wlow, swap(lo), hi).astype(BF16)
            e = jnp.broadcast_to(energy[:, at], (8, 128))
            for t, mine in ((a, e), (b, swap(e))):
                p = pieces(mine, 3)
                tile = jnp.where(row8 == 0, p[0], jnp.where(row8 == 1, p[1], jnp.where(row8 == 2, p[2], 0.0)))
                tile = jnp.concatenate([tile, jnp.zeros((8, 128), F32)], axis=0)
                rbuf[t, ROWS:BACK, :] = tile.astype(BF16)
        for t in slots:
            if t:
                c = remote(rbuf.at[t], gbuf.at[t - 1], gra_s.at[t - 1], gra_r.at[t - 1], along(-delta[t]))
                c.start()
                sent_grad[t] = c

    summed = rbuf[0].astype(F32)
    for t in range(1, 8):
        sent_grad[t].wait_recv()
        summed = summed + gbuf[t - 1].astype(F32)
    last = summed[ROWS : ROWS + 8, :]
    energy = 0.25 * jnp.sum(last, axis=0, keepdims=True)

    dot = jnp.zeros((8, 128), F32)
    for g in range(18):
        dot = dot + summed[g * 8 : g * 8 + 8, :] * spec[g]
    dot = both(dot) * scale
    pull = []
    for g in range(18):
        pull.append(scale * (summed[g * 8 : g * 8 + 8, :] - times(g) * (spec[g] * scale) * dot))
    for l in range(8):
        ha, hb = pull[l], pull[8 + l]
        h0 = pull[12 + l] if l < 4 else swap(pull[12 + l]) if l < 6 else pull[10 + l]
        pair = pull[8 + l // 2]
        h4 = jnp.where((row8 < 4) == (l % 2 == 0), pair, up(pair, 4))
        other = swap(ha)
        k1 = ha
        k2 = jnp.where(low, hb, h4)
        k5 = up(jnp.where(low, up(other, -3), up(other, -1)), 4)
        k6 = up(jnp.where(low, up(hb, -2), 2.0 * h0), 4)
        for m in range(STARTS[l], STARTS[l + 1]):
            y1, y2 = ahead[m, 0], ahead[m, 1]
            v = k1 * y1 + k2 * y2 + up(k5 * y1 + k6 * y2, 4)
            left[m] = (v + swap(v)) * SPREAD[m]

    @pl.loop(0, SLOTS // 3)
    def _(block):
        js = [block * 3 + u for u in range(3)]
        zp = [[None] + [zpow[j, c] for c in range(7)] for j in js]
        q = [[None] * 3 for _ in range(4)]

        def add(old, new):
            return new if old is None else old + new

        def mul(tile, factor):
            return tile if factor is None else tile * factor

        for (a, b), at in FLAT.items():
            level, deriv = [None] * 3, [None] * 3
            for c in range(8 - a - b):
                d = left[PLACE[a, b, c]]
                for u in range(3):
                    level[u] = add(level[u], mul(d, zp[u][c]))
                    if c:
                        deriv[u] = add(deriv[u], mul(d, zp[u][c - 1]))
            for u, j in enumerate(js):
                flat = planar[j, at - 1] if at else None
                q[0][u] = add(q[0][u], mul(level[u], flat))
                if deriv[u] is not None:
                    q[3][u] = add(q[3][u], mul(deriv[u], flat))
                for axis, lower in ((1, (a - 1, b)), (2, (a, b - 1))):
                    if lower in FLAT:
                        flat = planar[j, FLAT[lower] - 1] if FLAT[lower] else None
                        q[axis][u] = add(q[axis][u], mul(level[u], flat))
        for u, j in enumerate(js):
            r = radial[j]
            by_square = jnp.sum(slope_r[j] * q[0][u], axis=0, keepdims=True)
            gx, gy, gz = (jnp.sum(r * q[axis][u], axis=0, keepdims=True) for axis in (1, 2, 3))
            straight = jnp.where(row8 == 0, gx, jnp.where(row8 == 1, gy, jnp.where(row8 == 2, gz, 0.0)))
            pulls[j] = 0.5 * straight + offs[j] * by_square

    centre_grad = pulls[0]
    for j in range(1, SLOTS):
        centre_grad = centre_grad + pulls[j]
    centre_grad = centre_grad + swap(centre_grad)

    def placed(tiles, which, first, last):
        rows = []
        split = [pieces(tile, 2) for tile in tiles]
        for p in range(2):
            for hi in range(first, last):
                rows.append(jnp.concatenate(
                    [jnp.where(w == hi, s[p], 0.0) for w, s in zip(which, split)], axis=1
                ))
        return jnp.concatenate(rows, axis=0).astype(BF16)

    over_lanes = (((1,), (1,)), ((), ()))

    def scatter(first, last):
        n = (last - first) * 8
        total = jnp.zeros((n, 128), F32)
        for q in range(4):
            js = range(q * 3, q * 3 + 3)
            which = [index[j : j + 1, :] // 128 for j in js]
            rows = placed([pulls[j] for j in js], which, first, last)
            got = lax.dot_general(
                rows, ohn[:, q * 384 : (q + 1) * 384], over_lanes, preferred_element_type=F32
            )
            total = total + got[0:n] + got[n : 2 * n]
        return total.reshape(last - first, 8, 128)

    gtab[4 : 4 + faces] = scatter(4, 4 + faces)
    sent_back = []
    for f in range(top):
        c = remote(gtab.at[4 + f, 0:4], gret.at[f, 0:4], ret_s.at[f], ret_r.at[f], partner(f))
        c.start()
        sent_back.append(c)

    def home(tiles, which, hots):
        got = lax.dot_general(
            placed(tiles, which, 0, 4), hots, over_lanes, preferred_element_type=F32
        )
        return (got[0:32] + got[32:64]).reshape(4, 8, 128)

    topg[...] = home([gtab[4 + top]], [top_list // 128], oht[...])
    sent_top = []
    for d in range(8):
        who = above(d)
        c = remote(topg.at[who[1] // 2, 0:4], fintop.at[d, 0:4], fit_s.at[d], fit_r.at[d], who)
        c.start()
        sent_top.append(c)
    own = scatter(0, 4)
    for c in sent_back:
        c.wait_recv()
    which = [lists_ref[f] // 128 for f in range(top)]
    domg[...] = own + home([gret[f] for f in range(top)], which, ohs[...])
    sent_fin = [None] * 7
    for d in FAR:
        who = peer(d)
        c = remote(domg.at[who[1] // 2, 0:4], fin.at[d - 1, 0:4], fin_s.at[d - 1], fin_r.at[d - 1], who)
        c.start()
        sent_fin[d - 1] = c
    mine = domg[sp // 2]
    for d in range(8):
        sent_top[d].wait_recv()
        mine = mine + fintop[d]
    for d in reversed(FAR):
        sent_fin[d - 1].wait_recv()
        mine = mine + fin[d - 1]
    odd = jnp.where(lax.rem(sp, 2) == 1, 1, 0)
    mine = jnp.where(odd == 1, swap(mine), mine)
    out_ref[...] = jnp.where(row8 == 3, energy, centre_grad - mine)
    for c in sent_desc + sent_grad[1:] + sent_back + sent_top + sent_fin:
        c.wait_send()


def split_outputs(out_ref, energy_ref, force_ref):
    energy_ref[...] = out_ref[3:4, 0:64]
    force_ref[...] = out_ref[0:3, 0:64]


def body(positions, neighbours, counts, send_lists, sparse_points, weights):
    faces = send_lists.shape[1]
    points = sparse_points.shape[0]
    vmem = pl.BlockSpec(memory_space=pltpu.VMEM)
    hbm = pl.BlockSpec(memory_space=pl.ANY)
    dma = pltpu.SemaphoreType.DMA
    out = pl.pallas_call(
        lambda *refs: kernel(faces, *refs),
        out_shape=jax.ShapeDtypeStruct((8, 128), F32),
        in_specs=[hbm] * 6,
        out_specs=vmem,
        scratch_shapes=[
            pltpu.VMEM(positions.shape, F32),
            pltpu.VMEM(neighbours.shape, jnp.int32),
            pltpu.VMEM((1, counts.shape[0]), jnp.int32),
            pltpu.VMEM((faces, 1, 128), jnp.int32),
            pltpu.VMEM((points // 128, 128), F32),
            pltpu.VMEM((8, 8, 128), F32),
            pltpu.VMEM((8, 8, 128), F32),
            pltpu.VMEM((faces - 1, 8, 128), F32),
            pltpu.VMEM((4 + faces, 8, 128), F32),
            pltpu.VMEM((24, 128), jnp.int32),
            pltpu.VMEM((16, 128), jnp.int32),
            pltpu.VMEM((128, (faces - 1) * 128), BF16),
            pltpu.VMEM((128, 128), BF16),
            pltpu.VMEM((128, SLOTS * 128), BF16),
            pltpu.VMEM((SLOTS, 8, 128), F32),
            pltpu.VMEM((SLOTS, 8, 128), F32),
            pltpu.VMEM((SLOTS, 7, 8, 128), F32),
            pltpu.VMEM((SLOTS, 35, 8, 128), F32),
            pltpu.VMEM((120, 2, 8, 128), F32),
            pltpu.VMEM((SLOTS, 8, 128), F32),
            pltpu.VMEM((SLOTS, 8, 128), F32),
            pltpu.VMEM((120, 8, 128), F32),
            pltpu.VMEM((18, 8, 128), F32),
            pltpu.VMEM((8, ROWS, 128), BF16),
            pltpu.VMEM((8, BACK, 128), BF16),
            pltpu.VMEM((7, BACK, 128), BF16),
            pltpu.VMEM((2 * ROWS, 256), BF16),
            pltpu.VMEM((512, 256), BF16),
            pltpu.VMEM((points, 256), BF16),
            pltpu.VMEM((points, 512), BF16),
            pltpu.VMEM((2 * ROWS, 512), BF16),
            pltpu.VMEM((512, 2 * ROWS), BF16),
            pltpu.VMEM((2 * ROWS, points), BF16),
            pltpu.VMEM((points, 128), F32),
            pltpu.VMEM((120, 8, 128), F32),
            pltpu.VMEM((SLOTS, 8, 128), F32),
            pltpu.VMEM((4 + faces, 8, 128), F32),
            pltpu.VMEM((faces - 1, 8, 128), F32),
            pltpu.VMEM((4, 8, 128), F32),
            pltpu.VMEM((7, 8, 128), F32),
            pltpu.VMEM((4, 8, 128), F32),
            pltpu.VMEM((8, 8, 128), F32),
            dma((6,)),
            dma((7,)), dma((7,)),
            dma((8,)), dma((8,)),
            dma((faces - 1,)), dma((faces - 1,)),
            dma((7,)), dma((7,)),
            dma((7,)), dma((7,)),
            dma((faces - 1,)), dma((faces - 1,)),
            dma((7,)), dma((7,)),
            dma((8,)), dma((8,)),
        ],
        compiler_params=pltpu.CompilerParams(
            collective_id=0, has_side_effects=True, vmem_limit_bytes=60 * 2**20
        ),
        name="gap_forces",
    )(
        positions,
        neighbours,
        counts.reshape(1, -1),
        send_lists.transpose(1, 0, 2),
        sparse_points,
        weights.reshape(-1, 128),
    )
    energies, forces = pl.pallas_call(
        split_outputs,
        out_shape=(jax.ShapeDtypeStruct((1, 64), F32), jax.ShapeDtypeStruct((3, 64), F32)),
        in_specs=[vmem],
        out_specs=(vmem, vmem),
        compiler_params=pltpu.CompilerParams(vmem_limit_bytes=60 * 2**20),
        name="split_outputs",
    )(out)
    return energies.reshape(-1), forces


def solution(mesh):
    in_specs = (
        P(None, ("dom", "sp")),
        P(None, ("dom", "sp")),
        P(("dom", "sp")),
        P("dom", None, None),
        P("sp", None),
        P("sp"),
    )
    out_specs = (P(("dom", "sp")), P(None, ("dom", "sp")))
    return jax.shard_map(body, mesh=mesh, in_specs=in_specs, out_specs=out_specs, check_vma=False)
```

```python
import math

import jax
import jax.numpy as jnp
from jax import lax
from jax.experimental import pallas as pl
from jax.experimental.pallas import tpu as pltpu
from jax.sharding import PartitionSpec as P

F32, BF16 = jnp.float32, jnp.bfloat16
MESH = pl.DeviceIdType.MESH
SLOTS = 12
ROWS = 144
BACK = 160
CHUNK = 512
DIRECT = (7, 1, 6, 2, 5, 3)
FAR = (7, 1, 6, 2, 5, 3, 4)


def powers():
    found, starts = [], []
    for degree in range(8):
        starts.append(len(found))
        for a in range(degree, -1, -1):
            for b in range(degree - a, -1, -1):
                found.append((a, b, degree - a - b))
    return found, starts + [len(found)]


POWERS, STARTS = powers()
PLACE = {p: i for i, p in enumerate(POWERS)}
SPREAD = [
    float(math.factorial(sum(p)) * math.prod(math.factorial(e) for e in p)) for p in POWERS
]


FLAT = {(a, b): i for i, (a, b) in enumerate((a, b) for a in range(8) for b in range(8 - a))}


def packed_place(e):
    n, n2, l = e // 64, (e // 8) & 7, e & 7
    r = (n2 - n) & 7
    first = jnp.where(r > 4, n2, n)
    r = jnp.where(r > 4, 8 - r, r)
    row = jnp.where(r == 4, (first & 3) + 4 * (l & 1), first)
    diagonal = jnp.where(l < 4, 12 + l, 16 + (l & 1))
    group = jnp.where(
        r == 0, diagonal, jnp.where(r == 4, 8 + l // 2, jnp.where(r == 2, 8 + l, l))
    )
    half = jnp.where(r == 0, jnp.where((l == 4) | (l == 5), 0, 1), jnp.where(r > 2, 1, 0))
    return half * ROWS + group * 8 + row


def up(x, k):
    return x if k % 8 == 0 else pltpu.roll(x, (8 - k) % 8, 0)


def swap(x):
    return pltpu.roll(x, 64, 1)


def pieces(x, count):
    out = []
    for _ in range(count):
        p = x.astype(BF16).astype(F32)
        out.append(p)
        x = x - p
    return out


def one_hot(row):
    return jnp.where(lax.broadcasted_iota(jnp.int32, (128, 128), 0) == row, 1.0, 0.0).astype(BF16)


def kernel(
    faces, pos_hbm, near_hbm, count_hbm, lists_hbm, sparse_hbm, weight_hbm,
    out_ref,
    pos_ref, near_ref, count_ref, lists_ref, weight_ref,
    posbuf, topbuf, ghost_out, tab, pack, index, ohs, oht, ohp, ohn, looked, offs, zpow, planar, ahead, radial, slope_r, dens,
    spec, dbuf, rbuf, gbuf, vbuf, descs, slopes, sparse, fold, spread, folded, wide, left, pulls,
    gtab, gret, domg, fin, topg, fintop, domown, faceg, farin, total_ref,
    local_sem, pos_s, pos_r, top_s, top_r, gho_s, gho_r, des_s, des_r, gra_s, gra_r, ret_s, ret_r, fin_s, fin_r, fit_s, fit_r, far_s, far_r,
):
    dom, sp = lax.axis_index("dom"), lax.axis_index("sp")
    n_dom, n_sp = lax.axis_size("dom"), lax.axis_size("sp")
    below = n_dom // 2
    ring = 2 * n_sp
    z = (dom // below) * n_sp + sp
    rest = lax.rem(dom, below)
    side = 1 - 2 * lax.rem(dom, 2)

    def along(delta):
        there = lax.rem(z + delta + ring, ring)
        return (rest + (there // n_sp) * below, lax.rem(there, n_sp))

    def peer(delta):
        return (dom, lax.rem(sp + delta, n_sp))

    def partner(face):
        bit = lax.rem(dom // 2**face, 2)
        return (dom + (1 - 2 * bit) * 2**face, sp)

    delta = [0, 1, -1, 2, -2, 3, -3, 4 * side]
    lane = lax.broadcasted_iota(jnp.int32, (8, 128), 1)
    low = lane < 64
    row8 = lax.broadcasted_iota(jnp.int32, (8, 128), 0)

    def sends_far(d):
        return sp + d < n_sp if d >= 5 else sp + d >= n_sp

    def gets_far(d):
        return sp >= d if d >= 5 else sp < d

    def above(d):
        return (lax.rem(dom + below, n_dom), lax.rem(sp + d, n_sp))

    barrier = pltpu.get_barrier_semaphore()
    greeted = [above(d) for d in (0, 1, 7, 2, 6, 3, 5, 4)] + [peer(d) for d in FAR]
    greeted += [partner(f) for f in reversed(range(faces - 1))]
    for who in greeted:
        pl.semaphore_signal(barrier, inc=1, device_id=who, device_id_type=MESH)
    count = len(greeted)
    for d in DIRECT:
        count = count + (faces - 1) * jnp.where(sends_far(d), 1, 0)

        @pl.when(sends_far(d))
        def _():
            for f in range(faces - 1):
                who = (partner(f)[0], lax.rem(sp + d, n_sp))
                pl.semaphore_signal(barrier, inc=1, device_id=who, device_id_type=MESH)


    pairs = [
        (pos_hbm, pos_ref), (lists_hbm, lists_ref), (near_hbm, near_ref), (count_hbm, count_ref),
        (weight_hbm, weight_ref), (sparse_hbm, sparse),
    ]
    loads = [pltpu.make_async_copy(a, b, local_sem.at[i]) for i, (a, b) in enumerate(pairs)]
    for load in loads:
        load.start()

    loads[0].wait()
    loads[1].wait()
    top = faces - 1
    for buf in (posbuf, topbuf, tab, gret, fin, fintop):
        buf[:, 4:8, :] = jnp.zeros((buf.shape[0], 4, 128), F32)
    posbuf[sp] = jnp.zeros((8, 128), F32)
    posbuf[sp, 0:3, 0:64] = pos_ref[...]
    here = posbuf[sp]
    here = here + swap(here)
    here = jnp.where(row8 == 3, lists_ref[top].astype(F32), here)
    posbuf[sp] = here
    for load in loads[2:5]:
        load.wait()
    for f in range(top):
        ohs[:, f * 128 : (f + 1) * 128] = one_hot(lists_ref[f] & 127)
    pack[...] = jnp.zeros((24, 128), jnp.int32)
    pack[:, 0:64] = near_ref[...]
    index[0:8] = jnp.where(low, pack[0:8], swap(pack[8:16]))
    last = pack[16:24]
    last = jnp.where(low, last, swap(pltpu.roll(last, 4, 0)))
    index[8:16] = jnp.where(row8 < 4, last, 0)
    for j in range(SLOTS):
        ohn[:, j * 128 : (j + 1) * 128] = one_hot(index[j : j + 1, :] & 127)
    pl.semaphore_wait(barrier, count)

    def remote(src, dst, s, r, who):
        return pltpu.make_async_remote_copy(
            src_ref=src, dst_ref=dst, send_sem=s, recv_sem=r, device_id=who, device_id_type=MESH
        )

    sent_pos = [
        remote(posbuf.at[sp, 0:4], posbuf.at[sp, 0:4], pos_s.at[d - 1], pos_r.at[d - 1], peer(d))
        for d in range(1, 8)
    ]
    for d in FAR:
        sent_pos[d - 1].start()

    sent_top = [
        remote(posbuf.at[sp, 0:4], topbuf.at[sp, 0:4], top_s.at[d], top_r.at[d], above(d)) for d in range(8)
    ]
    for d in (0, 1, 7, 2, 6, 3, 5, 4):
        sent_top[d].start()

    place = packed_place(lax.broadcasted_iota(jnp.int32, (8, 512), 1))[0:1]
    numbers = lax.broadcasted_iota(jnp.int32, (2 * ROWS, 512), 0)
    fold[...] = jnp.where(numbers == place, 1.0, 0.0).astype(BF16)
    place = packed_place(lax.broadcasted_iota(jnp.int32, (512, 128), 0))
    for k in range(0, 2 * ROWS, 128):
        n = min(128, 2 * ROWS - k)
        numbers = k + lax.broadcasted_iota(jnp.int32, (512, 128), 1)
        spread[:, k : k + n] = jnp.where(numbers == place, 1.0, 0.0).astype(BF16)[:, 0:n]
    for load in loads[5:]:
        load.wait()
    points = sparse.shape[0]

    @pl.loop(0, points // 128)
    def _(c):
        column = jnp.broadcast_to(4.0 * weight_ref[pl.ds(c, 1), :], (128, 128)).T
        wide[pl.ds(pl.multiple_of(c * 128, 128), 128), :] = column

    @pl.loop(0, points // CHUNK)
    def _(c):
        at = pl.ds(pl.multiple_of(c * CHUNK, CHUNK), CHUNK)
        folded[:, at] = lax.dot_general(
            fold[...], sparse[at, :], (((1,), (1,)), ((), ())), preferred_element_type=F32
        ).astype(BF16)

    for c in sent_pos:
        c.wait()

    for hi in range(4):
        tab[hi] = jnp.where(low, posbuf[2 * hi], posbuf[2 * hi + 1])

    def gather(tiles, hots):
        parts = jnp.concatenate(pieces(tiles.reshape(32, 128), 3), axis=0).astype(BF16)
        out = jnp.dot(parts, hots, preferred_element_type=F32)
        return out[0:32] + out[32:64] + out[64:96]

    def chosen(out, which):
        tile = jnp.zeros((8, 128), F32)
        for hi in range(4):
            tile = jnp.where(which == hi, out[hi * 8 : hi * 8 + 8], tile)
        return tile

    out = gather(tab[0:4], ohs[...])
    sent_ghost = []
    for f in range(top):
        tile = chosen(out[:, f * 128 : (f + 1) * 128], lists_ref[f] // 128)
        ghost_out[f] = jnp.where(row8 == 3, lists_ref[f].astype(F32), tile)
        c = remote(ghost_out.at[f, 0:4], tab.at[4 + f, 0:4], gho_s.at[f], gho_r.at[f], partner(f))
        c.start()
        sent_ghost.append(c)

    def look(first, last, into):
        n = (last - first) * 8
        values = tab[first:last].reshape(n, 128)
        split = jnp.concatenate(pieces(values, 3), axis=0).astype(BF16)
        for q in range(4):
            at = slice(q * 384, (q + 1) * 384)
            got = jnp.dot(split, ohn[:, at], preferred_element_type=F32)
            got = got[0:n] + got[n : 2 * n] + got[2 * n : 3 * n]
            for u in range(3):
                j = q * 3 + u
                which = index[j : j + 1, :] // 128
                tile = looked[j] if into else jnp.zeros((8, 128), F32)
                for hi in range(first, last):
                    part = got[(hi - first) * 8 : (hi - first) * 8 + 8, u * 128 : (u + 1) * 128]
                    tile = jnp.where(which == hi, part, tile)
                looked[j] = tile

    look(0, 4, False)
    for c in sent_top:
        c.wait()
    far = jnp.concatenate(
        [jnp.where(low, topbuf[2 * hi], topbuf[2 * hi + 1]) for hi in range(4)], axis=0
    )
    top_list = topbuf[sp, 3:4, :].astype(jnp.int32)
    oht[...] = one_hot(top_list & 127)
    tab[4 + top] = chosen(gather(far, oht[...]), top_list // 128)

    for c in sent_ghost:
        c.wait()
    look(4, 4 + faces, True)

    pack[0:8] = jnp.zeros((8, 128), jnp.int32)
    pack[0:1, 0:64] = count_ref[...]
    counts = pack[0:8]
    counts = jnp.broadcast_to((counts + swap(counts))[0:1], (8, 128))
    upper = lane // 64
    centre = 0.05 + 0.15 * row8.astype(F32)
    for j in range(SLOTS):
        off = 0.5 * (looked[j] - here)
        offs[j] = off
        x, y, zz = (jnp.broadcast_to(off[axis : axis + 1], (8, 128)) for axis in range(3))
        squared = x * x + y * y + zz * zz
        slot = j + 8 * upper if j < 8 else 8 + j + 4 * upper
        live = jnp.where(slot < counts, 1.0, 0.0)
        inside = 1.0 - squared * (1.0 / 3.5)
        gap = squared - centre
        bell = jnp.exp(-30.0 * gap * gap) * live
        r = bell * (inside * inside)
        radial[j] = r
        slope_r[j] = r * (-60.0 * gap) + bell * ((-2.0 / 3.5) * inside)
        power = {0: None}
        for c in range(1, 8):
            power[c] = zz if c == 1 else power[c - 1] * (zz * (1.0 / c))
            zpow[j, c - 1] = power[c]
        ys = [None]
        for c in range(1, 8):
            ys.append(y if c == 1 else ys[c - 1] * (y * (1.0 / c)))
        xs = None
        for c in range(8):
            xs = None if c == 0 else x if c == 1 else xs * (x * (1.0 / c))
            for d in range(8 - c):
                if c + d:
                    planar[j, FLAT[c, d] - 1] = xs if d == 0 else ys[d] if c == 0 else xs * ys[d]

    for (a, b), at in FLAT.items():
        rs = [radial[j] for j in range(SLOTS)]
        if at:
            rs = [r * planar[j, at - 1] for j, r in enumerate(rs)]
        for c in range(8 - a - b):
            terms = [r if c == 0 else r * zpow[j, c - 1] for j, r in enumerate(rs)]
            while len(terms) > 1:
                terms = [sum(terms[i : i + 2][1:], terms[i]) for i in range(0, len(terms), 2)]
            dens[PLACE[a, b, c]] = terms[0] + swap(terms[0])

    def turned(d):
        return jnp.where(low, d, up(d, 2))

    zero, four = [], []
    for l in range(8):
        s0 = s1 = s2 = None
        for m in range(STARTS[l], STARTS[l + 1]):
            d = dens[m]
            t = turned(d)
            y1, y2 = up(t, 1), up(t, 2)
            ahead[m, 0] = y1
            ahead[m, 1] = y2
            f = d * SPREAD[m]
            a, b, c = f * d, f * y1, f * y2
            s0, s1, s2 = (a, b, c) if s0 is None else (s0 + a, s1 + b, s2 + c)
        spec[l] = s1
        spec[8 + l] = s2
        zero.append(s0)
        four.append(s2)
    for l in range(4):
        pair = jnp.where(row8 < 4, four[2 * l], up(four[2 * l + 1], 4))
        spec[8 + l] = jnp.where(low, spec[8 + l], pair)
        spec[12 + l] = jnp.where(low, spec[12 + l], zero[l])
    for l in range(2):
        spec[16 + l] = jnp.where(low, zero[4 + l], zero[6 + l])
    twice = jnp.where(low, 2.0, 1.0)

    def times(g):
        return 2.0 if g < 12 else twice if g < 16 else 1.0

    def both(tile):
        row = jnp.sum(tile, axis=0, keepdims=True)
        tile = jnp.broadcast_to(row, (8, 128))
        return tile + swap(tile)

    total = jnp.zeros((8, 128), F32)
    for g in range(18):
        v = spec[g]
        total = total + times(g) * v * v
    scale = lax.rsqrt(both(total) + 1e-06)
    for g in range(0, 18, 2):
        two = jnp.concatenate([spec[g] * scale, spec[g + 1] * scale], axis=0)
        dbuf[0, g * 8 : g * 8 + 16, :] = two.astype(BF16)

    sent_desc = [
        remote(dbuf.at[0], dbuf.at[t], des_s.at[t - 1], des_r.at[t - 1], along(delta[t]))
        for t in range(1, 8)
    ]
    for t in (7, 5, 6, 3, 4, 1, 2):
        sent_desc[t - 1].start()

    partner_lists = [tab[4 + f, 3:4, :].astype(jnp.int32) for f in range(top)]
    for f in range(top):
        ohp[:, f * 128 : (f + 1) * 128] = one_hot(partner_lists[f] & 127)

    wlow = lax.broadcasted_iota(jnp.int32, (ROWS, 128), 1) < 64
    sent_grad = [None] * 8
    for slots in ((7, 5, 6, 3), (4, 1, 2, 0)):
        for t in slots:
            if t:
                sent_desc[t - 1].wait_recv()
        for k in range(2):
            xa = dbuf[slots[2 * k]].astype(F32)
            xb = dbuf[slots[2 * k + 1]].astype(F32)
            at = slice(k * 128, (k + 1) * 128)
            vbuf[0:ROWS, at] = jnp.where(wlow, xa, swap(xb)).astype(BF16)
            vbuf[ROWS : 2 * ROWS, at] = jnp.where(wlow, swap(xa), xb).astype(BF16)
        descs[...] = jnp.dot(spread[...], vbuf[...], preferred_element_type=F32).astype(BF16)
        energy = jnp.zeros((8, 256), F32)
        for c in range(points // CHUNK):
            at = slice(c * CHUNK, (c + 1) * CHUNK)
            score = jnp.dot(sparse[at, :], descs[...], preferred_element_type=F32)
            w = wide[at, :]
            square = score * score
            ws = jnp.concatenate([w, w], axis=1) * square
            energy = energy + jnp.sum((ws * square).reshape(CHUNK // 8, 8, 256), axis=0)
            slopes[at, :] = (ws * score).astype(BF16)
        energy = jnp.sum(energy, axis=0, keepdims=True)
        grad = jnp.dot(folded[...], slopes[...], preferred_element_type=F32)
        for k in range(2):
            a, b = slots[2 * k], slots[2 * k + 1]
            at = slice(k * 128, (k + 1) * 128)
            lo, hi = grad[0:ROWS, at], grad[ROWS : 2 * ROWS, at]
            rbuf[a, 0:ROWS, :] = jnp.where(wlow, lo, swap(hi)).astype(BF16)
            rbuf[b, 0:ROWS, :] = jnp.where(wlow, swap(lo), hi).astype(BF16)
            e = jnp.broadcast_to(energy[:, at], (8, 128))
            for t, mine in ((a, e), (b, swap(e))):
                p = pieces(mine, 3)
                tile = jnp.where(row8 == 0, p[0], jnp.where(row8 == 1, p[1], jnp.where(row8 == 2, p[2], 0.0)))
                tile = jnp.concatenate([tile, jnp.zeros((8, 128), F32)], axis=0)
                rbuf[t, ROWS:BACK, :] = tile.astype(BF16)
        for t in slots:
            if t:
                c = remote(rbuf.at[t], gbuf.at[t - 1], gra_s.at[t - 1], gra_r.at[t - 1], along(-delta[t]))
                c.start()
                sent_grad[t] = c

    summed = rbuf[0].astype(F32)
    for t in range(1, 8):
        sent_grad[t].wait_recv()
        summed = summed + gbuf[t - 1].astype(F32)
    last = summed[ROWS : ROWS + 8, :]
    energy = 0.25 * jnp.sum(last, axis=0, keepdims=True)

    dot = jnp.zeros((8, 128), F32)
    for g in range(18):
        dot = dot + summed[g * 8 : g * 8 + 8, :] * spec[g]
    dot = both(dot) * scale
    pull = []
    for g in range(18):
        pull.append(scale * (summed[g * 8 : g * 8 + 8, :] - times(g) * (spec[g] * scale) * dot))
    for l in range(8):
        ha, hb = pull[l], pull[8 + l]
        h0 = pull[12 + l] if l < 4 else swap(pull[12 + l]) if l < 6 else pull[10 + l]
        pair = pull[8 + l // 2]
        h4 = jnp.where((row8 < 4) == (l % 2 == 0), pair, up(pair, 4))
        other = swap(ha)
        k1 = ha
        k2 = jnp.where(low, hb, h4)
        k5 = up(jnp.where(low, up(other, -3), up(other, -1)), 4)
        k6 = up(jnp.where(low, up(hb, -2), 2.0 * h0), 4)
        for m in range(STARTS[l], STARTS[l + 1]):
            y1, y2 = ahead[m, 0], ahead[m, 1]
            v = k1 * y1 + k2 * y2 + up(k5 * y1 + k6 * y2, 4)
            left[m] = (v + swap(v)) * SPREAD[m]

    @pl.loop(0, SLOTS // 3)
    def _(block):
        js = [block * 3 + u for u in range(3)]
        zp = [[None] + [zpow[j, c] for c in range(7)] for j in js]
        q = [[None] * 3 for _ in range(4)]

        def add(old, new):
            return new if old is None else old + new

        def mul(tile, factor):
            return tile if factor is None else tile * factor

        for (a, b), at in FLAT.items():
            level, deriv = [None] * 3, [None] * 3
            for c in range(8 - a - b):
                d = left[PLACE[a, b, c]]
                for u in range(3):
                    level[u] = add(level[u], mul(d, zp[u][c]))
                    if c:
                        deriv[u] = add(deriv[u], mul(d, zp[u][c - 1]))
            for u, j in enumerate(js):
                flat = planar[j, at - 1] if at else None
                q[0][u] = add(q[0][u], mul(level[u], flat))
                if deriv[u] is not None:
                    q[3][u] = add(q[3][u], mul(deriv[u], flat))
                for axis, lower in ((1, (a - 1, b)), (2, (a, b - 1))):
                    if lower in FLAT:
                        flat = planar[j, FLAT[lower] - 1] if FLAT[lower] else None
                        q[axis][u] = add(q[axis][u], mul(level[u], flat))
        for u, j in enumerate(js):
            r = radial[j]
            by_square = jnp.sum(slope_r[j] * q[0][u], axis=0, keepdims=True)
            gx, gy, gz = (jnp.sum(r * q[axis][u], axis=0, keepdims=True) for axis in (1, 2, 3))
            straight = jnp.where(row8 == 0, gx, jnp.where(row8 == 1, gy, jnp.where(row8 == 2, gz, 0.0)))
            pulls[j] = 0.5 * straight + offs[j] * by_square

    centre_grad = pulls[0]
    for j in range(1, SLOTS):
        centre_grad = centre_grad + pulls[j]
    centre_grad = centre_grad + swap(centre_grad)

    def placed(tiles, which, first, last):
        rows = []
        split = [pieces(tile, 2) for tile in tiles]
        for p in range(2):
            for hi in range(first, last):
                rows.append(jnp.concatenate(
                    [jnp.where(w == hi, s[p], 0.0) for w, s in zip(which, split)], axis=1
                ))
        return jnp.concatenate(rows, axis=0).astype(BF16)

    over_lanes = (((1,), (1,)), ((), ()))

    def scatter(first, last):
        n = (last - first) * 8
        total = jnp.zeros((n, 128), F32)
        for q in range(4):
            js = range(q * 3, q * 3 + 3)
            which = [index[j : j + 1, :] // 128 for j in js]
            rows = placed([pulls[j] for j in js], which, first, last)
            got = lax.dot_general(
                rows, ohn[:, q * 384 : (q + 1) * 384], over_lanes, preferred_element_type=F32
            )
            total = total + got[0:n] + got[n : 2 * n]
        return total.reshape(last - first, 8, 128)

    gtab[4 : 4 + faces] = scatter(4, 4 + faces)
    sent_back = []
    for f in range(top):
        c = remote(gtab.at[4 + f, 0:4], gret.at[f, 0:4], ret_s.at[f], ret_r.at[f], partner(f))
        c.start()
        sent_back.append(c)

    def home(tiles, which, hots):
        got = lax.dot_general(
            placed(tiles, which, 0, 4), hots, over_lanes, preferred_element_type=F32
        )
        return (got[0:32] + got[32:64]).reshape(4, 8, 128)

    topg[...] = home([gtab[4 + top]], [top_list // 128], oht[...])
    sent_top = []
    for d in range(8):
        who = above(d)
        c = remote(topg.at[who[1] // 2, 0:4], fintop.at[d, 0:4], fit_s.at[d], fit_r.at[d], who)
        c.start()
        sent_top.append(c)
    own = scatter(0, 4)
    domown[...] = own
    def final(src, d):
        who = peer(d)
        return remote(
            src.at[who[1] // 2, 0:4], fin.at[d - 1, 0:4], fin_s.at[d - 1], fin_r.at[d - 1], who
        )

    sent_fin = {d: final(domg, d) for d in FAR}
    for d in DIRECT:
        pl.when(sends_far(d))(final(domown, d).start)
    for f in range(top):
        hots = ohp[:, f * 128 : (f + 1) * 128]
        faceg[f] = home([gtab[4 + f]], [partner_lists[f] // 128], hots)
    sent_far = {}
    for k, d in enumerate(DIRECT):
        there = lax.rem(sp + d, n_sp)
        sent_far[d] = [
            remote(
                faceg.at[f, there // 2, 0:4], farin.at[f, k, 0:4],
                far_s.at[f * 6 + k], far_r.at[f * 6 + k], (partner(f)[0], there),
            )
            for f in range(top)
        ]

        @pl.when(sends_far(d))
        def _():
            for c in sent_far[d]:
                c.start()

    for c in sent_back:
        c.wait_recv()
    which = [lists_ref[f] // 128 for f in range(top)]
    domg[...] = own + home([gret[f] for f in range(top)], which, ohs[...])
    for d in FAR:
        if d in DIRECT:
            pl.when(jnp.logical_not(sends_far(d)))(sent_fin[d].start)
        else:
            sent_fin[d].start()
    mine = domg[sp // 2]
    for d in range(8):
        sent_top[d].wait_recv()
        mine = mine + fintop[d]
    for d in reversed(FAR):
        sent_fin[d].wait_recv()
        mine = mine + fin[d - 1]
    total_ref[...] = mine
    for k, d in enumerate(DIRECT):

        @pl.when(gets_far(d))
        def _():
            for f in range(top):
                sent_far[d][f].wait_recv()
                total_ref[0:4, :] = total_ref[0:4, :] + farin[f, k, 0:4, :]

        @pl.when(sends_far(d))
        def _():
            for c in sent_far[d]:
                c.wait_send()

    mine = total_ref[...]
    odd = jnp.where(lax.rem(sp, 2) == 1, 1, 0)
    mine = jnp.where(odd == 1, swap(mine), mine)
    out_ref[...] = jnp.where(row8 == 3, energy, centre_grad - mine)
    for c in sent_desc + sent_grad[1:] + sent_back + sent_top + list(sent_fin.values()):
        c.wait_send()


def split_outputs(out_ref, energy_ref, force_ref):
    energy_ref[...] = out_ref[3:4, 0:64]
    force_ref[...] = out_ref[0:3, 0:64]


def body(positions, neighbours, counts, send_lists, sparse_points, weights):
    faces = send_lists.shape[1]
    points = sparse_points.shape[0]
    vmem = pl.BlockSpec(memory_space=pltpu.VMEM)
    hbm = pl.BlockSpec(memory_space=pl.ANY)
    dma = pltpu.SemaphoreType.DMA
    out = pl.pallas_call(
        lambda *refs: kernel(faces, *refs),
        out_shape=jax.ShapeDtypeStruct((8, 128), F32),
        in_specs=[hbm] * 6,
        out_specs=vmem,
        scratch_shapes=[
            pltpu.VMEM(positions.shape, F32),
            pltpu.VMEM(neighbours.shape, jnp.int32),
            pltpu.VMEM((1, counts.shape[0]), jnp.int32),
            pltpu.VMEM((faces, 1, 128), jnp.int32),
            pltpu.VMEM((points // 128, 128), F32),
            pltpu.VMEM((8, 8, 128), F32),
            pltpu.VMEM((8, 8, 128), F32),
            pltpu.VMEM((faces - 1, 8, 128), F32),
            pltpu.VMEM((4 + faces, 8, 128), F32),
            pltpu.VMEM((24, 128), jnp.int32),
            pltpu.VMEM((16, 128), jnp.int32),
            pltpu.VMEM((128, (faces - 1) * 128), BF16),
            pltpu.VMEM((128, 128), BF16),
            pltpu.VMEM((128, (faces - 1) * 128), BF16),
            pltpu.VMEM((128, SLOTS * 128), BF16),
            pltpu.VMEM((SLOTS, 8, 128), F32),
            pltpu.VMEM((SLOTS, 8, 128), F32),
            pltpu.VMEM((SLOTS, 7, 8, 128), F32),
            pltpu.VMEM((SLOTS, 35, 8, 128), F32),
            pltpu.VMEM((120, 2, 8, 128), F32),
            pltpu.VMEM((SLOTS, 8, 128), F32),
            pltpu.VMEM((SLOTS, 8, 128), F32),
            pltpu.VMEM((120, 8, 128), F32),
            pltpu.VMEM((18, 8, 128), F32),
            pltpu.VMEM((8, ROWS, 128), BF16),
            pltpu.VMEM((8, BACK, 128), BF16),
            pltpu.VMEM((7, BACK, 128), BF16),
            pltpu.VMEM((2 * ROWS, 256), BF16),
            pltpu.VMEM((512, 256), BF16),
            pltpu.VMEM((points, 256), BF16),
            pltpu.VMEM((points, 512), BF16),
            pltpu.VMEM((2 * ROWS, 512), BF16),
            pltpu.VMEM((512, 2 * ROWS), BF16),
            pltpu.VMEM((2 * ROWS, points), BF16),
            pltpu.VMEM((points, 128), F32),
            pltpu.VMEM((120, 8, 128), F32),
            pltpu.VMEM((SLOTS, 8, 128), F32),
            pltpu.VMEM((4 + faces, 8, 128), F32),
            pltpu.VMEM((faces - 1, 8, 128), F32),
            pltpu.VMEM((4, 8, 128), F32),
            pltpu.VMEM((7, 8, 128), F32),
            pltpu.VMEM((4, 8, 128), F32),
            pltpu.VMEM((8, 8, 128), F32),
            pltpu.VMEM((4, 8, 128), F32),
            pltpu.VMEM((faces - 1, 4, 8, 128), F32),
            pltpu.VMEM((faces - 1, 6, 8, 128), F32),
            pltpu.VMEM((8, 128), F32),
            dma((6,)),
            dma((7,)), dma((7,)),
            dma((8,)), dma((8,)),
            dma((faces - 1,)), dma((faces - 1,)),
            dma((7,)), dma((7,)),
            dma((7,)), dma((7,)),
            dma((faces - 1,)), dma((faces - 1,)),
            dma((7,)), dma((7,)),
            dma((8,)), dma((8,)),
            dma(((faces - 1) * 6,)), dma(((faces - 1) * 6,)),
        ],
        compiler_params=pltpu.CompilerParams(
            collective_id=0, has_side_effects=True, vmem_limit_bytes=60 * 2**20
        ),
        name="gap_forces",
    )(
        positions,
        neighbours,
        counts.reshape(1, -1),
        send_lists.transpose(1, 0, 2),
        sparse_points,
        weights.reshape(-1, 128),
    )
    energies, forces = pl.pallas_call(
        split_outputs,
        out_shape=(jax.ShapeDtypeStruct((1, 64), F32), jax.ShapeDtypeStruct((3, 64), F32)),
        in_specs=[vmem],
        out_specs=(vmem, vmem),
        compiler_params=pltpu.CompilerParams(vmem_limit_bytes=60 * 2**20),
        name="split_outputs",
    )(out)
    return energies.reshape(-1), forces


def solution(mesh):
    in_specs = (
        P(None, ("dom", "sp")),
        P(None, ("dom", "sp")),
        P(("dom", "sp")),
        P("dom", None, None),
        P("sp", None),
        P("sp"),
    )
    out_specs = (P(("dom", "sp")), P(None, ("dom", "sp")))
    return jax.shard_map(body, mesh=mesh, in_specs=in_specs, out_specs=out_specs, check_vma=False)
```

```python
import math

import jax
import jax.numpy as jnp
from jax import lax
from jax.experimental import pallas as pl
from jax.experimental.pallas import tpu as pltpu
from jax.sharding import PartitionSpec as P

F32, BF16 = jnp.float32, jnp.bfloat16
MESH = pl.DeviceIdType.MESH
SLOTS = 12
ROWS = 144
CHUNK = 512
DIRECT = (7, 1, 6, 2, 5, 3)
FAR = (7, 1, 6, 2, 5, 3, 4)


def powers():
    found, starts = [], []
    for degree in range(8):
        starts.append(len(found))
        for a in range(degree, -1, -1):
            for b in range(degree - a, -1, -1):
                found.append((a, b, degree - a - b))
    return found, starts + [len(found)]


POWERS, STARTS = powers()
PLACE = {p: i for i, p in enumerate(POWERS)}
SPREAD = [
    float(math.factorial(sum(p)) * math.prod(math.factorial(e) for e in p)) for p in POWERS
]


FLAT = {(a, b): i for i, (a, b) in enumerate((a, b) for a in range(8) for b in range(8 - a))}


def packed_place(e):
    n, n2, l = e // 64, (e // 8) & 7, e & 7
    r = (n2 - n) & 7
    first = jnp.where(r > 4, n2, n)
    r = jnp.where(r > 4, 8 - r, r)
    row = jnp.where(r == 4, (first & 3) + 4 * (l & 1), first)
    diagonal = jnp.where(l < 4, 12 + l, 16 + (l & 1))
    group = jnp.where(
        r == 0, diagonal, jnp.where(r == 4, 8 + l // 2, jnp.where(r == 2, 8 + l, l))
    )
    half = jnp.where(r == 0, jnp.where((l == 4) | (l == 5), 0, 1), jnp.where(r > 2, 1, 0))
    return half * ROWS + group * 8 + row


def up(x, k):
    return x if k % 8 == 0 else pltpu.roll(x, (8 - k) % 8, 0)


def swap(x):
    return pltpu.roll(x, 64, 1)


def pieces(x, count):
    out = []
    for _ in range(count):
        p = x.astype(BF16).astype(F32)
        out.append(p)
        x = x - p
    return out


def one_hot(row):
    return jnp.where(lax.broadcasted_iota(jnp.int32, (128, 128), 0) == row, 1.0, 0.0).astype(BF16)


def kernel(
    faces, pos_hbm, near_hbm, count_hbm, lists_hbm, sparse_hbm, weight_hbm,
    out_ref,
    pos_ref, near_ref, count_ref, lists_ref, weight_ref,
    posbuf, topbuf, ghost_out, tab, pack, index, ohs, oht, ohp, ohn, looked, offs, zpow, planar, ahead, radial, slope_r, dens,
    spec, dbuf, rbuf, gbuf, eout, ein, vbuf, descs, slopes, sparse, fold, spread, folded, wide, left, pulls,
    gtab, gret, domg, fin, topg, fintop, domown, faceg, farin, total_ref,
    local_sem, pos_s, pos_r, top_s, top_r, gho_s, gho_r, des_s, des_r, gra_s, gra_r, ret_s, ret_r, fin_s, fin_r, fit_s, fit_r, far_s, far_r, ene_s, ene_r,
):
    dom, sp = lax.axis_index("dom"), lax.axis_index("sp")
    n_dom, n_sp = lax.axis_size("dom"), lax.axis_size("sp")
    below = n_dom // 2
    ring = 2 * n_sp
    z = (dom // below) * n_sp + sp
    rest = lax.rem(dom, below)
    side = 1 - 2 * lax.rem(dom, 2)

    def along(delta):
        there = lax.rem(z + delta + ring, ring)
        return (rest + (there // n_sp) * below, lax.rem(there, n_sp))

    def peer(delta):
        return (dom, lax.rem(sp + delta, n_sp))

    def partner(face):
        bit = lax.rem(dom // 2**face, 2)
        return (dom + (1 - 2 * bit) * 2**face, sp)

    delta = [0, 1, -1, 2, -2, 3, -3, 4 * side]
    lane = lax.broadcasted_iota(jnp.int32, (8, 128), 1)
    low = lane < 64
    row8 = lax.broadcasted_iota(jnp.int32, (8, 128), 0)

    def sends_far(d):
        return sp + d < n_sp if d >= 5 else sp + d >= n_sp

    def gets_far(d):
        return sp >= d if d >= 5 else sp < d

    def above(d):
        return (lax.rem(dom + below, n_dom), lax.rem(sp + d, n_sp))

    barrier = pltpu.get_barrier_semaphore()
    greeted = [above(d) for d in (0, 1, 7, 2, 6, 3, 5, 4)] + [peer(d) for d in FAR]
    greeted += [partner(f) for f in reversed(range(faces - 1))]
    for who in greeted:
        pl.semaphore_signal(barrier, inc=1, device_id=who, device_id_type=MESH)
    count = len(greeted)
    for d in DIRECT:
        count = count + (faces - 1) * jnp.where(sends_far(d), 1, 0)

        @pl.when(sends_far(d))
        def _():
            for f in range(faces - 1):
                who = (partner(f)[0], lax.rem(sp + d, n_sp))
                pl.semaphore_signal(barrier, inc=1, device_id=who, device_id_type=MESH)


    pairs = [
        (pos_hbm, pos_ref), (lists_hbm, lists_ref), (near_hbm, near_ref), (count_hbm, count_ref),
        (weight_hbm, weight_ref), (sparse_hbm, sparse),
    ]
    loads = [pltpu.make_async_copy(a, b, local_sem.at[i]) for i, (a, b) in enumerate(pairs)]
    for load in loads:
        load.start()

    loads[0].wait()
    loads[1].wait()
    top = faces - 1
    for buf in (posbuf, topbuf, tab, gret, fin, fintop):
        buf[:, 4:8, :] = jnp.zeros((buf.shape[0], 4, 128), F32)
    posbuf[sp] = jnp.zeros((8, 128), F32)
    posbuf[sp, 0:3, 0:64] = pos_ref[...]
    here = posbuf[sp]
    here = here + swap(here)
    here = jnp.where(row8 == 3, lists_ref[top].astype(F32), here)
    posbuf[sp] = here
    for load in loads[2:5]:
        load.wait()
    for f in range(top):
        ohs[:, f * 128 : (f + 1) * 128] = one_hot(lists_ref[f] & 127)
    pack[...] = jnp.zeros((24, 128), jnp.int32)
    pack[:, 0:64] = near_ref[...]
    index[0:8] = jnp.where(low, pack[0:8], swap(pack[8:16]))
    last = pack[16:24]
    last = jnp.where(low, last, swap(pltpu.roll(last, 4, 0)))
    index[8:16] = jnp.where(row8 < 4, last, 0)
    for j in range(SLOTS):
        ohn[:, j * 128 : (j + 1) * 128] = one_hot(index[j : j + 1, :] & 127)
    pl.semaphore_wait(barrier, count)

    def remote(src, dst, s, r, who):
        return pltpu.make_async_remote_copy(
            src_ref=src, dst_ref=dst, send_sem=s, recv_sem=r, device_id=who, device_id_type=MESH
        )

    sent_pos = [
        remote(posbuf.at[sp, 0:4], posbuf.at[sp, 0:4], pos_s.at[d - 1], pos_r.at[d - 1], peer(d))
        for d in range(1, 8)
    ]
    for d in FAR:
        sent_pos[d - 1].start()

    sent_top = [
        remote(posbuf.at[sp, 0:4], topbuf.at[sp, 0:4], top_s.at[d], top_r.at[d], above(d)) for d in range(8)
    ]
    for d in (0, 1, 7, 2, 6, 3, 5, 4):
        sent_top[d].start()

    place = packed_place(lax.broadcasted_iota(jnp.int32, (8, 512), 1))[0:1]
    numbers = lax.broadcasted_iota(jnp.int32, (2 * ROWS, 512), 0)
    fold[...] = jnp.where(numbers == place, 1.0, 0.0).astype(BF16)
    place = packed_place(lax.broadcasted_iota(jnp.int32, (512, 128), 0))
    for k in range(0, 2 * ROWS, 128):
        n = min(128, 2 * ROWS - k)
        numbers = k + lax.broadcasted_iota(jnp.int32, (512, 128), 1)
        spread[:, k : k + n] = jnp.where(numbers == place, 1.0, 0.0).astype(BF16)[:, 0:n]
    for load in loads[5:]:
        load.wait()
    points = sparse.shape[0]

    @pl.loop(0, points // 128)
    def _(c):
        column = jnp.broadcast_to(4.0 * weight_ref[pl.ds(c, 1), :], (128, 128)).T
        wide[pl.ds(pl.multiple_of(c * 128, 128), 128), :] = column

    @pl.loop(0, points // CHUNK)
    def _(c):
        at = pl.ds(pl.multiple_of(c * CHUNK, CHUNK), CHUNK)
        folded[:, at] = lax.dot_general(
            fold[...], sparse[at, :], (((1,), (1,)), ((), ())), preferred_element_type=F32
        ).astype(BF16)

    for c in sent_pos:
        c.wait()

    for hi in range(4):
        tab[hi] = jnp.where(low, posbuf[2 * hi], posbuf[2 * hi + 1])

    def gather(tiles, hots):
        parts = jnp.concatenate(pieces(tiles.reshape(32, 128), 3), axis=0).astype(BF16)
        out = jnp.dot(parts, hots, preferred_element_type=F32)
        return out[0:32] + out[32:64] + out[64:96]

    def chosen(out, which):
        tile = jnp.zeros((8, 128), F32)
        for hi in range(4):
            tile = jnp.where(which == hi, out[hi * 8 : hi * 8 + 8], tile)
        return tile

    out = gather(tab[0:4], ohs[...])
    sent_ghost = []
    for f in range(top):
        tile = chosen(out[:, f * 128 : (f + 1) * 128], lists_ref[f] // 128)
        ghost_out[f] = jnp.where(row8 == 3, lists_ref[f].astype(F32), tile)
        c = remote(ghost_out.at[f, 0:4], tab.at[4 + f, 0:4], gho_s.at[f], gho_r.at[f], partner(f))
        c.start()
        sent_ghost.append(c)

    def look(first, last, into):
        n = (last - first) * 8
        values = tab[first:last].reshape(n, 128)
        split = jnp.concatenate(pieces(values, 3), axis=0).astype(BF16)
        for q in range(4):
            at = slice(q * 384, (q + 1) * 384)
            got = jnp.dot(split, ohn[:, at], preferred_element_type=F32)
            got = got[0:n] + got[n : 2 * n] + got[2 * n : 3 * n]
            for u in range(3):
                j = q * 3 + u
                which = index[j : j + 1, :] // 128
                tile = looked[j] if into else jnp.zeros((8, 128), F32)
                for hi in range(first, last):
                    part = got[(hi - first) * 8 : (hi - first) * 8 + 8, u * 128 : (u + 1) * 128]
                    tile = jnp.where(which == hi, part, tile)
                looked[j] = tile

    look(0, 4, False)
    for c in sent_top:
        c.wait()
    far = jnp.concatenate(
        [jnp.where(low, topbuf[2 * hi], topbuf[2 * hi + 1]) for hi in range(4)], axis=0
    )
    top_list = topbuf[sp, 3:4, :].astype(jnp.int32)
    oht[...] = one_hot(top_list & 127)
    tab[4 + top] = chosen(gather(far, oht[...]), top_list // 128)

    for c in sent_ghost:
        c.wait()
    look(4, 4 + faces, True)

    pack[0:8] = jnp.zeros((8, 128), jnp.int32)
    pack[0:1, 0:64] = count_ref[...]
    counts = pack[0:8]
    counts = jnp.broadcast_to((counts + swap(counts))[0:1], (8, 128))
    upper = lane // 64
    centre = 0.05 + 0.15 * row8.astype(F32)
    for j in range(SLOTS):
        off = 0.5 * (looked[j] - here)
        offs[j] = off
        x, y, zz = (jnp.broadcast_to(off[axis : axis + 1], (8, 128)) for axis in range(3))
        squared = x * x + y * y + zz * zz
        slot = j + 8 * upper if j < 8 else 8 + j + 4 * upper
        live = jnp.where(slot < counts, 1.0, 0.0)
        inside = 1.0 - squared * (1.0 / 3.5)
        gap = squared - centre
        bell = jnp.exp(-30.0 * gap * gap) * live
        r = bell * (inside * inside)
        radial[j] = r
        slope_r[j] = r * (-60.0 * gap) + bell * ((-2.0 / 3.5) * inside)
        power = {0: None}
        for c in range(1, 8):
            power[c] = zz if c == 1 else power[c - 1] * (zz * (1.0 / c))
            zpow[j, c - 1] = power[c]
        ys = [None]
        for c in range(1, 8):
            ys.append(y if c == 1 else ys[c - 1] * (y * (1.0 / c)))
        xs = None
        for c in range(8):
            xs = None if c == 0 else x if c == 1 else xs * (x * (1.0 / c))
            for d in range(8 - c):
                if c + d:
                    planar[j, FLAT[c, d] - 1] = xs if d == 0 else ys[d] if c == 0 else xs * ys[d]

    for (a, b), at in FLAT.items():
        rs = [radial[j] for j in range(SLOTS)]
        if at:
            rs = [r * planar[j, at - 1] for j, r in enumerate(rs)]
        for c in range(8 - a - b):
            terms = [r if c == 0 else r * zpow[j, c - 1] for j, r in enumerate(rs)]
            while len(terms) > 1:
                terms = [sum(terms[i : i + 2][1:], terms[i]) for i in range(0, len(terms), 2)]
            dens[PLACE[a, b, c]] = terms[0] + swap(terms[0])

    def turned(d):
        return jnp.where(low, d, up(d, 2))

    zero, four = [], []
    for l in range(8):
        s0 = s1 = s2 = None
        for m in range(STARTS[l], STARTS[l + 1]):
            d = dens[m]
            t = turned(d)
            y1, y2 = up(t, 1), up(t, 2)
            ahead[m, 0] = y1
            ahead[m, 1] = y2
            f = d * SPREAD[m]
            a, b, c = f * d, f * y1, f * y2
            s0, s1, s2 = (a, b, c) if s0 is None else (s0 + a, s1 + b, s2 + c)
        spec[l] = s1
        spec[8 + l] = s2
        zero.append(s0)
        four.append(s2)
    for l in range(4):
        pair = jnp.where(row8 < 4, four[2 * l], up(four[2 * l + 1], 4))
        spec[8 + l] = jnp.where(low, spec[8 + l], pair)
        spec[12 + l] = jnp.where(low, spec[12 + l], zero[l])
    for l in range(2):
        spec[16 + l] = jnp.where(low, zero[4 + l], zero[6 + l])
    twice = jnp.where(low, 2.0, 1.0)

    def times(g):
        return 2.0 if g < 12 else twice if g < 16 else 1.0

    def both(tile):
        row = jnp.sum(tile, axis=0, keepdims=True)
        tile = jnp.broadcast_to(row, (8, 128))
        return tile + swap(tile)

    total = jnp.zeros((8, 128), F32)
    for g in range(18):
        v = spec[g]
        total = total + times(g) * v * v
    scale = lax.rsqrt(both(total) + 1e-06)
    for g in range(0, 18, 2):
        two = jnp.concatenate([spec[g] * scale, spec[g + 1] * scale], axis=0)
        dbuf[0, g * 8 : g * 8 + 16, :] = two.astype(BF16)

    sent_desc = [
        remote(dbuf.at[0], dbuf.at[t], des_s.at[t - 1], des_r.at[t - 1], along(delta[t]))
        for t in range(1, 8)
    ]
    for t in (7, 5, 6, 3, 4, 1, 2):
        sent_desc[t - 1].start()

    partner_lists = [tab[4 + f, 3:4, :].astype(jnp.int32) for f in range(top)]
    for f in range(top):
        ohp[:, f * 128 : (f + 1) * 128] = one_hot(partner_lists[f] & 127)

    wlow = lax.broadcasted_iota(jnp.int32, (ROWS, 128), 1) < 64
    sent_grad, sent_energy = [None] * 8, [None] * 8
    for slots in ((7, 5, 6, 3), (4, 1, 2, 0)):
        for t in slots:
            if t:
                sent_desc[t - 1].wait_recv()
        for k in range(2):
            xa = dbuf[slots[2 * k]].astype(F32)
            xb = dbuf[slots[2 * k + 1]].astype(F32)
            at = slice(k * 128, (k + 1) * 128)
            vbuf[0:ROWS, at] = jnp.where(wlow, xa, swap(xb)).astype(BF16)
            vbuf[ROWS : 2 * ROWS, at] = jnp.where(wlow, swap(xa), xb).astype(BF16)
        descs[...] = jnp.dot(spread[...], vbuf[...], preferred_element_type=F32).astype(BF16)
        energy = jnp.zeros((8, 256), F32)
        for c in range(points // CHUNK):
            at = slice(c * CHUNK, (c + 1) * CHUNK)
            score = jnp.dot(sparse[at, :], descs[...], preferred_element_type=F32)
            w = wide[at, :]
            square = score * score
            ws = jnp.concatenate([w, w], axis=1) * square
            energy = energy + jnp.sum((ws * square).reshape(CHUNK // 8, 8, 256), axis=0)
            slopes[at, :] = (ws * score).astype(BF16)
        energy = jnp.sum(energy, axis=0, keepdims=True)
        grad = jnp.dot(folded[...], slopes[...], preferred_element_type=F32)
        for k in range(2):
            a, b = slots[2 * k], slots[2 * k + 1]
            at = slice(k * 128, (k + 1) * 128)
            lo, hi = grad[0:ROWS, at], grad[ROWS : 2 * ROWS, at]
            rbuf[a] = jnp.where(wlow, lo, swap(hi)).astype(BF16)
            rbuf[b] = jnp.where(wlow, swap(lo), hi).astype(BF16)
            e = jnp.broadcast_to(energy[:, at], (8, 128))
            for t, mine in ((a, e), (b, swap(e))):
                eout[t] = mine
        for t in slots:
            if t:
                c = remote(rbuf.at[t], gbuf.at[t - 1], gra_s.at[t - 1], gra_r.at[t - 1], along(-delta[t]))
                c.start()
                sent_grad[t] = c
        for t in slots:
            if t:
                c = remote(
                    eout.at[t, 0:1], ein.at[t - 1, 0:1], ene_s.at[t - 1], ene_r.at[t - 1], along(-delta[t])
                )
                c.start()
                sent_energy[t] = c

    summed = rbuf[0].astype(F32)
    for t in range(1, 8):
        sent_grad[t].wait_recv()
        summed = summed + gbuf[t - 1].astype(F32)
    dot = jnp.zeros((8, 128), F32)
    for g in range(18):
        dot = dot + summed[g * 8 : g * 8 + 8, :] * spec[g]
    dot = both(dot) * scale
    pull = []
    for g in range(18):
        pull.append(scale * (summed[g * 8 : g * 8 + 8, :] - times(g) * (spec[g] * scale) * dot))
    for l in range(8):
        ha, hb = pull[l], pull[8 + l]
        h0 = pull[12 + l] if l < 4 else swap(pull[12 + l]) if l < 6 else pull[10 + l]
        pair = pull[8 + l // 2]
        h4 = jnp.where((row8 < 4) == (l % 2 == 0), pair, up(pair, 4))
        other = swap(ha)
        k1 = ha
        k2 = jnp.where(low, hb, h4)
        k5 = up(jnp.where(low, up(other, -3), up(other, -1)), 4)
        k6 = up(jnp.where(low, up(hb, -2), 2.0 * h0), 4)
        for m in range(STARTS[l], STARTS[l + 1]):
            y1, y2 = ahead[m, 0], ahead[m, 1]
            v = k1 * y1 + k2 * y2 + up(k5 * y1 + k6 * y2, 4)
            left[m] = (v + swap(v)) * SPREAD[m]

    @pl.loop(0, SLOTS // 3)
    def _(block):
        js = [block * 3 + u for u in range(3)]
        zp = [[None] + [zpow[j, c] for c in range(7)] for j in js]
        q = [[None] * 3 for _ in range(4)]

        def add(old, new):
            return new if old is None else old + new

        def mul(tile, factor):
            return tile if factor is None else tile * factor

        for (a, b), at in FLAT.items():
            level, deriv = [None] * 3, [None] * 3
            for c in range(8 - a - b):
                d = left[PLACE[a, b, c]]
                for u in range(3):
                    level[u] = add(level[u], mul(d, zp[u][c]))
                    if c:
                        deriv[u] = add(deriv[u], mul(d, zp[u][c - 1]))
            for u, j in enumerate(js):
                flat = planar[j, at - 1] if at else None
                q[0][u] = add(q[0][u], mul(level[u], flat))
                if deriv[u] is not None:
                    q[3][u] = add(q[3][u], mul(deriv[u], flat))
                for axis, lower in ((1, (a - 1, b)), (2, (a, b - 1))):
                    if lower in FLAT:
                        flat = planar[j, FLAT[lower] - 1] if FLAT[lower] else None
                        q[axis][u] = add(q[axis][u], mul(level[u], flat))
        for u, j in enumerate(js):
            r = radial[j]
            by_square = jnp.sum(slope_r[j] * q[0][u], axis=0, keepdims=True)
            gx, gy, gz = (jnp.sum(r * q[axis][u], axis=0, keepdims=True) for axis in (1, 2, 3))
            straight = jnp.where(row8 == 0, gx, jnp.where(row8 == 1, gy, jnp.where(row8 == 2, gz, 0.0)))
            pulls[j] = 0.5 * straight + offs[j] * by_square

    centre_grad = pulls[0]
    for j in range(1, SLOTS):
        centre_grad = centre_grad + pulls[j]
    centre_grad = centre_grad + swap(centre_grad)

    def placed(tiles, which, first, last):
        rows = []
        split = [pieces(tile, 2) for tile in tiles]
        for p in range(2):
            for hi in range(first, last):
                rows.append(jnp.concatenate(
                    [jnp.where(w == hi, s[p], 0.0) for w, s in zip(which, split)], axis=1
                ))
        return jnp.concatenate(rows, axis=0).astype(BF16)

    over_lanes = (((1,), (1,)), ((), ()))

    def scatter(first, last):
        n = (last - first) * 8
        total = jnp.zeros((n, 128), F32)
        for q in range(4):
            js = range(q * 3, q * 3 + 3)
            which = [index[j : j + 1, :] // 128 for j in js]
            rows = placed([pulls[j] for j in js], which, first, last)
            got = lax.dot_general(
                rows, ohn[:, q * 384 : (q + 1) * 384], over_lanes, preferred_element_type=F32
            )
            total = total + got[0:n] + got[n : 2 * n]
        return total.reshape(last - first, 8, 128)

    gtab[4 : 4 + faces] = scatter(4, 4 + faces)
    sent_back = []
    for f in range(top):
        c = remote(gtab.at[4 + f, 0:4], gret.at[f, 0:4], ret_s.at[f], ret_r.at[f], partner(f))
        c.start()
        sent_back.append(c)

    def home(tiles, which, hots):
        got = lax.dot_general(
            placed(tiles, which, 0, 4), hots, over_lanes, preferred_element_type=F32
        )
        return (got[0:32] + got[32:64]).reshape(4, 8, 128)

    topg[...] = home([gtab[4 + top]], [top_list // 128], oht[...])
    sent_top = []
    for d in range(8):
        who = above(d)
        c = remote(topg.at[who[1] // 2, 0:4], fintop.at[d, 0:4], fit_s.at[d], fit_r.at[d], who)
        c.start()
        sent_top.append(c)
    own = scatter(0, 4)
    domown[...] = own
    def final(src, d):
        who = peer(d)
        return remote(
            src.at[who[1] // 2, 0:4], fin.at[d - 1, 0:4], fin_s.at[d - 1], fin_r.at[d - 1], who
        )

    sent_fin = {d: final(domg, d) for d in FAR}
    for d in DIRECT:
        pl.when(sends_far(d))(final(domown, d).start)
    for f in range(top):
        hots = ohp[:, f * 128 : (f + 1) * 128]
        faceg[f] = home([gtab[4 + f]], [partner_lists[f] // 128], hots)
    sent_far = {}
    for k, d in enumerate(DIRECT):
        there = lax.rem(sp + d, n_sp)
        sent_far[d] = [
            remote(
                faceg.at[f, there // 2, 0:4], farin.at[f, k, 0:4],
                far_s.at[f * 6 + k], far_r.at[f * 6 + k], (partner(f)[0], there),
            )
            for f in range(top)
        ]

        @pl.when(sends_far(d))
        def _():
            for c in sent_far[d]:
                c.start()

    for c in sent_back:
        c.wait_recv()
    which = [lists_ref[f] // 128 for f in range(top)]
    domg[...] = own + home([gret[f] for f in range(top)], which, ohs[...])
    for d in FAR:
        if d in DIRECT:
            pl.when(jnp.logical_not(sends_far(d)))(sent_fin[d].start)
        else:
            sent_fin[d].start()
    mine = domg[sp // 2]
    for d in range(8):
        sent_top[d].wait_recv()
        mine = mine + fintop[d]
    for d in reversed(FAR):
        sent_fin[d].wait_recv()
        mine = mine + fin[d - 1]
    total_ref[...] = mine
    for k, d in enumerate(DIRECT):

        @pl.when(gets_far(d))
        def _():
            for f in range(top):
                sent_far[d][f].wait_recv()
                total_ref[0:4, :] = total_ref[0:4, :] + farin[f, k, 0:4, :]

        @pl.when(sends_far(d))
        def _():
            for c in sent_far[d]:
                c.wait_send()

    energy = eout[0, 0:1, :]
    for t in range(1, 8):
        sent_energy[t].wait_recv()
        energy = energy + ein[t - 1, 0:1, :]
    energy = 0.25 * energy
    mine = total_ref[...]
    odd = jnp.where(lax.rem(sp, 2) == 1, 1, 0)
    mine = jnp.where(odd == 1, swap(mine), mine)
    out_ref[...] = jnp.where(row8 == 3, energy, centre_grad - mine)
    for c in sent_desc + sent_grad[1:] + sent_energy[1:] + sent_back + sent_top + list(sent_fin.values()):
        c.wait_send()


def split_outputs(out_ref, energy_ref, force_ref):
    energy_ref[...] = out_ref[3:4, 0:64]
    force_ref[...] = out_ref[0:3, 0:64]


def body(positions, neighbours, counts, send_lists, sparse_points, weights):
    faces = send_lists.shape[1]
    points = sparse_points.shape[0]
    vmem = pl.BlockSpec(memory_space=pltpu.VMEM)
    hbm = pl.BlockSpec(memory_space=pl.ANY)
    dma = pltpu.SemaphoreType.DMA
    out = pl.pallas_call(
        lambda *refs: kernel(faces, *refs),
        out_shape=jax.ShapeDtypeStruct((8, 128), F32),
        in_specs=[hbm] * 6,
        out_specs=vmem,
        scratch_shapes=[
            pltpu.VMEM(positions.shape, F32),
            pltpu.VMEM(neighbours.shape, jnp.int32),
            pltpu.VMEM((1, counts.shape[0]), jnp.int32),
            pltpu.VMEM((faces, 1, 128), jnp.int32),
            pltpu.VMEM((points // 128, 128), F32),
            pltpu.VMEM((8, 8, 128), F32),
            pltpu.VMEM((8, 8, 128), F32),
            pltpu.VMEM((faces - 1, 8, 128), F32),
            pltpu.VMEM((4 + faces, 8, 128), F32),
            pltpu.VMEM((24, 128), jnp.int32),
            pltpu.VMEM((16, 128), jnp.int32),
            pltpu.VMEM((128, (faces - 1) * 128), BF16),
            pltpu.VMEM((128, 128), BF16),
            pltpu.VMEM((128, (faces - 1) * 128), BF16),
            pltpu.VMEM((128, SLOTS * 128), BF16),
            pltpu.VMEM((SLOTS, 8, 128), F32),
            pltpu.VMEM((SLOTS, 8, 128), F32),
            pltpu.VMEM((SLOTS, 7, 8, 128), F32),
            pltpu.VMEM((SLOTS, 35, 8, 128), F32),
            pltpu.VMEM((120, 2, 8, 128), F32),
            pltpu.VMEM((SLOTS, 8, 128), F32),
            pltpu.VMEM((SLOTS, 8, 128), F32),
            pltpu.VMEM((120, 8, 128), F32),
            pltpu.VMEM((18, 8, 128), F32),
            pltpu.VMEM((8, ROWS, 128), BF16),
            pltpu.VMEM((8, ROWS, 128), BF16),
            pltpu.VMEM((7, ROWS, 128), BF16),
            pltpu.VMEM((8, 8, 128), F32),
            pltpu.VMEM((7, 8, 128), F32),
            pltpu.VMEM((2 * ROWS, 256), BF16),
            pltpu.VMEM((512, 256), BF16),
            pltpu.VMEM((points, 256), BF16),
            pltpu.VMEM((points, 512), BF16),
            pltpu.VMEM((2 * ROWS, 512), BF16),
            pltpu.VMEM((512, 2 * ROWS), BF16),
            pltpu.VMEM((2 * ROWS, points), BF16),
            pltpu.VMEM((points, 128), F32),
            pltpu.VMEM((120, 8, 128), F32),
            pltpu.VMEM((SLOTS, 8, 128), F32),
            pltpu.VMEM((4 + faces, 8, 128), F32),
            pltpu.VMEM((faces - 1, 8, 128), F32),
            pltpu.VMEM((4, 8, 128), F32),
            pltpu.VMEM((7, 8, 128), F32),
            pltpu.VMEM((4, 8, 128), F32),
            pltpu.VMEM((8, 8, 128), F32),
            pltpu.VMEM((4, 8, 128), F32),
            pltpu.VMEM((faces - 1, 4, 8, 128), F32),
            pltpu.VMEM((faces - 1, 6, 8, 128), F32),
            pltpu.VMEM((8, 128), F32),
            dma((6,)),
            dma((7,)), dma((7,)),
            dma((8,)), dma((8,)),
            dma((faces - 1,)), dma((faces - 1,)),
            dma((7,)), dma((7,)),
            dma((7,)), dma((7,)),
            dma((faces - 1,)), dma((faces - 1,)),
            dma((7,)), dma((7,)),
            dma((8,)), dma((8,)),
            dma(((faces - 1) * 6,)), dma(((faces - 1) * 6,)),
            dma((7,)), dma((7,)),
        ],
        compiler_params=pltpu.CompilerParams(
            collective_id=0, has_side_effects=True, vmem_limit_bytes=60 * 2**20
        ),
        name="gap_forces",
    )(
        positions,
        neighbours,
        counts.reshape(1, -1),
        send_lists.transpose(1, 0, 2),
        sparse_points,
        weights.reshape(-1, 128),
    )
    energies, forces = pl.pallas_call(
        split_outputs,
        out_shape=(jax.ShapeDtypeStruct((1, 64), F32), jax.ShapeDtypeStruct((3, 64), F32)),
        in_specs=[vmem],
        out_specs=(vmem, vmem),
        compiler_params=pltpu.CompilerParams(vmem_limit_bytes=60 * 2**20),
        name="split_outputs",
    )(out)
    return energies.reshape(-1), forces


def solution(mesh):
    in_specs = (
        P(None, ("dom", "sp")),
        P(None, ("dom", "sp")),
        P(("dom", "sp")),
        P("dom", None, None),
        P("sp", None),
        P("sp"),
    )
    out_specs = (P(("dom", "sp")), P(None, ("dom", "sp")))
    return jax.shard_map(body, mesh=mesh, in_specs=in_specs, out_specs=out_specs, check_vma=False)
```

```python
import math

import jax
import jax.numpy as jnp
from jax import lax
from jax.experimental import pallas as pl
from jax.experimental.pallas import tpu as pltpu
from jax.sharding import PartitionSpec as P

F32, BF16 = jnp.float32, jnp.bfloat16
MESH = pl.DeviceIdType.MESH
SLOTS = 12
ROWS = 144
CHUNK = 512
DIRECT = (7, 1, 6, 2, 5, 3)
FAR = (7, 1, 6, 2, 5, 3, 4)


def powers():
    found, starts = [], []
    for degree in range(8):
        starts.append(len(found))
        for a in range(degree, -1, -1):
            for b in range(degree - a, -1, -1):
                found.append((a, b, degree - a - b))
    return found, starts + [len(found)]


POWERS, STARTS = powers()
PLACE = {p: i for i, p in enumerate(POWERS)}
SPREAD = [
    float(math.factorial(sum(p)) * math.prod(math.factorial(e) for e in p)) for p in POWERS
]


FLAT = {(a, b): i for i, (a, b) in enumerate((a, b) for a in range(8) for b in range(8 - a))}


def packed_place(e):
    n, n2, l = e // 64, (e // 8) & 7, e & 7
    r = (n2 - n) & 7
    first = jnp.where(r > 4, n2, n)
    r = jnp.where(r > 4, 8 - r, r)
    row = jnp.where(r == 4, (first & 3) + 4 * (l & 1), first)
    diagonal = jnp.where(l < 4, 12 + l, 16 + (l & 1))
    group = jnp.where(
        r == 0, diagonal, jnp.where(r == 4, 8 + l // 2, jnp.where(r == 2, 8 + l, l))
    )
    half = jnp.where(r == 0, jnp.where((l == 4) | (l == 5), 0, 1), jnp.where(r > 2, 1, 0))
    return half * ROWS + group * 8 + row


def up(x, k):
    return x if k % 8 == 0 else pltpu.roll(x, (8 - k) % 8, 0)


def swap(x):
    return pltpu.roll(x, 64, 1)


def pieces(x, count):
    out = []
    for _ in range(count):
        p = x.astype(BF16).astype(F32)
        out.append(p)
        x = x - p
    return out


def one_hot(row):
    return jnp.where(lax.broadcasted_iota(jnp.int32, (128, 128), 0) == row, 1.0, 0.0).astype(BF16)


def kernel(
    faces, pos_hbm, near_hbm, count_hbm, lists_hbm, sparse_hbm, weight_hbm,
    out_ref,
    pos_ref, near_ref, count_ref, lists_ref, weight_ref,
    posbuf, topbuf, ghost_out, tab, pack, index, ohs, oht, ohp, ohn, looked, offs, zpow, planar, ahead, radial, slope_r, dens,
    spec, dbuf, rbuf, gbuf, eout, ein, vbuf, descs, slopes, sparse, fold, spread, folded, wide, left, pulls,
    gtab, gret, domg, fin, topg, fintop, domown, faceg, farin, total_ref,
    local_sem, pos_s, pos_r, top_s, top_r, gho_s, gho_r, des_s, des_r, gra_s, gra_r, ret_s, ret_r, fin_s, fin_r, fit_s, fit_r, far_s, far_r, ene_s, ene_r,
):
    dom, sp = lax.axis_index("dom"), lax.axis_index("sp")
    n_dom, n_sp = lax.axis_size("dom"), lax.axis_size("sp")
    below = n_dom // 2
    ring = 2 * n_sp
    z = (dom // below) * n_sp + sp
    rest = lax.rem(dom, below)
    side = 1 - 2 * lax.rem(dom, 2)

    def along(delta):
        there = lax.rem(z + delta + ring, ring)
        return (rest + (there // n_sp) * below, lax.rem(there, n_sp))

    def peer(delta):
        return (dom, lax.rem(sp + delta, n_sp))

    def partner(face):
        bit = lax.rem(dom // 2**face, 2)
        return (dom + (1 - 2 * bit) * 2**face, sp)

    delta = [0, 1, -1, 2, -2, 3, -3, 4 * side]
    lane = lax.broadcasted_iota(jnp.int32, (8, 128), 1)
    low = lane < 64
    row8 = lax.broadcasted_iota(jnp.int32, (8, 128), 0)

    def sends_far(d):
        return sp + d < n_sp if d >= 5 else sp + d >= n_sp

    def gets_far(d):
        return sp >= d if d >= 5 else sp < d

    def above(d):
        return (lax.rem(dom + below, n_dom), lax.rem(sp + d, n_sp))

    barrier = pltpu.get_barrier_semaphore()
    greeted = [above(d) for d in (0, 1, 7, 2, 6, 3, 5, 4)] + [peer(d) for d in FAR]
    greeted += [partner(f) for f in reversed(range(faces - 1))]
    for who in greeted:
        pl.semaphore_signal(barrier, inc=1, device_id=who, device_id_type=MESH)
    count = len(greeted)
    for d in DIRECT:
        count = count + (faces - 1) * jnp.where(sends_far(d), 1, 0)

        @pl.when(sends_far(d))
        def _():
            for f in range(faces - 1):
                who = (partner(f)[0], lax.rem(sp + d, n_sp))
                pl.semaphore_signal(barrier, inc=1, device_id=who, device_id_type=MESH)


    pairs = [
        (pos_hbm, pos_ref), (lists_hbm, lists_ref), (near_hbm, near_ref), (count_hbm, count_ref),
        (weight_hbm, weight_ref), (sparse_hbm, sparse),
    ]
    loads = [pltpu.make_async_copy(a, b, local_sem.at[i]) for i, (a, b) in enumerate(pairs)]
    for load in loads:
        load.start()

    loads[0].wait()
    loads[1].wait()
    top = faces - 1
    for buf in (posbuf, topbuf, tab, gret, fin, fintop):
        buf[:, 4:8, :] = jnp.zeros((buf.shape[0], 4, 128), F32)
    posbuf[sp] = jnp.zeros((8, 128), F32)
    posbuf[sp, 0:3, 0:64] = pos_ref[...]
    here = posbuf[sp]
    here = here + swap(here)
    here = jnp.where(row8 == 3, lists_ref[top].astype(F32), here)
    posbuf[sp] = here
    for load in loads[2:5]:
        load.wait()
    for f in range(top):
        ohs[:, f * 128 : (f + 1) * 128] = one_hot(lists_ref[f] & 127)
    pack[...] = jnp.zeros((24, 128), jnp.int32)
    pack[:, 0:64] = near_ref[...]
    index[0:8] = jnp.where(low, pack[0:8], swap(pack[8:16]))
    last = pack[16:24]
    last = jnp.where(low, last, swap(pltpu.roll(last, 4, 0)))
    index[8:16] = jnp.where(row8 < 4, last, 0)
    for j in range(SLOTS):
        ohn[:, j * 128 : (j + 1) * 128] = one_hot(index[j : j + 1, :] & 127)
    pl.semaphore_wait(barrier, count)

    def remote(src, dst, s, r, who):
        return pltpu.make_async_remote_copy(
            src_ref=src, dst_ref=dst, send_sem=s, recv_sem=r, device_id=who, device_id_type=MESH
        )

    sent_pos = [
        remote(posbuf.at[sp, 0:4], posbuf.at[sp, 0:4], pos_s.at[d - 1], pos_r.at[d - 1], peer(d))
        for d in range(1, 8)
    ]
    for d in FAR:
        sent_pos[d - 1].start()

    sent_top = [
        remote(posbuf.at[sp, 0:4], topbuf.at[sp, 0:4], top_s.at[d], top_r.at[d], above(d)) for d in range(8)
    ]
    for d in (0, 1, 7, 2, 6, 3, 5, 4):
        sent_top[d].start()

    place = packed_place(lax.broadcasted_iota(jnp.int32, (8, 512), 1))[0:1]
    numbers = lax.broadcasted_iota(jnp.int32, (2 * ROWS, 512), 0)
    fold[...] = jnp.where(numbers == place, 1.0, 0.0).astype(BF16)
    place = packed_place(lax.broadcasted_iota(jnp.int32, (512, 128), 0))
    for k in range(0, 2 * ROWS, 128):
        n = min(128, 2 * ROWS - k)
        numbers = k + lax.broadcasted_iota(jnp.int32, (512, 128), 1)
        spread[:, k : k + n] = jnp.where(numbers == place, 1.0, 0.0).astype(BF16)[:, 0:n]
    for load in loads[5:]:
        load.wait()
    points = sparse.shape[0]

    @pl.loop(0, points // 128)
    def _(c):
        column = jnp.broadcast_to(4.0 * weight_ref[pl.ds(c, 1), :], (128, 128)).T
        wide[pl.ds(pl.multiple_of(c * 128, 128), 128), :] = column

    @pl.loop(0, points // CHUNK)
    def _(c):
        at = pl.ds(pl.multiple_of(c * CHUNK, CHUNK), CHUNK)
        folded[:, at] = lax.dot_general(
            fold[...], sparse[at, :], (((1,), (1,)), ((), ())), preferred_element_type=F32
        ).astype(BF16)

    for c in sent_pos:
        c.wait()

    for hi in range(4):
        tab[hi] = jnp.where(low, posbuf[2 * hi], posbuf[2 * hi + 1])

    def gather(tiles, hots):
        parts = jnp.concatenate(pieces(tiles.reshape(32, 128), 3), axis=0).astype(BF16)
        out = jnp.dot(parts, hots, preferred_element_type=F32)
        return out[0:32] + out[32:64] + out[64:96]

    def chosen(out, which):
        tile = jnp.zeros((8, 128), F32)
        for hi in range(4):
            tile = jnp.where(which == hi, out[hi * 8 : hi * 8 + 8], tile)
        return tile

    out = gather(tab[0:4], ohs[...])
    sent_ghost = []
    for f in range(top):
        tile = chosen(out[:, f * 128 : (f + 1) * 128], lists_ref[f] // 128)
        ghost_out[f] = jnp.where(row8 == 3, lists_ref[f].astype(F32), tile)
        c = remote(ghost_out.at[f, 0:4], tab.at[4 + f, 0:4], gho_s.at[f], gho_r.at[f], partner(f))
        c.start()
        sent_ghost.append(c)

    def look(first, last, into):
        n = (last - first) * 8
        values = tab[first:last].reshape(n, 128)
        split = jnp.concatenate(pieces(values, 3), axis=0).astype(BF16)
        for q in range(4):
            at = slice(q * 384, (q + 1) * 384)
            got = jnp.dot(split, ohn[:, at], preferred_element_type=F32)
            got = got[0:n] + got[n : 2 * n] + got[2 * n : 3 * n]
            for u in range(3):
                j = q * 3 + u
                which = index[j : j + 1, :] // 128
                tile = looked[j] if into else jnp.zeros((8, 128), F32)
                for hi in range(first, last):
                    part = got[(hi - first) * 8 : (hi - first) * 8 + 8, u * 128 : (u + 1) * 128]
                    tile = jnp.where(which == hi, part, tile)
                looked[j] = tile

    look(0, 4, False)
    for c in sent_top:
        c.wait()
    far = jnp.concatenate(
        [jnp.where(low, topbuf[2 * hi], topbuf[2 * hi + 1]) for hi in range(4)], axis=0
    )
    top_list = topbuf[sp, 3:4, :].astype(jnp.int32)
    oht[...] = one_hot(top_list & 127)
    tab[4 + top] = chosen(gather(far, oht[...]), top_list // 128)

    for c in sent_ghost:
        c.wait()
    look(4, 4 + faces, True)

    pack[0:8] = jnp.zeros((8, 128), jnp.int32)
    pack[0:1, 0:64] = count_ref[...]
    counts = pack[0:8]
    counts = jnp.broadcast_to((counts + swap(counts))[0:1], (8, 128))
    upper = lane // 64
    centre = 0.05 + 0.15 * row8.astype(F32)
    for j in range(SLOTS):
        off = 0.5 * (looked[j] - here)
        offs[j] = off
        x, y, zz = (jnp.broadcast_to(off[axis : axis + 1], (8, 128)) for axis in range(3))
        squared = x * x + y * y + zz * zz
        slot = j + 8 * upper if j < 8 else 8 + j + 4 * upper
        live = jnp.where(slot < counts, 1.0, 0.0)
        inside = 1.0 - squared * (1.0 / 3.5)
        gap = squared - centre
        bell = jnp.exp(-30.0 * gap * gap) * live
        r = bell * (inside * inside)
        radial[j] = r
        slope_r[j] = r * (-60.0 * gap) + bell * ((-2.0 / 3.5) * inside)
        power = {0: None}
        for c in range(1, 8):
            power[c] = zz if c == 1 else power[c - 1] * (zz * (1.0 / c))
            zpow[j, c - 1] = power[c]
        ys = [None]
        for c in range(1, 8):
            ys.append(y if c == 1 else ys[c - 1] * (y * (1.0 / c)))
        xs = None
        for c in range(8):
            xs = None if c == 0 else x if c == 1 else xs * (x * (1.0 / c))
            for d in range(8 - c):
                if c + d:
                    planar[j, FLAT[c, d] - 1] = xs if d == 0 else ys[d] if c == 0 else xs * ys[d]

    for (a, b), at in FLAT.items():
        rs = [radial[j] for j in range(SLOTS)]
        if at:
            rs = [r * planar[j, at - 1] for j, r in enumerate(rs)]
        for c in range(8 - a - b):
            terms = [r if c == 0 else r * zpow[j, c - 1] for j, r in enumerate(rs)]
            while len(terms) > 1:
                terms = [sum(terms[i : i + 2][1:], terms[i]) for i in range(0, len(terms), 2)]
            dens[PLACE[a, b, c]] = terms[0] + swap(terms[0])

    def turned(d):
        return jnp.where(low, d, up(d, 2))

    zero, four = [], []
    for l in range(8):
        s0 = s1 = s2 = None
        for m in range(STARTS[l], STARTS[l + 1]):
            d = dens[m]
            t = turned(d)
            y1, y2 = up(t, 1), up(t, 2)
            ahead[m, 0] = y1
            ahead[m, 1] = y2
            f = d * SPREAD[m]
            a, b, c = f * d, f * y1, f * y2
            s0, s1, s2 = (a, b, c) if s0 is None else (s0 + a, s1 + b, s2 + c)
        spec[l] = s1
        spec[8 + l] = s2
        zero.append(s0)
        four.append(s2)
    for l in range(4):
        pair = jnp.where(row8 < 4, four[2 * l], up(four[2 * l + 1], 4))
        spec[8 + l] = jnp.where(low, spec[8 + l], pair)
        spec[12 + l] = jnp.where(low, spec[12 + l], zero[l])
    for l in range(2):
        spec[16 + l] = jnp.where(low, zero[4 + l], zero[6 + l])
    twice = jnp.where(low, 2.0, 1.0)

    def times(g):
        return 2.0 if g < 12 else twice if g < 16 else 1.0

    def both(tile):
        row = jnp.sum(tile, axis=0, keepdims=True)
        tile = jnp.broadcast_to(row, (8, 128))
        return tile + swap(tile)

    total = jnp.zeros((8, 128), F32)
    for g in range(18):
        v = spec[g]
        total = total + times(g) * v * v
    scale = lax.rsqrt(both(total) + 1e-06)
    for g in range(0, 18, 2):
        two = jnp.concatenate([spec[g] * scale, spec[g + 1] * scale], axis=0)
        dbuf[0, g * 8 : g * 8 + 16, :] = two.astype(BF16)

    sent_desc = [
        remote(dbuf.at[0], dbuf.at[t], des_s.at[t - 1], des_r.at[t - 1], along(delta[t]))
        for t in range(1, 8)
    ]
    for t in (7, 5, 6, 3, 4, 1, 2):
        sent_desc[t - 1].start()

    partner_lists = [tab[4 + f, 3:4, :].astype(jnp.int32) for f in range(top)]
    for f in range(top):
        ohp[:, f * 128 : (f + 1) * 128] = one_hot(partner_lists[f] & 127)

    wlow = lax.broadcasted_iota(jnp.int32, (ROWS, 128), 1) < 64
    sent_grad, sent_energy = [None] * 8, [None] * 8
    for slots in ((7, 5, 6, 3), (4, 1, 2, 0)):
        for t in slots:
            if t:
                sent_desc[t - 1].wait_recv()
        for k in range(2):
            xa = dbuf[slots[2 * k]].astype(F32)
            xb = dbuf[slots[2 * k + 1]].astype(F32)
            at = slice(k * 128, (k + 1) * 128)
            vbuf[0:ROWS, at] = jnp.where(wlow, xa, swap(xb)).astype(BF16)
            vbuf[ROWS : 2 * ROWS, at] = jnp.where(wlow, swap(xa), xb).astype(BF16)
        descs[...] = jnp.dot(spread[...], vbuf[...], preferred_element_type=F32).astype(BF16)
        energy = jnp.zeros((8, 256), F32)
        for c in range(points // CHUNK):
            at = slice(c * CHUNK, (c + 1) * CHUNK)
            score = jnp.dot(sparse[at, :], descs[...], preferred_element_type=F32)
            w = wide[at, :]
            square = score * score
            ws = jnp.concatenate([w, w], axis=1) * square
            energy = energy + jnp.sum((ws * square).reshape(CHUNK // 8, 8, 256), axis=0)
            slopes[at, :] = (ws * score).astype(BF16)
            part = jnp.dot(folded[:, at], slopes[at, :], preferred_element_type=F32)
            grad = part if c == 0 else grad + part
        energy = jnp.sum(energy, axis=0, keepdims=True)
        for k in range(2):
            a, b = slots[2 * k], slots[2 * k + 1]
            at = slice(k * 128, (k + 1) * 128)
            lo, hi = grad[0:ROWS, at], grad[ROWS : 2 * ROWS, at]
            rbuf[a] = jnp.where(wlow, lo, swap(hi)).astype(BF16)
            rbuf[b] = jnp.where(wlow, swap(lo), hi).astype(BF16)
            e = jnp.broadcast_to(energy[:, at], (8, 128))
            for t, mine in ((a, e), (b, swap(e))):
                eout[t] = mine
        for t in slots:
            if t:
                c = remote(rbuf.at[t], gbuf.at[t - 1], gra_s.at[t - 1], gra_r.at[t - 1], along(-delta[t]))
                c.start()
                sent_grad[t] = c
        for t in slots:
            if t:
                c = remote(
                    eout.at[t, 0:1], ein.at[t - 1, 0:1], ene_s.at[t - 1], ene_r.at[t - 1], along(-delta[t])
                )
                c.start()
                sent_energy[t] = c

    summed = rbuf[0].astype(F32)
    for t in range(1, 8):
        sent_grad[t].wait_recv()
        summed = summed + gbuf[t - 1].astype(F32)
    dot = jnp.zeros((8, 128), F32)
    for g in range(18):
        dot = dot + summed[g * 8 : g * 8 + 8, :] * spec[g]
    dot = both(dot) * scale
    pull = []
    for g in range(18):
        pull.append(scale * (summed[g * 8 : g * 8 + 8, :] - times(g) * (spec[g] * scale) * dot))
    for l in range(8):
        ha, hb = pull[l], pull[8 + l]
        h0 = pull[12 + l] if l < 4 else swap(pull[12 + l]) if l < 6 else pull[10 + l]
        pair = pull[8 + l // 2]
        h4 = jnp.where((row8 < 4) == (l % 2 == 0), pair, up(pair, 4))
        other = swap(ha)
        k1 = ha
        k2 = jnp.where(low, hb, h4)
        k5 = up(jnp.where(low, up(other, -3), up(other, -1)), 4)
        k6 = up(jnp.where(low, up(hb, -2), 2.0 * h0), 4)
        for m in range(STARTS[l], STARTS[l + 1]):
            y1, y2 = ahead[m, 0], ahead[m, 1]
            v = k1 * y1 + k2 * y2 + up(k5 * y1 + k6 * y2, 4)
            left[m] = (v + swap(v)) * SPREAD[m]

    @pl.loop(0, SLOTS // 6)
    def _(block):
        js = [block * 6 + u for u in range(6)]
        zp = [[None] + [zpow[j, c] for c in range(7)] for j in js]
        q = [[None] * 6 for _ in range(4)]

        def add(old, new):
            return new if old is None else old + new

        def mul(tile, factor):
            return tile if factor is None else tile * factor

        for (a, b), at in FLAT.items():
            level, deriv = [None] * 6, [None] * 6
            for c in range(8 - a - b):
                d = left[PLACE[a, b, c]]
                for u in range(6):
                    level[u] = add(level[u], mul(d, zp[u][c]))
                    if c:
                        deriv[u] = add(deriv[u], mul(d, zp[u][c - 1]))
            for u, j in enumerate(js):
                flat = planar[j, at - 1] if at else None
                q[0][u] = add(q[0][u], mul(level[u], flat))
                if deriv[u] is not None:
                    q[3][u] = add(q[3][u], mul(deriv[u], flat))
                for axis, lower in ((1, (a - 1, b)), (2, (a, b - 1))):
                    if lower in FLAT:
                        flat = planar[j, FLAT[lower] - 1] if FLAT[lower] else None
                        q[axis][u] = add(q[axis][u], mul(level[u], flat))
        for u, j in enumerate(js):
            r = radial[j]
            by_square = jnp.sum(slope_r[j] * q[0][u], axis=0, keepdims=True)
            gx, gy, gz = (jnp.sum(r * q[axis][u], axis=0, keepdims=True) for axis in (1, 2, 3))
            straight = jnp.where(row8 == 0, gx, jnp.where(row8 == 1, gy, jnp.where(row8 == 2, gz, 0.0)))
            pulls[j] = 0.5 * straight + offs[j] * by_square

    centre_grad = pulls[0]
    for j in range(1, SLOTS):
        centre_grad = centre_grad + pulls[j]
    centre_grad = centre_grad + swap(centre_grad)

    def placed(tiles, which, first, last):
        rows = []
        split = [pieces(tile, 2) for tile in tiles]
        for p in range(2):
            for hi in range(first, last):
                rows.append(jnp.concatenate(
                    [jnp.where(w == hi, s[p], 0.0) for w, s in zip(which, split)], axis=1
                ))
        return jnp.concatenate(rows, axis=0).astype(BF16)

    over_lanes = (((1,), (1,)), ((), ()))

    def scatter(first, last):
        n = (last - first) * 8
        total = jnp.zeros((n, 128), F32)
        for q in range(4):
            js = range(q * 3, q * 3 + 3)
            which = [index[j : j + 1, :] // 128 for j in js]
            rows = placed([pulls[j] for j in js], which, first, last)
            got = lax.dot_general(
                rows, ohn[:, q * 384 : (q + 1) * 384], over_lanes, preferred_element_type=F32
            )
            total = total + got[0:n] + got[n : 2 * n]
        return total.reshape(last - first, 8, 128)

    gtab[4 : 4 + faces] = scatter(4, 4 + faces)
    sent_back = []
    for f in range(top):
        c = remote(gtab.at[4 + f, 0:4], gret.at[f, 0:4], ret_s.at[f], ret_r.at[f], partner(f))
        c.start()
        sent_back.append(c)

    def home(tiles, which, hots):
        got = lax.dot_general(
            placed(tiles, which, 0, 4), hots, over_lanes, preferred_element_type=F32
        )
        return (got[0:32] + got[32:64]).reshape(4, 8, 128)

    topg[...] = home([gtab[4 + top]], [top_list // 128], oht[...])
    sent_top = []
    for d in range(8):
        who = above(d)
        c = remote(topg.at[who[1] // 2, 0:4], fintop.at[d, 0:4], fit_s.at[d], fit_r.at[d], who)
        c.start()
        sent_top.append(c)
    own = scatter(0, 4)
    domown[...] = own
    def final(src, d):
        who = peer(d)
        return remote(
            src.at[who[1] // 2, 0:4], fin.at[d - 1, 0:4], fin_s.at[d - 1], fin_r.at[d - 1], who
        )

    sent_fin = {d: final(domg, d) for d in FAR}
    for d in DIRECT:
        pl.when(sends_far(d))(final(domown, d).start)
    for f in range(top):
        hots = ohp[:, f * 128 : (f + 1) * 128]
        faceg[f] = home([gtab[4 + f]], [partner_lists[f] // 128], hots)
    sent_far = {}
    for k, d in enumerate(DIRECT):
        there = lax.rem(sp + d, n_sp)
        sent_far[d] = [
            remote(
                faceg.at[f, there // 2, 0:4], farin.at[f, k, 0:4],
                far_s.at[f * 6 + k], far_r.at[f * 6 + k], (partner(f)[0], there),
            )
            for f in range(top)
        ]

        @pl.when(sends_far(d))
        def _():
            for c in sent_far[d]:
                c.start()

    for c in sent_back:
        c.wait_recv()
    which = [lists_ref[f] // 128 for f in range(top)]
    domg[...] = own + home([gret[f] for f in range(top)], which, ohs[...])
    for d in FAR:
        if d in DIRECT:
            pl.when(jnp.logical_not(sends_far(d)))(sent_fin[d].start)
        else:
            sent_fin[d].start()
    mine = domg[sp // 2]
    for d in range(8):
        sent_top[d].wait_recv()
        mine = mine + fintop[d]
    for d in reversed(FAR):
        sent_fin[d].wait_recv()
        mine = mine + fin[d - 1]
    total_ref[...] = mine
    for k, d in enumerate(DIRECT):

        @pl.when(gets_far(d))
        def _():
            for f in range(top):
                sent_far[d][f].wait_recv()
                total_ref[0:4, :] = total_ref[0:4, :] + farin[f, k, 0:4, :]

        @pl.when(sends_far(d))
        def _():
            for c in sent_far[d]:
                c.wait_send()

    energy = eout[0, 0:1, :]
    for t in range(1, 8):
        sent_energy[t].wait_recv()
        energy = energy + ein[t - 1, 0:1, :]
    energy = 0.25 * energy
    mine = total_ref[...]
    odd = jnp.where(lax.rem(sp, 2) == 1, 1, 0)
    mine = jnp.where(odd == 1, swap(mine), mine)
    out_ref[...] = jnp.where(row8 == 3, energy, centre_grad - mine)
    for c in sent_desc + sent_grad[1:] + sent_energy[1:] + sent_back + sent_top + list(sent_fin.values()):
        c.wait_send()


def split_outputs(out_ref, energy_ref, force_ref):
    energy_ref[...] = out_ref[3:4, 0:64]
    force_ref[...] = out_ref[0:3, 0:64]


def body(positions, neighbours, counts, send_lists, sparse_points, weights):
    faces = send_lists.shape[1]
    points = sparse_points.shape[0]
    vmem = pl.BlockSpec(memory_space=pltpu.VMEM)
    hbm = pl.BlockSpec(memory_space=pl.ANY)
    dma = pltpu.SemaphoreType.DMA
    out = pl.pallas_call(
        lambda *refs: kernel(faces, *refs),
        out_shape=jax.ShapeDtypeStruct((8, 128), F32),
        in_specs=[hbm] * 6,
        out_specs=vmem,
        scratch_shapes=[
            pltpu.VMEM(positions.shape, F32),
            pltpu.VMEM(neighbours.shape, jnp.int32),
            pltpu.VMEM((1, counts.shape[0]), jnp.int32),
            pltpu.VMEM((faces, 1, 128), jnp.int32),
            pltpu.VMEM((points // 128, 128), F32),
            pltpu.VMEM((8, 8, 128), F32),
            pltpu.VMEM((8, 8, 128), F32),
            pltpu.VMEM((faces - 1, 8, 128), F32),
            pltpu.VMEM((4 + faces, 8, 128), F32),
            pltpu.VMEM((24, 128), jnp.int32),
            pltpu.VMEM((16, 128), jnp.int32),
            pltpu.VMEM((128, (faces - 1) * 128), BF16),
            pltpu.VMEM((128, 128), BF16),
            pltpu.VMEM((128, (faces - 1) * 128), BF16),
            pltpu.VMEM((128, SLOTS * 128), BF16),
            pltpu.VMEM((SLOTS, 8, 128), F32),
            pltpu.VMEM((SLOTS, 8, 128), F32),
            pltpu.VMEM((SLOTS, 7, 8, 128), F32),
            pltpu.VMEM((SLOTS, 35, 8, 128), F32),
            pltpu.VMEM((120, 2, 8, 128), F32),
            pltpu.VMEM((SLOTS, 8, 128), F32),
            pltpu.VMEM((SLOTS, 8, 128), F32),
            pltpu.VMEM((120, 8, 128), F32),
            pltpu.VMEM((18, 8, 128), F32),
            pltpu.VMEM((8, ROWS, 128), BF16),
            pltpu.VMEM((8, ROWS, 128), BF16),
            pltpu.VMEM((7, ROWS, 128), BF16),
            pltpu.VMEM((8, 8, 128), F32),
            pltpu.VMEM((7, 8, 128), F32),
            pltpu.VMEM((2 * ROWS, 256), BF16),
            pltpu.VMEM((512, 256), BF16),
            pltpu.VMEM((points, 256), BF16),
            pltpu.VMEM((points, 512), BF16),
            pltpu.VMEM((2 * ROWS, 512), BF16),
            pltpu.VMEM((512, 2 * ROWS), BF16),
            pltpu.VMEM((2 * ROWS, points), BF16),
            pltpu.VMEM((points, 128), F32),
            pltpu.VMEM((120, 8, 128), F32),
            pltpu.VMEM((SLOTS, 8, 128), F32),
            pltpu.VMEM((4 + faces, 8, 128), F32),
            pltpu.VMEM((faces - 1, 8, 128), F32),
            pltpu.VMEM((4, 8, 128), F32),
            pltpu.VMEM((7, 8, 128), F32),
            pltpu.VMEM((4, 8, 128), F32),
            pltpu.VMEM((8, 8, 128), F32),
            pltpu.VMEM((4, 8, 128), F32),
            pltpu.VMEM((faces - 1, 4, 8, 128), F32),
            pltpu.VMEM((faces - 1, 6, 8, 128), F32),
            pltpu.VMEM((8, 128), F32),
            dma((6,)),
            dma((7,)), dma((7,)),
            dma((8,)), dma((8,)),
            dma((faces - 1,)), dma((faces - 1,)),
            dma((7,)), dma((7,)),
            dma((7,)), dma((7,)),
            dma((faces - 1,)), dma((faces - 1,)),
            dma((7,)), dma((7,)),
            dma((8,)), dma((8,)),
            dma(((faces - 1) * 6,)), dma(((faces - 1) * 6,)),
            dma((7,)), dma((7,)),
        ],
        compiler_params=pltpu.CompilerParams(
            collective_id=0, has_side_effects=True, vmem_limit_bytes=60 * 2**20
        ),
        name="gap_forces",
    )(
        positions,
        neighbours,
        counts.reshape(1, -1),
        send_lists.transpose(1, 0, 2),
        sparse_points,
        weights.reshape(-1, 128),
    )
    energies, forces = pl.pallas_call(
        split_outputs,
        out_shape=(jax.ShapeDtypeStruct((1, 64), F32), jax.ShapeDtypeStruct((3, 64), F32)),
        in_specs=[vmem],
        out_specs=(vmem, vmem),
        compiler_params=pltpu.CompilerParams(vmem_limit_bytes=60 * 2**20),
        name="split_outputs",
    )(out)
    return energies.reshape(-1), forces


def solution(mesh):
    in_specs = (
        P(None, ("dom", "sp")),
        P(None, ("dom", "sp")),
        P(("dom", "sp")),
        P("dom", None, None),
        P("sp", None),
        P("sp"),
    )
    out_specs = (P(("dom", "sp")), P(None, ("dom", "sp")))
    return jax.shard_map(body, mesh=mesh, in_specs=in_specs, out_specs=out_specs, check_vma=False)
```
